768 devices in a mesh: row: 96 (over z, x, y_hi), col: 8 (over y_lo, core).
Axes of the slice: x: 4, y: 8 (y_hi: 2, y_lo: 4; y = y_hi * 4 + y_lo), z: 12, core: 2. Of those that a mesh axis runs over, the one named last changes fastest.
Arguments:
- values: float32 [768, 16, 64, 64], P('row', 'col'), as said below
- radius: int32 [768], replicated, may hold values from 3 to 7, as said below
- branch: int32 [2, 768], replicated, may hold values from 0 to 1
Outputs:
- purified: float32 [768, 16, 64, 64], P('row', 'col')
- traces: float32 [2], replicated
The draws below stay inside these ranges and needn't reach their ends.
Inputs may be any that keep to these rules, and one draw needn't show every extreme that they name: values is symmetric: the block in slot k of block row I is the transpose of the block in slot 16 - k of block row I + k - 8, and every block outside the pattern is zero. Some block row has radius 3 and some has radius 7.
All inputs are finite; a program needn't handle non-finite values.
Results may differ from the reference program's by a relative error of at most 0.00017.
Values sent between devices are 32-bit elements; how exact they have to be, the bound alone decides.
No kernel may reach another device: no remote copies, remote signals or barrier semaphores. Data moves between devices by JAX's collectives and lax.ppermute only.
A program may use at most 128 MiB of HBM per device.

```python
import jax
import jax.numpy as jnp
from jax import lax

B = 64
NNZ = 16
STEPS = 2
NB = 768


def pattern_radius(key, count):
    raw = jax.random.randint(jax.random.fold_in(key, 11), (count,), 3, 8)
    low_end = jnp.full((1,), 3, jnp.int32)
    high_end = jnp.full((1,), 7, jnp.int32)
    return jnp.concatenate([low_end, raw[1:-1].astype(jnp.int32), high_end])


def draw_radius(key, part):
    return pattern_radius(key, NB)


def draw_values(key, part):
    radius = pattern_radius(key, NB)
    key = jax.random.fold_in(key, 5)
    sigma = 0.45 / (7.0 * B) ** 0.5
    gauss_part = jax.random.normal(key, (NB, NNZ, B, B), jnp.float32)
    scales = jnp.ones((NB,), jnp.float32)
    gauss_part = gauss_part * sigma
    row_ids = jnp.arange(NB, dtype=jnp.int32)
    blocks = []
    for slot in range(NNZ):
        partner = jnp.roll(gauss_part[:, (NNZ - slot) % NNZ], -(slot - 8), axis=0)
        swapped = jnp.transpose(partner, (0, 2, 1))
        block = (gauss_part[:, slot] + swapped) * 0.70710678
        if slot == 8:
            block = block + 0.5 * jnp.eye(B, dtype=jnp.float32)[None]
        column = row_ids + slot - 8
        inside = (column >= 0) & (column < NB)
        other = jnp.roll(radius, -(slot - 8))
        keep = inside & (abs(slot - 8) <= jnp.minimum(radius, other))
        weight = jnp.roll(scales, -(slot - 8)) * keep.astype(jnp.float32)
        blocks.append(block * weight[:, None, None])
    return jnp.stack(blocks, axis=1)


def set_ends(values, key, low, largest):
    longest = values.shape.index(max(values.shape))
    spots = []
    for shift in (0, 1):
        where = [jax.random.randint(jax.random.fold_in(key, axis), (), 0, length) for axis, length in enumerate(values.shape)]
        where[longest] = (where[longest] + shift) % values.shape[longest]
        spots.append(tuple(where))
    return values.at[spots[0]].set(low).at[spots[1]].set(largest)


def setup_inputs(seed: int = 0) -> dict:
    keys = jax.random.split(jax.random.key(seed), 4)
    values = draw_values(jax.random.fold_in(keys[3], 71), 0)
    radius = draw_radius(jax.random.fold_in(keys[3], 71), 0)
    branch = set_ends(jax.random.randint(keys[2], (STEPS, NB), 0, 2), jax.random.fold_in(keys[2], 1), 0, 1).astype(jnp.int32)
    return {"values": values, "radius": radius, "branch": branch}


def pattern_columns(count):
    row_ids = jnp.arange(count, dtype=jnp.int32)[:, None]
    slot_ids = jnp.arange(NNZ, dtype=jnp.int32)[None, :]
    column = row_ids + slot_ids - 8
    return slot_ids, column


def pattern_mask(radius):
    count = radius.shape[0]
    slot_ids, column = pattern_columns(count)
    inside = (column >= 0) & (column < count)
    partner = radius[jnp.clip(column, 0, count - 1)]
    reach = jnp.minimum(radius[:, None], partner)
    return (inside & (jnp.abs(slot_ids - 8) <= reach)).astype(jnp.float32)


def square(values):
    count = values.shape[0]
    padded = jnp.pad(values, ((0, 0), (8, 8), (0, 0), (0, 0)))

    def turn(offset, running):
        upper_blocks = lax.dynamic_index_in_dim(values, offset, 1, keepdims=False)
        lower_blocks = lax.dynamic_slice_in_dim(padded, offset, NNZ, 1)
        products = jnp.einsum('kxy,ksxz->ksyz', upper_blocks, lower_blocks, precision=lax.Precision.HIGHEST)
        widened = jnp.pad(products, ((8, 8), (0, 0), (0, 0), (0, 0)))
        shifted = lax.dynamic_slice_in_dim(widened, 16 - offset, count, 0)
        return running + shifted

    start = jnp.zeros(values.shape, jnp.float32)
    return lax.fori_loop(0, NNZ, turn, start)


def reference(values, radius, branch):
    count = values.shape[0]
    pattern = pattern_mask(radius)[:, :, None, None]
    slot_ids, column = pattern_columns(count)
    clipped = jnp.clip(column, 0, count - 1)
    current = values
    traces = []
    for step_index in range(STEPS):
        squared = square(current) * pattern
        traces.append(jnp.sum(jnp.trace(squared[:, 8], axis1=1, axis2=2)))
        flags = branch[step_index]
        pick = flags[:, None] * flags[clipped]
        current = jnp.where((pick == 1)[:, :, None, None], 2.0 * current - squared, squared)
    return current, jnp.stack(traces)
```

```python
import jax
import jax.numpy as jnp
from jax import lax
from jax.experimental import pallas as pl
from jax.experimental.pallas import tpu as pltpu
from jax.sharding import PartitionSpec as P

F32 = jnp.float32
BF16 = jnp.bfloat16
B = 64
H = 8
N = H * B
W = 3 * N
HALF = 224
VMEM = pl.BlockSpec(memory_space=pltpu.VMEM)
SMEM = pl.BlockSpec(memory_space=pltpu.SMEM)
RAD, BR = 4, (28, 52)


def params(mib):
    return pltpu.CompilerParams(vmem_limit_bytes=mib << 20)


def halves(x):
    hi = x.astype(BF16)
    return hi, (x - hi.astype(F32)).astype(BF16)


def dot3(a, b, dims):
    (ah, al), (bh, bl) = a, b

    def one(x, y):
        return lax.dot_general(x, y, (dims, ((), ())), preferred_element_type=F32)

    return one(ah, bh) + (one(ah, bl) + one(al, bh))


NN = ((1,), (0,))
NT = ((1,), (1,))


def strip(i):
    return slice(i * B, (i + 1) * B)


def window_vector(s_ref, start):
    block = lax.shift_right_logical(lax.broadcasted_iota(jnp.int32, (1, W), 1), 6)
    out = jnp.zeros((1, W), jnp.int32)
    for w in range(3 * H):
        out = jnp.where(block == w, s_ref[start + w], out)
    return out


def strip_rules(s_ref, radii, flags, i, start):
    block = lax.shift_right_logical(lax.broadcasted_iota(jnp.int32, (1, W), 1), 6)
    reach = jnp.minimum(radii, s_ref[RAD + H + i])
    keep = jnp.abs(block - (H + i)) <= reach
    pick = (flags * s_ref[start + H + i]) == 1
    return keep, pick


def pack_kernel(v_ref, out_ref):
    for i in range(H):
        out_ref[strip(i), :] = jnp.concatenate([v_ref[i, 0], v_ref[i, 1]], axis=1)


def square_kernel(s_ref, *refs):
    packs, (p1_ref, al_ref, au_ref, up_ref, down_ref, tr_ref) = refs[:8], refs[8:14]
    q_ref, r_ref, rh, rl, t_ref = refs[14:]
    yl, core = s_ref[0], s_ref[1]
    for k in range(4):
        for other in range(2):
            place = 2 * ((yl - k) & 3) + (core + other - 2 * core * other)
            q_ref[:, pl.ds(pl.multiple_of(place * 128, 128), 128)] = packs[4 * other + k][...]
    total = jnp.zeros((1, 2 * N), F32)
    for i in range(H):
        own = q_ref[strip(i), :]
        total += jnp.sum(own * own, axis=0, keepdims=True)
        at = i * B
        if i % 2:
            own = pltpu.roll(jnp.concatenate([own, jnp.zeros((B, 128), F32)], axis=1), B, 1)
            at -= B
        parts = [own]
        if at:
            parts.insert(0, jnp.zeros((B, at), F32))
        left = W - at - own.shape[1]
        if left:
            parts.append(jnp.zeros((B, left), F32))
        full = jnp.concatenate(parts, axis=1)
        r_ref[strip(i), :] = full
        rh[strip(i), :], rl[strip(i), :] = halves(full)
    tr_ref[...] = jnp.broadcast_to(jnp.sum(total, axis=1, keepdims=True), tr_ref.shape)

    def part(rows, cols):
        return rh[rows, cols], rl[rows, cols]

    lo, hi = slice(0, 256), slice(256, 512)
    p00 = dot3(part(lo, slice(0, 1280)), part(lo, slice(0, 1280)), NT)
    p01 = dot3(part(lo, slice(256, 1280)), part(hi, slice(256, 1280)), NT)
    p11 = dot3(part(hi, slice(256, W)), part(hi, slice(256, W)), NT)
    p1_ref[lo, lo] = p00
    p1_ref[lo, hi] = p01
    p1_ref[hi, lo] = p01.T
    p1_ref[hi, hi] = p11
    every = slice(0, N)
    mid = slice(N, 2 * N)
    al_ref[lo, :] = dot3(part(lo, mid), part(every, slice(0, N)), NN)
    al_ref[hi, lo] = jnp.zeros((256, 256), F32)
    al_ref[hi, hi] = dot3(part(hi, mid), part(every, slice(256, N)), NN)
    au_ref[lo, lo] = dot3(part(lo, mid), part(every, slice(2 * N, 2 * N + 256)), NN)
    au_ref[lo, hi] = jnp.zeros((256, 256), F32)
    au_ref[hi, :] = dot3(part(hi, mid), part(every, slice(2 * N, W)), NN)

    lane = lax.broadcasted_iota(jnp.int32, (B, 256), 1)
    mine = pl.ds(pl.multiple_of(core * HALF, 8), HALF)
    t_ref[lo, :] = au_ref[hi, lo]
    for a in range(1, 4):
        turned = pltpu.roll(au_ref[strip(H - a), hi], a * B, 1)
        t_ref[strip(3 + a), :] = jnp.where(lane < a * B, au_ref[strip(a), lo], turned)
    up_ref[...] = t_ref[mine, :]
    t_ref[lo, :] = al_ref[lo, hi]
    for a in range(3):
        turned = pltpu.roll(al_ref[strip(6 - a), hi], (a + 1) * B, 1)
        t_ref[strip(4 + a), :] = jnp.where(lane >= (a + 1) * B, al_ref[strip(a), lo], turned)
    down_ref[...] = t_ref[mine, :]

    radii = window_vector(s_ref, RAD)
    flags = window_vector(s_ref, BR[0])
    for i in range(H):
        keep, pick = strip_rules(s_ref, radii, flags, i, BR[0])
        for ref, at in ((al_ref, 0), (p1_ref, N), (au_ref, 2 * N)):
            span = slice(at, at + N)
            squared = jnp.where(keep[:, span], ref[strip(i), :], 0.0)
            ref[strip(i), :] = jnp.where(
                pick[:, span], 2.0 * r_ref[strip(i), span] - squared, squared
            )


def second_kernel(s_ref, p1_ref, al_ref, au_ref, tr_ref, ua, ub, da, db,
                  own_ref, part_ref, x1_ref, sums_ref, t_ref, z_ref, r_ref, mh, ml):
    core, col = s_ref[1], s_ref[2]
    lo, hi = slice(0, 256), slice(256, 512)
    lane = lax.broadcasted_iota(jnp.int32, (B, 256), 1)
    mine = pl.ds(pl.multiple_of(core * HALF, 8), HALF)
    theirs = pl.ds(pl.multiple_of((1 - core) * HALF, 8), HALF)
    nothing = jnp.zeros((256, 256), F32)
    zero = jnp.zeros((B, 256), F32)

    radii = window_vector(s_ref, RAD)
    flags = window_vector(s_ref, BR[0])

    t_ref[mine, :] = ua[...]
    t_ref[theirs, :] = ub[...]
    z_ref[lo, hi] = t_ref[lo, :].T
    z_ref[hi, lo] = nothing
    first = [zero]
    last = [zero]
    for a in range(1, 4):
        first.append(jnp.where(lane < a * B, t_ref[strip(3 + a), :], 0.0))
        turned = pltpu.roll(t_ref[strip(7 - a), :], a * B, 1)
        last.append(jnp.where(lane < a * B, turned, 0.0))
    z_ref[lo, lo] = jnp.concatenate(first, axis=0).T
    z_ref[hi, hi] = jnp.concatenate(last, axis=0).T
    square2 = jnp.zeros((1, N), F32)
    square1 = jnp.zeros((1, N), F32)
    for i in range(H):
        keep, pick = strip_rules(s_ref, radii, flags, i, BR[0])
        span = slice(0, N)
        add = jnp.where(keep[:, span], z_ref[strip(i), :], 0.0)
        new = al_ref[strip(i), :] + jnp.where(pick[:, span], -add, add)
        r_ref[strip(i), span] = new
        square2 += jnp.sum(new * new, axis=0, keepdims=True)
        inner = p1_ref[strip(i), :]
        r_ref[strip(i), N : 2 * N] = inner
        square1 += jnp.sum(inner * inner, axis=0, keepdims=True)
    t_ref[mine, :] = da[...]
    t_ref[theirs, :] = db[...]
    z_ref[lo, hi] = nothing
    z_ref[hi, lo] = t_ref[lo, :].T
    first = []
    last = []
    for a in range(3):
        first.append(jnp.where(lane >= (a + 1) * B, t_ref[strip(4 + a), :], 0.0))
        turned = pltpu.roll(t_ref[strip(6 - a), :], (a + 1) * B, 1)
        last.append(jnp.where(lane >= (a + 1) * B, turned, 0.0))
    z_ref[lo, lo] = jnp.concatenate(first + [zero], axis=0).T
    z_ref[hi, hi] = jnp.concatenate(last + [zero], axis=0).T
    for i in range(H):
        keep, pick = strip_rules(s_ref, radii, flags, i, BR[0])
        span = slice(2 * N, W)
        add = jnp.where(keep[:, span], z_ref[strip(i), :], 0.0)
        r_ref[strip(i), span] = au_ref[strip(i), :] + jnp.where(pick[:, span], -add, add)

    outer = jnp.sum(square1 + 2.0 * square2, axis=1, keepdims=True)
    spot = lax.broadcasted_iota(jnp.int32, (1, 128), 1)
    both = jnp.where(spot == 0, tr_ref[...], jnp.where(spot == 1, outer, 0.0))
    sums_ref[...] = jnp.broadcast_to(both, sums_ref.shape)

    blank = jnp.zeros((N, N), BF16)
    for ref in (mh, ml):
        for rows in (slice(0, N), slice(2 * N, W)):
            ref[rows, 0:N] = blank
            ref[rows, 2 * N : W] = blank
    mid = slice(N, 2 * N)
    for i in range(H):
        rows = slice(N + i * B, N + (i + 1) * B)
        mh[rows, :], ml[rows, :] = halves(r_ref[strip(i), :])
    mh[0:N, mid], ml[0:N, mid] = halves(r_ref[:, 0:N].T)
    mh[2 * N : W, mid], ml[2 * N : W, mid] = halves(r_ref[:, 2 * N : W].T)

    upper = (col >= 4).astype(jnp.int32)
    wide = lax.broadcasted_iota(jnp.int32, (B, 128), 1) >= B
    for i in range(H):
        rows = slice(N + i * B, N + (i + 1) * B)
        pair = pl.ds(pl.multiple_of((i + 2 * col) * B, B), 128)
        own_ref[strip(i), :] = dot3((mh[rows, :], ml[rows, :]), (mh[pair, :], ml[pair, :]), NT)
        begin = (i - i % 2 + 2 * col) * B
        if i % 2:
            held = r_ref[strip(i), pl.ds(pl.multiple_of(begin, 128), 256)]
            x1_ref[strip(i), :] = held[:, B : B + 128]
        else:
            x1_ref[strip(i), :] = r_ref[strip(i), pl.ds(pl.multiple_of(begin, 128), 128)]
        there = pl.ds(pl.multiple_of((16 * upper + i) * B, B), B)
        block = i + 6 - 2 * col + 16 * upper
        pair = pl.ds(pl.multiple_of(block * B, B), 128)
        share = dot3((mh[there, mid], ml[there, mid]), (mh[pair, mid], ml[pair, mid]), NT)
        index = block + wide.astype(jnp.int32)
        part_ref[strip(i), :] = jnp.where((index >= H) & (index < 2 * H), share, 0.0)


def last_kernel(s_ref, own_ref, part_ref, x1_ref, out_ref):
    col = s_ref[2]
    wide = lax.broadcasted_iota(jnp.int32, (B, 128), 1) >= B
    for i in range(H):
        squared = own_ref[strip(i), :] + part_ref[strip(i), :]
        keep, pick = [], []
        for h in range(2):
            far = jnp.abs(2 * col + h - H)
            reach = jnp.minimum(s_ref[RAD + H + i], s_ref[RAD + i + 2 * col + h])
            keep.append((far <= reach).astype(F32))
            pick.append((s_ref[BR[1] + H + i] * s_ref[BR[1] + i + 2 * col + h]).astype(F32))
        squared = squared * jnp.where(wide, keep[1], keep[0])
        chosen = jnp.where(wide, pick[1], pick[0]) == 1.0
        new = jnp.where(chosen, 2.0 * x1_ref[strip(i), :] - squared, squared)
        out_ref[i, 0] = new[:, :B]
        out_ref[i, 1] = new[:, B:]


def shape(*dims):
    return jax.ShapeDtypeStruct(dims, F32)


def cost(flops, moved):
    return pl.CostEstimate(flops=flops, bytes_accessed=moved, transcendentals=0)


def per_device(rows, values, radius, branch):
    both = ("row", "col")
    row, col = lax.axis_index("row"), lax.axis_index("col")
    pad = ((H, H),)
    radii = lax.dynamic_slice(jnp.pad(radius, pad, constant_values=-1), (H * row,), (3 * H,))
    flags = lax.dynamic_slice(jnp.pad(branch, ((0, 0),) + pad), (0, H * row), (2, 3 * H))
    scalars = jnp.concatenate(
        [jnp.stack([col // 2, col % 2, col, row]).astype(jnp.int32), radii, flags[0], flags[1]]
    )

    def swap(x):
        return lax.ppermute(x, "col", [(c, c ^ 1) for c in range(8)])

    def to_rows(x, pairs):
        return lax.ppermute(x, both, pairs)

    packed = pl.pallas_call(
        pack_kernel, out_shape=shape(N, 128), in_specs=[VMEM], out_specs=VMEM, name="pack",
        compiler_params=params(16),
    )(values)
    mine = [packed] + [
        lax.ppermute(packed, "col", [(c, (c + 2 * k) % 8) for c in range(8)]) for k in (1, 2, 3)
    ]
    others = [swap(x) for x in mine]

    inner, left, right, up, down, trace = pl.pallas_call(
        square_kernel,
        out_shape=[shape(N, N)] * 3 + [shape(HALF, 256)] * 2 + [shape(1, 128)],
        in_specs=[SMEM] + [VMEM] * 8,
        out_specs=[VMEM] * 6,
        scratch_shapes=[
            pltpu.VMEM((N, 2 * N), F32),
            pltpu.VMEM((N, W), F32),
            pltpu.VMEM((N, W), BF16),
            pltpu.VMEM((N, W), BF16),
            pltpu.VMEM((2 * HALF, 256), F32),
        ],
        compiler_params=params(48),
        name="square",
    )(scalars, *mine, *others)

    def index(r, c):
        return r * 8 + c

    def mirror(c):
        return 2 * (3 - c // 2) + c % 2

    ends = [(r, c) for r in range(rows - 1) for c in range(8)]
    ua = to_rows(up, [(index(r, c), index(r + 1, mirror(c))) for r, c in ends])
    da = to_rows(down, [(index(r + 1, c), index(r, mirror(c))) for r, c in ends])
    ub, db = swap(ua), swap(da)

    own, part, x1, sums = pl.pallas_call(
        second_kernel,
        out_shape=[shape(N, 128)] * 3 + [shape(rows, 128)],
        in_specs=[SMEM] + [VMEM] * 8,
        out_specs=[VMEM] * 4,
        scratch_shapes=[
            pltpu.VMEM((2 * HALF, 256), F32),
            pltpu.VMEM((N, N), F32),
            pltpu.VMEM((N, W), F32),
            pltpu.VMEM((W, W), BF16),
            pltpu.VMEM((W, W), BF16),
        ],
        compiler_params=params(48),
        name="second",
    )(scalars, inner, left, right, trace, ua, ub, da, db)

    pairs = [(index(r, c), index(r + 1, 7 - c)) for r, c in ends if c >= 4]
    pairs += [(index(r + 1, c), index(r, 7 - c)) for r, c in ends if c < 4]
    part = to_rows(part, pairs)
    sums = lax.all_to_all(sums, "row", 0, 0, tiled=True)
    purified = pl.pallas_call(
        last_kernel,
        out_shape=shape(H, 2, B, B),
        in_specs=[SMEM] + [VMEM] * 3,
        out_specs=VMEM,
        compiler_params=params(16),
        name="last",
    )(scalars, own, part, x1)
    return purified, jnp.sum(sums, axis=0)[:2]


def solution(mesh):
    rows = mesh.shape["row"]

    def run(values, radius, branch):
        return per_device(rows, values, radius, branch)

    in_specs = (P("row", "col", None, None), P(), P())
    out_specs = (P("row", "col", None, None), P())
    return jax.shard_map(
        run, mesh=mesh, in_specs=in_specs, out_specs=out_specs, check_vma=False
    )
```

```python
import jax
import jax.numpy as jnp
from jax import lax
from jax.experimental import pallas as pl
from jax.experimental.pallas import tpu as pltpu
from jax.sharding import PartitionSpec as P

F32 = jnp.float32
BF16 = jnp.bfloat16
B = 64
H = 8
N = H * B
W = 3 * N
HALF = 224
VMEM = pl.BlockSpec(memory_space=pltpu.VMEM)
SMEM = pl.BlockSpec(memory_space=pltpu.SMEM)
RAD, BR = 4, (28, 52)


def params(mib):
    return pltpu.CompilerParams(vmem_limit_bytes=mib << 20)


def halves(x):
    hi = x.astype(BF16)
    return hi, (x - hi.astype(F32)).astype(BF16)


def dot3(a, b, dims):
    (ah, al), (bh, bl) = a, b

    def one(x, y):
        return lax.dot_general(x, y, (dims, ((), ())), preferred_element_type=F32)

    return one(ah, bh) + (one(ah, bl) + one(al, bh))


NN = ((1,), (0,))
NT = ((1,), (1,))


def strip(i):
    return slice(i * B, (i + 1) * B)


class Rules:
    def __init__(self, s_ref, start, rows, cols):
        self.s_ref, self.start, self.rows, self.cols = s_ref, start, rows, cols
        block = lax.shift_right_logical(lax.broadcasted_iota(jnp.int32, (1, N), 1), 6)
        radii = flags = jnp.zeros((1, N), jnp.int32)
        for k in range(H):
            radii = jnp.where(block == k, s_ref[RAD + cols + k], radii)
            flags = jnp.where(block == k, s_ref[start + cols + k], flags)
        self.block, self.radii, self.flags = block + cols, radii, flags

    def strip(self, i):
        reach = jnp.minimum(self.radii, self.s_ref[RAD + self.rows + i])
        keep = jnp.abs(self.block - (self.rows + i)) <= reach
        return keep, self.flags * self.s_ref[self.start + self.rows + i] == 1


def pack_kernel(v_ref, out_ref):
    for i in range(H):
        out_ref[strip(i), :] = jnp.concatenate([v_ref[i, 0], v_ref[i, 1]], axis=1)


def square_kernel(s_ref, *refs):
    packs, (p1_ref, g0_ref, pg_ref, send_ref, tr_ref) = refs[:8], refs[8:13]
    q_ref, r_ref, rh, rl, t_ref = refs[13:]
    yl, core, upper = s_ref[0], s_ref[1], s_ref[3]
    for k in range(4):
        for other in range(2):
            place = 2 * ((yl - k) & 3) + (core + other - 2 * core * other)
            q_ref[:, pl.ds(pl.multiple_of(place * 128, 128), 128)] = packs[4 * other + k][...]
    total = jnp.zeros((1, 2 * N), F32)
    for i in range(H):
        own = q_ref[strip(i), :]
        total += jnp.sum(own * own, axis=0, keepdims=True)
        at = i * B
        if i % 2:
            own = pltpu.roll(jnp.concatenate([own, jnp.zeros((B, 128), F32)], axis=1), B, 1)
            at -= B
        parts = [own]
        if at:
            parts.insert(0, jnp.zeros((B, at), F32))
        left = W - at - own.shape[1]
        if left:
            parts.append(jnp.zeros((B, left), F32))
        full = jnp.concatenate(parts, axis=1)
        r_ref[strip(i), :] = full
        rh[strip(i), :], rl[strip(i), :] = halves(full)
    tr_ref[...] = jnp.broadcast_to(jnp.sum(total, axis=1, keepdims=True), tr_ref.shape)

    def part(rows, cols):
        return rh[rows, cols], rl[rows, cols]

    lo, hi = slice(0, 256), slice(256, 512)
    mid = slice(N, 2 * N)
    side = pl.ds(pl.multiple_of(2 * N * upper, 128), N)
    pg_ref[...] = dot3(part(slice(None), mid), part(slice(None), side), NN)

    @pl.when(upper == 0)
    def _():
        g0_ref[...] = r_ref[:, 0:N]

    @pl.when(upper == 1)
    def _():
        g0_ref[...] = r_ref[:, 2 * N : W].T
        pg_ref[...] = pg_ref[...].T

    lane = lax.broadcasted_iota(jnp.int32, (B, 256), 1)
    t_ref[lo, :] = pg_ref[lo, hi]
    for a in range(3):
        turned = pltpu.roll(pg_ref[strip(6 - a), hi], (a + 1) * B, 1)
        t_ref[strip(4 + a), :] = jnp.where(lane >= (a + 1) * B, pg_ref[strip(a), lo], turned)
    send_ref[...] = t_ref[pl.ds(pl.multiple_of(core * HALF, 8), HALF), :]

    p01 = dot3(part(lo, slice(256, 1280)), part(hi, slice(256, 1280)), NT)
    p1_ref[lo, lo] = dot3(part(lo, slice(0, 1280)), part(lo, slice(0, 1280)), NT)
    p1_ref[lo, hi] = p01
    p1_ref[hi, lo] = p01.T
    p1_ref[hi, hi] = dot3(part(hi, slice(256, W)), part(hi, slice(256, W)), NT)
    rules = Rules(s_ref, BR[0], H, H)
    for i in range(H):
        keep, pick = rules.strip(i)
        squared = jnp.where(keep, p1_ref[strip(i), :], 0.0)
        p1_ref[strip(i), :] = jnp.where(pick, 2.0 * r_ref[strip(i), mid] - squared, squared)


def second_kernel(s_ref, p1_ref, g0_ref, pg_ref, tr_ref, xa, xb,
                  own_ref, far_ref, near_ref, sums_ref, t_ref, g_ref, mh, ml):
    core, col, upper = s_ref[1], s_ref[2], s_ref[3]
    lane = lax.broadcasted_iota(jnp.int32, (B, 256), 1)
    t_ref[pl.ds(pl.multiple_of(core * HALF, 8), HALF), :] = xa[...]
    t_ref[pl.ds(pl.multiple_of((1 - core) * HALF, 8), HALF), :] = xb[...]
    zero = jnp.zeros((B, 256), F32)
    base, other = H * (1 - upper), H * upper

    def at(block, size):
        return pl.ds(pl.multiple_of(block * B, B), size)

    def row(block, size=B):
        return at(block + 1, size)

    def lanes(block):
        return pl.ds(pl.multiple_of(block * B, 128), N)

    rules = Rules(s_ref, BR[0], H + H * upper, H * upper)
    outer = jnp.zeros((1, N), F32)
    inner = jnp.zeros((1, N), F32)
    for i in range(H):
        if i < 4:
            left = zero
            if i < 3:
                left = jnp.where(lane >= (i + 1) * B, t_ref[strip(4 + i), :], 0.0)
            right = t_ref[strip(i), :]
        else:
            left = right = zero
            if i < 7:
                turned = pltpu.roll(t_ref[strip(10 - i), :], (i - 3) * B, 1)
                right = jnp.where(lane >= (i - 3) * B, turned, 0.0)
        keep, pick = rules.strip(i)
        squared = pg_ref[strip(i), :] + jnp.concatenate([left, right], axis=1)
        squared = jnp.where(keep, squared, 0.0)
        new = jnp.where(pick, 2.0 * g0_ref[strip(i), :] - squared, squared)
        g_ref[strip(i), :] = new
        outer += jnp.sum(new * new, axis=0, keepdims=True)
        mh[row(H + i), 0:N], ml[row(H + i), 0:N] = halves(new)
        new = p1_ref[strip(i), :]
        inner += jnp.sum(new * new, axis=0, keepdims=True)
        mh[row(base + i), lanes(base)], ml[row(base + i), lanes(base)] = halves(new)
    mh[row(0, N), N : 2 * N], ml[row(0, N), N : 2 * N] = halves(g_ref[...].T)
    blank = jnp.zeros((N, N), BF16)
    mh[row(other, N), lanes(other)] = blank
    ml[row(other, N), lanes(other)] = blank

    spot = lax.broadcasted_iota(jnp.int32, (1, 128), 1)
    both = jnp.where(spot == 0, tr_ref[...], 0.0)
    both = jnp.where(spot == 1, jnp.sum(inner, axis=1, keepdims=True), both)
    both = jnp.where(spot == 2, jnp.sum(outer, axis=1, keepdims=True), both)
    sums_ref[...] = jnp.broadcast_to(both, sums_ref.shape)

    wide = (lax.broadcasted_iota(jnp.int32, (B, 128), 1) >= B).astype(jnp.int32)
    shift = 6 - 2 * col

    def share(i, rows, panel):
        block = rows + i + shift
        pair = row(jnp.clip(block, -1, 2 * H - 1), 128)
        span = lanes(panel)
        product = dot3(
            (mh[row(rows + i), span], ml[row(rows + i), span]),
            (mh[pair, span], ml[pair, span]), NT,
        )
        index = block + wide - base
        return jnp.where((index >= 0) & (index < H), product, 0.0)

    for i in range(H):
        far_ref[strip(i), :] = share(i, other, base)
        near_ref[strip(i), :] = share(i, base, other)
        here = row(base + i)
        block = base + i + 2 * col - H
        pair = row(block, 128)
        own_ref[0, strip(i), :] = dot3((mh[here, :], ml[here, :]), (mh[pair, :], ml[pair, :]), NT)
        if i % 2:
            span = pl.ds(pl.multiple_of((block - 1) * B, 128), 256)
            held = mh[here, span].astype(F32) + ml[here, span].astype(F32)
            held = held[:, B : B + 128]
        else:
            span = pl.ds(pl.multiple_of(block * B, 128), 128)
            held = mh[here, span].astype(F32) + ml[here, span].astype(F32)
        own_ref[1, strip(i), :] = held


def last_kernel(s_ref, own_ref, far_ref, near_ref, sums_ref, out_ref, traces_ref):
    col, upper = s_ref[2], s_ref[3]
    wide = lax.broadcasted_iota(jnp.int32, (B, 128), 1) >= B
    for i in range(H):
        squared = own_ref[0, strip(i), :] + (far_ref[strip(i), :] + near_ref[strip(i), :])
        keep, pick = [], []
        for h in range(2):
            far = jnp.abs(2 * col + h - H)
            reach = jnp.minimum(s_ref[RAD + H + i], s_ref[RAD + i + 2 * col + h])
            keep.append((far <= reach).astype(F32))
            pick.append((s_ref[BR[1] + H + i] * s_ref[BR[1] + i + 2 * col + h]).astype(F32))
        squared = squared * jnp.where(wide, keep[1], keep[0])
        chosen = jnp.where(wide, pick[1], pick[0]) == 1.0
        new = jnp.where(chosen, 2.0 * own_ref[1, strip(i), :] - squared, squared)
        out_ref[i, 0] = new[:, :B]
        out_ref[i, 1] = new[:, B:]
    sums = sums_ref[...]
    count = sums.shape[0]
    spot = lax.broadcasted_iota(jnp.int32, sums.shape, 1)
    line = lax.broadcasted_iota(jnp.int32, sums.shape, 0)
    turned = jnp.concatenate([sums[count - 1 :], sums[: count - 1]], axis=0)
    sums = jnp.where((spot == 2) & (upper + 0 * line == 1), turned, sums)
    total = jnp.sum(sums, axis=0, keepdims=True)
    spot = lax.broadcasted_iota(jnp.int32, total.shape, 1)
    weight = jnp.where(spot == 1, 1.0, jnp.where(spot == 2, 2.0, 0.0))
    traces_ref[0] = jnp.sum(jnp.where(spot == 0, total, 0.0))
    traces_ref[1] = jnp.sum(total * weight)


def shape(*dims):
    return jax.ShapeDtypeStruct(dims, F32)


def per_device(rows, values, radius, branch):
    both = ("row", "col")
    row, col = lax.axis_index("row"), lax.axis_index("col")
    pad = ((H, H),)
    radii = lax.dynamic_slice(jnp.pad(radius, pad, constant_values=-1), (H * row,), (3 * H,))
    flags = lax.dynamic_slice(jnp.pad(branch, ((0, 0),) + pad), (0, H * row), (2, 3 * H))
    scalars = jnp.concatenate(
        [jnp.stack([col // 2, col % 2, col, col // 4]).astype(jnp.int32), radii, flags[0], flags[1]]
    )

    def swap(x):
        return lax.ppermute(x, "col", [(c, c ^ 1) for c in range(8)])

    def to_rows(x, pairs):
        return lax.ppermute(x, both, pairs)

    packed = pl.pallas_call(
        pack_kernel, out_shape=shape(N, 128), in_specs=[VMEM], out_specs=VMEM, name="pack",
        compiler_params=params(16),
    )(values)
    mine = [packed] + [
        lax.ppermute(packed, "col", [(c, (c + 2 * k) % 8) for c in range(8)]) for k in (1, 2, 3)
    ]
    others = [swap(x) for x in mine]

    inner, old, product, send, trace = pl.pallas_call(
        square_kernel,
        out_shape=[shape(N, N)] * 3 + [shape(HALF, 256), shape(1, 128)],
        in_specs=[SMEM] + [VMEM] * 8,
        out_specs=[VMEM] * 5,
        scratch_shapes=[
            pltpu.VMEM((N, 2 * N), F32),
            pltpu.VMEM((N, W), F32),
            pltpu.VMEM((N, W), BF16),
            pltpu.VMEM((N, W), BF16),
            pltpu.VMEM((2 * HALF, 256), F32),
        ],
        compiler_params=params(48),
        name="square",
    )(scalars, *mine, *others)

    def index(r, c):
        return r * 8 + c

    ends = [(r, c) for r in range(rows - 1) for c in range(4)]
    pairs = [(index(r, c + 4), index(r + 1, c)) for r, c in ends]
    xa = lax.ppermute(send, both, pairs + [(b, a) for a, b in pairs])
    xb = swap(xa)

    own, far, near, sums = pl.pallas_call(
        second_kernel,
        out_shape=[shape(2, N, 128), shape(N, 128), shape(N, 128), shape(rows, 128)],
        in_specs=[SMEM] + [VMEM] * 6,
        out_specs=[VMEM] * 4,
        scratch_shapes=[
            pltpu.VMEM((2 * HALF, 256), F32),
            pltpu.VMEM((N, N), F32),
            pltpu.VMEM((18 * B, 2 * N), BF16),
            pltpu.VMEM((18 * B, 2 * N), BF16),
        ],
        compiler_params=params(48),
        name="second",
    )(scalars, inner, old, product, trace, xa, xb)

    pairs = [(index(r, 7 - c), index(r + 1, c)) for r, c in ends]
    far = lax.ppermute(far, both, pairs + [(b, a) for a, b in pairs])
    near = lax.ppermute(near, "col", [(c, 7 - c) for c in range(8)])
    sums = lax.all_to_all(sums, "row", 0, 0, tiled=True)
    return pl.pallas_call(
        last_kernel,
        out_shape=[shape(H, 2, B, B), shape(2)],
        in_specs=[SMEM] + [VMEM] * 4,
        out_specs=[VMEM, SMEM],
        compiler_params=params(16),
        name="last",
    )(scalars, own, far, near, sums)


def solution(mesh):
    rows = mesh.shape["row"]

    def run(values, radius, branch):
        return per_device(rows, values, radius, branch)

    in_specs = (P("row", "col", None, None), P(), P())
    out_specs = (P("row", "col", None, None), P())
    return jax.shard_map(
        run, mesh=mesh, in_specs=in_specs, out_specs=out_specs, check_vma=False
    )
```

```python
import jax
import jax.numpy as jnp
from jax import lax
from jax.experimental import pallas as pl
from jax.experimental.pallas import tpu as pltpu
from jax.sharding import PartitionSpec as P

F32 = jnp.float32
BF16 = jnp.bfloat16
B = 64
H = 8
N = H * B
W = 3 * N
VMEM = pl.BlockSpec(memory_space=pltpu.VMEM)
SMEM = pl.BlockSpec(memory_space=pltpu.SMEM)
RAD, BR = 4, (28, 52)


def params(mib):
    return pltpu.CompilerParams(vmem_limit_bytes=mib << 20)


def halves(x):
    hi = x.astype(BF16)
    return hi, (x - hi.astype(F32)).astype(BF16)


def dot3(a, b, dims):
    (ah, al), (bh, bl) = a, b

    def one(x, y):
        return lax.dot_general(x, y, (dims, ((), ())), preferred_element_type=F32)

    return one(ah, bh) + (one(ah, bl) + one(al, bh))


NN = ((1,), (0,))
NT = ((1,), (1,))


def strip(i):
    return slice(i * B, (i + 1) * B)


class Rules:
    def __init__(self, s_ref, start, rows, cols):
        self.s_ref, self.start, self.rows, self.cols = s_ref, start, rows, cols
        block = lax.shift_right_logical(lax.broadcasted_iota(jnp.int32, (1, N), 1), 6)
        radii = flags = jnp.zeros((1, N), jnp.int32)
        for k in range(H):
            radii = jnp.where(block == k, s_ref[RAD + cols + k], radii)
            flags = jnp.where(block == k, s_ref[start + cols + k], flags)
        self.block, self.radii, self.flags = block + cols, radii, flags

    def strip(self, i):
        reach = jnp.minimum(self.radii, self.s_ref[RAD + self.rows + i])
        keep = jnp.abs(self.block - (self.rows + i)) <= reach
        return keep, self.flags * self.s_ref[self.start + self.rows + i] == 1


def pack_kernel(v_ref, out_ref, diag_ref):
    for i in range(H):
        out_ref[strip(i), :] = jnp.concatenate([v_ref[i, 0], v_ref[i, 1]], axis=1)
    for i in range(4):
        diag_ref[strip(i), :] = jnp.concatenate([v_ref[i, 0], v_ref[i + 4, 0]], axis=1)


def triangle_kernel(s_ref, own_ref, near_ref, d1_ref, d2_ref, out_ref, low, high):
    odd, core, upper = (s_ref[0] & 1) == 1, s_ref[1], s_ref[3]
    low[...] = jnp.where(odd, near_ref[...], own_ref[...])
    high[...] = jnp.where(odd, own_ref[...], near_ref[...])

    def rows(ref, first, last):
        return ref[first * B : (last + 1) * B, :]

    @pl.when((upper == 0) & (core == 0))
    def _():
        out_ref[0:256, :] = rows(high, 3, 6)
        out_ref[256:512, :] = d1_ref[...] + d2_ref[...]
        out_ref[512:640, :] = jnp.zeros((128, 128), F32)

    @pl.when((upper == 0) & (core == 1))
    def _():
        out_ref[0:384, :] = rows(high, 1, 6)
        out_ref[384:512, :] = rows(low, 5, 6)
        out_ref[512:640, :] = jnp.zeros((128, 128), F32)

    @pl.when((upper == 1) & (core == 0))
    def _():
        out_ref[0:448, :] = rows(low, 1, 7)
        out_ref[448:640, :] = rows(high, 1, 3)

    @pl.when((upper == 1) & (core == 1))
    def _():
        out_ref[0:320, :] = rows(low, 1, 5)
        out_ref[320:384, :] = rows(high, 1, 1)
        out_ref[384:640, :] = jnp.zeros((256, 128), F32)


def square_kernel(s_ref, *refs):
    packs, (p1_ref, v_ref, vh_ref, vl_ref, pv_ref, tr_ref) = refs[:8], refs[8:14]
    q_ref, r_ref, rh, rl = refs[14:]
    yl, core, upper = s_ref[0], s_ref[1], s_ref[3]
    for k in range(4):
        for other in range(2):
            place = 2 * (yl ^ k) + (core ^ other)
            q_ref[:, pl.ds(pl.multiple_of(place * 128, 128), 128)] = packs[4 * other + k][...]
    total = jnp.zeros((1, 2 * N), F32)
    for i in range(H):
        own = q_ref[strip(i), :]
        total += jnp.sum(own * own, axis=0, keepdims=True)
        at = i * B
        if i % 2:
            own = pltpu.roll(jnp.concatenate([own, jnp.zeros((B, 128), F32)], axis=1), B, 1)
            at -= B
        parts = [own]
        if at:
            parts.insert(0, jnp.zeros((B, at), F32))
        left = W - at - own.shape[1]
        if left:
            parts.append(jnp.zeros((B, left), F32))
        full = jnp.concatenate(parts, axis=1)
        r_ref[strip(i), :] = full
        rh[strip(i), :], rl[strip(i), :] = halves(full)
    tr_ref[...] = jnp.broadcast_to(jnp.sum(total, axis=1, keepdims=True), tr_ref.shape)

    def part(rows, cols):
        return rh[rows, cols], rl[rows, cols]

    lo, hi = slice(0, 256), slice(256, 512)
    mid = slice(N, 2 * N)
    side = pl.ds(pl.multiple_of(2 * N * upper, 128), N)
    v_ref[...] = r_ref[:, side]
    vh_ref[...], vl_ref[...] = rh[:, side], rl[:, side]
    pv_ref[...] = dot3(part(slice(None), mid), (vh_ref[...], vl_ref[...]), NN)

    p01 = dot3(part(lo, slice(256, 1280)), part(hi, slice(256, 1280)), NT)
    p1_ref[lo, lo] = dot3(part(lo, slice(0, 1280)), part(lo, slice(0, 1280)), NT)
    p1_ref[lo, hi] = p01
    p1_ref[hi, lo] = p01.T
    p1_ref[hi, hi] = dot3(part(hi, slice(256, W)), part(hi, slice(256, W)), NT)
    rules = Rules(s_ref, BR[0], H, H)
    for i in range(H):
        keep, pick = rules.strip(i)
        squared = jnp.where(keep, p1_ref[strip(i), :], 0.0)
        p1_ref[strip(i), :] = jnp.where(pick, 2.0 * r_ref[strip(i), mid] - squared, squared)


def second_kernel(s_ref, p1_ref, v_ref, vh_ref, vl_ref, pv_ref, tr_ref, ta, tb,
                  own_ref, far_ref, near_ref, sums_ref, t_ref, w_ref, mh, ml):
    core, col, upper = s_ref[1], s_ref[2], s_ref[3]
    lane = lax.broadcasted_iota(jnp.int32, (B, N), 1)
    zero = jnp.zeros((B, 128), F32)
    base, other = H * (1 - upper), H * upper
    t_ref[core, :, :] = ta[...]
    t_ref[1 - core, :, :] = tb[...]

    def line(which, start):
        return t_ref[which, start * B : (start + 1) * B, :]

    @pl.when(upper == 0)
    def _():
        w_ref[strip(0), :] = jnp.zeros((B, N), F32)
        for k in range(1, H):
            parts = [line(0, k - 1), zero, zero, zero]
            if k < 6:
                parts[1] = line(1, k - 1)
            if k < 4:
                parts[2] = line(0, 6 + k)
            if k < 2:
                parts[3] = line(1, 4 + k)
            turned = pltpu.roll(jnp.concatenate(parts, axis=1), k * B, 1)
            w_ref[strip(k), :] = jnp.where(lane >= k * B, turned, 0.0)

    @pl.when(upper == 1)
    def _():
        w_ref[strip(7), :] = jnp.zeros((B, N), F32)
        for k in range(7):
            diag = line(0, 4 + k % 4)
            if k >= 4:
                diag = pltpu.roll(diag, B, 1)
            parts = [zero, zero, zero, diag]
            if k >= 5:
                parts[0] = line(1, k + 1)
            if k >= 3:
                parts[1] = line(0, k - 3)
            if k >= 1:
                parts[2] = line(1, k - 1)
            turned = pltpu.roll(jnp.concatenate(parts, axis=1), ((k + 2) % 8) * B, 1)
            w_ref[strip(k), :] = jnp.where(lane < (k + 1) * B, turned, 0.0)

    full = w_ref[...]
    above = lax.shift_right_logical(lax.broadcasted_iota(jnp.int32, (N, N), 0), 6)
    along = lax.shift_right_logical(lax.broadcasted_iota(jnp.int32, (N, N), 1), 6)
    full = jnp.where(above == along, full, full + full.T)
    w_ref[...] = pv_ref[...] + dot3((vh_ref[...], vl_ref[...]), halves(full), NN)

    def at(block, size):
        return pl.ds(pl.multiple_of(block * B, B), size)

    def row(block, size=B):
        return at(block + 1, size)

    def lanes(block):
        return pl.ds(pl.multiple_of(block * B, 128), N)

    rules = Rules(s_ref, BR[0], H, 2 * H * upper)
    inner = jnp.zeros((1, N), F32)
    for i in range(H):
        keep, pick = rules.strip(i)
        squared = jnp.where(keep, w_ref[strip(i), :], 0.0)
        new = jnp.where(pick, 2.0 * v_ref[strip(i), :] - squared, squared)
        w_ref[strip(i), :] = new
        here = row(base + i)
        mh[here, lanes(other)], ml[here, lanes(other)] = halves(new)
        new = p1_ref[strip(i), :]
        inner += jnp.sum(new * new, axis=0, keepdims=True)
        mh[here, lanes(base)], ml[here, lanes(base)] = halves(new)
    turned = w_ref[...].T
    there = row(other, N)
    mh[there, lanes(base)], ml[there, lanes(base)] = halves(turned)
    blank = jnp.zeros((N, N), BF16)
    mh[there, lanes(other)] = blank
    ml[there, lanes(other)] = blank

    @pl.when(upper == 1)
    def _():
        w_ref[...] = turned

    outer = jnp.zeros((1, N), F32)
    for i in range(H):
        outer += jnp.sum(w_ref[strip(i), :] * w_ref[strip(i), :], axis=0, keepdims=True)

    spot = lax.broadcasted_iota(jnp.int32, (1, 128), 1)
    both = jnp.where(spot == 0, tr_ref[...], 0.0)
    both = jnp.where(spot == 1, jnp.sum(inner, axis=1, keepdims=True), both)
    both = jnp.where(spot == 2, jnp.sum(outer, axis=1, keepdims=True), both)
    sums_ref[...] = jnp.broadcast_to(both, sums_ref.shape)

    wide = (lax.broadcasted_iota(jnp.int32, (B, 128), 1) >= B).astype(jnp.int32)
    shift = 6 - 2 * col

    def share(i, rows, panel):
        block = rows + i + shift
        pair = row(jnp.clip(block, -1, 2 * H - 1), 128)
        span = lanes(panel)
        product = dot3(
            (mh[row(rows + i), span], ml[row(rows + i), span]),
            (mh[pair, span], ml[pair, span]), NT,
        )
        index = block + wide - base
        return jnp.where((index >= 0) & (index < H), product, 0.0)

    for i in range(H):
        far_ref[strip(i), :] = share(i, other, base)
        near_ref[strip(i), :] = share(i, base, other)
        here = row(base + i)
        block = base + i + 2 * col - H
        pair = row(block, 128)
        own_ref[0, strip(i), :] = dot3((mh[here, :], ml[here, :]), (mh[pair, :], ml[pair, :]), NT)
        if i % 2:
            span = pl.ds(pl.multiple_of((block - 1) * B, 128), 256)
            held = mh[here, span].astype(F32) + ml[here, span].astype(F32)
            held = held[:, B : B + 128]
        else:
            span = pl.ds(pl.multiple_of(block * B, 128), 128)
            held = mh[here, span].astype(F32) + ml[here, span].astype(F32)
        own_ref[1, strip(i), :] = held


def last_kernel(s_ref, own_ref, far_ref, near_ref, sums_ref, out_ref, traces_ref):
    col, upper = s_ref[2], s_ref[3]
    wide = lax.broadcasted_iota(jnp.int32, (B, 128), 1) >= B
    for i in range(H):
        squared = own_ref[0, strip(i), :] + (far_ref[strip(i), :] + near_ref[strip(i), :])
        keep, pick = [], []
        for h in range(2):
            far = jnp.abs(2 * col + h - H)
            reach = jnp.minimum(s_ref[RAD + H + i], s_ref[RAD + i + 2 * col + h])
            keep.append((far <= reach).astype(F32))
            pick.append((s_ref[BR[1] + H + i] * s_ref[BR[1] + i + 2 * col + h]).astype(F32))
        squared = squared * jnp.where(wide, keep[1], keep[0])
        chosen = jnp.where(wide, pick[1], pick[0]) == 1.0
        new = jnp.where(chosen, 2.0 * own_ref[1, strip(i), :] - squared, squared)
        out_ref[i, 0] = new[:, :B]
        out_ref[i, 1] = new[:, B:]
    sums = sums_ref[...]
    count = sums.shape[0]
    spot = lax.broadcasted_iota(jnp.int32, sums.shape, 1)
    line = lax.broadcasted_iota(jnp.int32, sums.shape, 0)
    turned = jnp.concatenate([sums[count - 1 :], sums[: count - 1]], axis=0)
    sums = jnp.where((spot == 2) & (upper + 0 * line == 1), turned, sums)
    total = jnp.sum(sums, axis=0, keepdims=True)
    spot = lax.broadcasted_iota(jnp.int32, total.shape, 1)
    weight = jnp.where(spot == 1, 1.0, jnp.where(spot == 2, 2.0, 0.0))
    traces_ref[0] = jnp.sum(jnp.where(spot == 0, total, 0.0))
    traces_ref[1] = jnp.sum(total * weight)


def shape(*dims):
    return jax.ShapeDtypeStruct(dims, F32)


def per_device(rows, values, radius, branch):
    both = ("row", "col")
    row, col = lax.axis_index("row"), lax.axis_index("col")
    pad = ((H, H),)
    radii = lax.dynamic_slice(jnp.pad(radius, pad, constant_values=-1), (H * row,), (3 * H,))
    flags = lax.dynamic_slice(jnp.pad(branch, ((0, 0),) + pad), (0, H * row), (2, 3 * H))
    scalars = jnp.concatenate(
        [jnp.stack([col // 2, col % 2, col, col // 4]).astype(jnp.int32), radii, flags[0], flags[1]]
    )

    def swap(x):
        return lax.ppermute(x, "col", [(c, c ^ 1) for c in range(8)])

    def to_rows(x, pairs):
        return lax.ppermute(x, both, pairs)

    def index(r, c):
        return r * 8 + c

    ends = [(r, c) for r in range(rows - 1) for c in range(4)]

    packed, diag = pl.pallas_call(
        pack_kernel, out_shape=[shape(N, 128), shape(256, 128)], in_specs=[VMEM],
        out_specs=[VMEM] * 2, compiler_params=params(16), name="pack",
    )(values)
    near = lax.ppermute(packed, "col", [(c, c ^ 2) for c in range(8)])
    cross = lax.ppermute(packed, "col", [(c, c ^ 4) for c in range(8)])
    d1 = lax.ppermute(diag, "col", [(4, 2)])
    d2 = lax.ppermute(diag, "col", [(4, 0)])
    triangle = pl.pallas_call(
        triangle_kernel,
        out_shape=shape(640, 128),
        in_specs=[SMEM] + [VMEM] * 4,
        out_specs=VMEM,
        scratch_shapes=[pltpu.VMEM((N, 128), F32)] * 2,
        compiler_params=params(16),
        name="triangle",
    )(scalars, packed, near, d1, d2)
    pairs = [(index(r, c + 4), index(r + 1, c)) for r, c in ends]
    ta = lax.ppermute(triangle, both, pairs + [(b, a) for a, b in pairs])
    forward = lax.ppermute(cross, "col", [(c, c ^ 2) for c in range(8)])
    mine = [packed, near, cross, forward]
    others = [swap(x) for x in mine]
    tb = swap(ta)

    *old, trace = pl.pallas_call(
        square_kernel,
        out_shape=[
            shape(N, N), shape(N, N), jax.ShapeDtypeStruct((N, N), BF16),
            jax.ShapeDtypeStruct((N, N), BF16), shape(N, N), shape(1, 128),
        ],
        in_specs=[SMEM] + [VMEM] * 8,
        out_specs=[VMEM] * 6,
        scratch_shapes=[
            pltpu.VMEM((N, 2 * N), F32),
            pltpu.VMEM((N, W), F32),
            pltpu.VMEM((N, W), BF16),
            pltpu.VMEM((N, W), BF16),
        ],
        compiler_params=params(48),
        name="square",
    )(scalars, *mine, *others)

    own, far, near, sums = pl.pallas_call(
        second_kernel,
        out_shape=[shape(2, N, 128), shape(N, 128), shape(N, 128), shape(rows, 128)],
        in_specs=[SMEM] + [VMEM] * 8,
        out_specs=[VMEM] * 4,
        scratch_shapes=[
            pltpu.VMEM((2, 640, 128), F32),
            pltpu.VMEM((N, N), F32),
            pltpu.VMEM((18 * B, 2 * N), BF16),
            pltpu.VMEM((18 * B, 2 * N), BF16),
        ],
        compiler_params=params(48),
        name="second",
    )(scalars, *old, trace, ta, tb)

    pairs = [(index(r, 7 - c), index(r + 1, c)) for r, c in ends]
    far = lax.ppermute(far, both, pairs + [(b, a) for a, b in pairs])
    near = lax.ppermute(near, "col", [(c, 7 - c) for c in range(8)])
    sums = lax.all_to_all(sums, "row", 0, 0, tiled=True)
    return pl.pallas_call(
        last_kernel,
        out_shape=[shape(H, 2, B, B), shape(2)],
        in_specs=[SMEM] + [VMEM] * 4,
        out_specs=[VMEM, SMEM],
        compiler_params=params(16),
        name="last",
    )(scalars, own, far, near, sums)


def solution(mesh):
    rows = mesh.shape["row"]

    def run(values, radius, branch):
        return per_device(rows, values, radius, branch)

    in_specs = (P("row", "col", None, None), P(), P())
    out_specs = (P("row", "col", None, None), P())
    return jax.shard_map(
        run, mesh=mesh, in_specs=in_specs, out_specs=out_specs, check_vma=False
    )
```

```python
import jax
import jax.numpy as jnp
from jax import lax
from jax.experimental import pallas as pl
from jax.experimental.pallas import tpu as pltpu
from jax.sharding import PartitionSpec as P

F32 = jnp.float32
BF16 = jnp.bfloat16
B = 64
H = 8
N = H * B
W = 3 * N
VMEM = pl.BlockSpec(memory_space=pltpu.VMEM)
SMEM = pl.BlockSpec(memory_space=pltpu.SMEM)
RAD, BR = 4, (28, 52)


def params(mib):
    return pltpu.CompilerParams(vmem_limit_bytes=mib << 20)


def halves(x):
    hi = x.astype(BF16)
    return hi, (x - hi.astype(F32)).astype(BF16)


def dot3(a, b, dims):
    (ah, al), (bh, bl) = a, b

    def one(x, y):
        return lax.dot_general(x, y, (dims, ((), ())), preferred_element_type=F32)

    return one(ah, bh) + (one(ah, bl) + one(al, bh))


NN = ((1,), (0,))
NT = ((1,), (1,))


def strip(i):
    return slice(i * B, (i + 1) * B)


class Rules:
    def __init__(self, s_ref, start, rows, cols):
        self.s_ref, self.start, self.rows, self.cols = s_ref, start, rows, cols
        block = lax.shift_right_logical(lax.broadcasted_iota(jnp.int32, (1, N), 1), 6)
        radii = flags = jnp.zeros((1, N), jnp.int32)
        for k in range(H):
            radii = jnp.where(block == k, s_ref[RAD + cols + k], radii)
            flags = jnp.where(block == k, s_ref[start + cols + k], flags)
        self.block, self.radii, self.flags = block + cols, radii, flags

    def strip(self, i):
        reach = jnp.minimum(self.radii, self.s_ref[RAD + self.rows + i])
        keep = jnp.abs(self.block - (self.rows + i)) <= reach
        return keep, self.flags * self.s_ref[self.start + self.rows + i] == 1


def pack_kernel(v_ref, out_ref, diag_ref):
    for i in range(H):
        out_ref[strip(i), :] = jnp.concatenate([v_ref[i, 0], v_ref[i, 1]], axis=1)
    for i in range(4):
        diag_ref[strip(i), :] = jnp.concatenate([v_ref[i, 0], v_ref[i + 4, 0]], axis=1)


def triangle_kernel(s_ref, own_ref, near_ref, d1_ref, d2_ref, out_ref, low, high):
    odd, core, upper = (s_ref[0] & 1) == 1, s_ref[1], s_ref[3]
    low[...] = jnp.where(odd, near_ref[...], own_ref[...])
    high[...] = jnp.where(odd, own_ref[...], near_ref[...])

    def rows(ref, first, last):
        return ref[first * B : (last + 1) * B, :]

    @pl.when((upper == 0) & (core == 0))
    def _():
        out_ref[0:256, :] = rows(high, 3, 6)
        out_ref[256:512, :] = d1_ref[...] + d2_ref[...]
        out_ref[512:640, :] = jnp.zeros((128, 128), F32)

    @pl.when((upper == 0) & (core == 1))
    def _():
        out_ref[0:384, :] = rows(high, 1, 6)
        out_ref[384:512, :] = rows(low, 5, 6)
        out_ref[512:640, :] = jnp.zeros((128, 128), F32)

    @pl.when((upper == 1) & (core == 0))
    def _():
        out_ref[0:448, :] = rows(low, 1, 7)
        out_ref[448:640, :] = rows(high, 1, 3)

    @pl.when((upper == 1) & (core == 1))
    def _():
        out_ref[0:320, :] = rows(low, 1, 5)
        out_ref[320:384, :] = rows(high, 1, 1)
        out_ref[384:640, :] = jnp.zeros((256, 128), F32)


def square_kernel(s_ref, *refs):
    packs, (p1_ref, v_ref, vh_ref, vl_ref, pv_ref, tr_ref) = refs[:8], refs[8:14]
    q_ref, r_ref, rh, rl = refs[14:]
    yl, core, upper = s_ref[0], s_ref[1], s_ref[3]
    for k in range(4):
        for other in range(2):
            place = 2 * (yl ^ k) + (core ^ other)
            q_ref[:, pl.ds(pl.multiple_of(place * 128, 128), 128)] = packs[4 * other + k][...]
    total = jnp.zeros((1, 2 * N), F32)
    for i in range(H):
        own = q_ref[strip(i), :]
        total += jnp.sum(own * own, axis=0, keepdims=True)
        at = i * B
        if i % 2:
            own = pltpu.roll(jnp.concatenate([own, jnp.zeros((B, 128), F32)], axis=1), B, 1)
            at -= B
        parts = [own]
        if at:
            parts.insert(0, jnp.zeros((B, at), F32))
        left = W - at - own.shape[1]
        if left:
            parts.append(jnp.zeros((B, left), F32))
        full = jnp.concatenate(parts, axis=1)
        r_ref[strip(i), :] = full
        rh[strip(i), :], rl[strip(i), :] = halves(full)
    tr_ref[...] = jnp.broadcast_to(jnp.sum(total, axis=1, keepdims=True), tr_ref.shape)

    def part(rows, cols):
        return rh[rows, cols], rl[rows, cols]

    lo, hi = slice(0, 256), slice(256, 512)
    mid = slice(N, 2 * N)
    side = pl.ds(pl.multiple_of(2 * N * upper, 128), N)
    v_ref[...] = r_ref[:, side]
    vh_ref[...], vl_ref[...] = rh[:, side], rl[:, side]
    pv_ref[...] = dot3(part(slice(None), mid), (vh_ref[...], vl_ref[...]), NN)

    p01 = dot3(part(lo, slice(256, 1280)), part(hi, slice(256, 1280)), NT)
    p1_ref[lo, lo] = dot3(part(lo, slice(0, 1280)), part(lo, slice(0, 1280)), NT)
    p1_ref[lo, hi] = p01
    p1_ref[hi, lo] = p01.T
    p1_ref[hi, hi] = dot3(part(hi, slice(256, W)), part(hi, slice(256, W)), NT)
    rules = Rules(s_ref, BR[0], H, H)
    for i in range(H):
        keep, pick = rules.strip(i)
        squared = jnp.where(keep, p1_ref[strip(i), :], 0.0)
        p1_ref[strip(i), :] = jnp.where(pick, 2.0 * r_ref[strip(i), mid] - squared, squared)


def second_kernel(s_ref, p1_ref, v_ref, vh_ref, vl_ref, pv_ref, tr_ref, ta, tb,
                  own_ref, far_ref, near_ref, sums_ref, t_ref, w_ref, mh, ml):
    core, col, upper = s_ref[1], s_ref[2], s_ref[3]
    lane = lax.broadcasted_iota(jnp.int32, (B, N), 1)
    zero = jnp.zeros((B, 128), F32)
    base, other = H * (1 - upper), H * upper
    t_ref[core, :, :] = ta[...]
    t_ref[1 - core, :, :] = tb[...]

    def line(which, start):
        return t_ref[which, start * B : (start + 1) * B, :]

    @pl.when(upper == 0)
    def _():
        w_ref[strip(0), :] = jnp.zeros((B, N), F32)
        for k in range(1, H):
            parts = [line(0, k - 1), zero, zero, zero]
            if k < 6:
                parts[1] = line(1, k - 1)
            if k < 4:
                parts[2] = line(0, 6 + k)
            if k < 2:
                parts[3] = line(1, 4 + k)
            turned = pltpu.roll(jnp.concatenate(parts, axis=1), k * B, 1)
            w_ref[strip(k), :] = jnp.where(lane >= k * B, turned, 0.0)

    @pl.when(upper == 1)
    def _():
        w_ref[strip(7), :] = jnp.zeros((B, N), F32)
        for k in range(7):
            diag = line(0, 4 + k % 4)
            if k >= 4:
                diag = pltpu.roll(diag, B, 1)
            parts = [zero, zero, zero, diag]
            if k >= 5:
                parts[0] = line(1, k + 1)
            if k >= 3:
                parts[1] = line(0, k - 3)
            if k >= 1:
                parts[2] = line(1, k - 1)
            turned = pltpu.roll(jnp.concatenate(parts, axis=1), ((k + 2) % 8) * B, 1)
            w_ref[strip(k), :] = jnp.where(lane < (k + 1) * B, turned, 0.0)

    full = w_ref[...]
    above = lax.shift_right_logical(lax.broadcasted_iota(jnp.int32, (N, N), 0), 6)
    along = lax.shift_right_logical(lax.broadcasted_iota(jnp.int32, (N, N), 1), 6)
    full = jnp.where(above == along, full, full + full.T)
    w_ref[...] = pv_ref[...] + dot3((vh_ref[...], vl_ref[...]), halves(full), NN)

    def at(block, size):
        return pl.ds(pl.multiple_of(block * B, B), size)

    def row(block, size=B):
        return at(block + 1, size)

    def lanes(block):
        return pl.ds(pl.multiple_of(block * B, 128), N)

    rules = Rules(s_ref, BR[0], H, 2 * H * upper)
    inner = jnp.zeros((1, N), F32)
    for i in range(H):
        keep, pick = rules.strip(i)
        squared = jnp.where(keep, w_ref[strip(i), :], 0.0)
        new = jnp.where(pick, 2.0 * v_ref[strip(i), :] - squared, squared)
        w_ref[strip(i), :] = new
        here = row(base + i)
        mh[here, lanes(other)], ml[here, lanes(other)] = halves(new)
        new = p1_ref[strip(i), :]
        inner += jnp.sum(new * new, axis=0, keepdims=True)
        mh[here, lanes(base)], ml[here, lanes(base)] = halves(new)
    turned = w_ref[...].T
    there = row(other, N)
    mh[there, lanes(base)], ml[there, lanes(base)] = halves(turned)
    blank = jnp.zeros((N, N), BF16)
    mh[there, lanes(other)] = blank
    ml[there, lanes(other)] = blank

    @pl.when(upper == 1)
    def _():
        w_ref[...] = turned

    outer = jnp.zeros((1, N), F32)
    for i in range(H):
        outer += jnp.sum(w_ref[strip(i), :] * w_ref[strip(i), :], axis=0, keepdims=True)

    spot = lax.broadcasted_iota(jnp.int32, (1, 128), 1)
    both = jnp.where(spot == 0, tr_ref[...], 0.0)
    both = jnp.where(spot == 1, jnp.sum(inner, axis=1, keepdims=True), both)
    both = jnp.where(spot == 2, jnp.sum(outer, axis=1, keepdims=True), both)
    sums_ref[...] = jnp.broadcast_to(both, sums_ref.shape)

    wide = (lax.broadcasted_iota(jnp.int32, (B, 128), 1) >= B).astype(jnp.int32)
    shift = 6 - 2 * col

    def share(i, rows, panel):
        block = rows + i + shift
        pair = row(jnp.clip(block, -1, 2 * H - 1), 128)
        span = lanes(panel)
        product = dot3(
            (mh[row(rows + i), span], ml[row(rows + i), span]),
            (mh[pair, span], ml[pair, span]), NT,
        )
        index = block + wide - base
        return jnp.where((index >= 0) & (index < H), product, 0.0)

    for i in range(H):
        far_ref[strip(i), :] = share(i, other, base)
        near_ref[strip(i), :] = share(i, base, other)
        here = row(base + i)
        block = base + i + 2 * col - H
        pair = row(block, 128)
        own_ref[0, strip(i), :] = dot3((mh[here, :], ml[here, :]), (mh[pair, :], ml[pair, :]), NT)
        if i % 2:
            span = pl.ds(pl.multiple_of((block - 1) * B, 128), 256)
            held = mh[here, span].astype(F32) + ml[here, span].astype(F32)
            held = held[:, B : B + 128]
        else:
            span = pl.ds(pl.multiple_of(block * B, 128), 128)
            held = mh[here, span].astype(F32) + ml[here, span].astype(F32)
        own_ref[1, strip(i), :] = held


def last_kernel(s_ref, own_ref, far_ref, near_ref, sums_ref, out_ref, traces_ref):
    col, upper = s_ref[2], s_ref[3]
    wide = lax.broadcasted_iota(jnp.int32, (B, 128), 1) >= B
    for i in range(H):
        squared = own_ref[0, strip(i), :] + (far_ref[strip(i), :] + near_ref[strip(i), :])
        keep, pick = [], []
        for h in range(2):
            far = jnp.abs(2 * col + h - H)
            reach = jnp.minimum(s_ref[RAD + H + i], s_ref[RAD + i + 2 * col + h])
            keep.append((far <= reach).astype(F32))
            pick.append((s_ref[BR[1] + H + i] * s_ref[BR[1] + i + 2 * col + h]).astype(F32))
        squared = squared * jnp.where(wide, keep[1], keep[0])
        chosen = jnp.where(wide, pick[1], pick[0]) == 1.0
        new = jnp.where(chosen, 2.0 * own_ref[1, strip(i), :] - squared, squared)
        out_ref[i, 0] = new[:, :B]
        out_ref[i, 1] = new[:, B:]
    sums = sums_ref[...]
    count = sums.shape[0]
    spot = lax.broadcasted_iota(jnp.int32, sums.shape, 1)
    line = lax.broadcasted_iota(jnp.int32, sums.shape, 0)
    turned = jnp.concatenate([sums[count - 1 :], sums[: count - 1]], axis=0)
    sums = jnp.where((spot == 2) & (upper + 0 * line == 1), turned, sums)
    total = jnp.sum(sums, axis=0, keepdims=True)
    spot = lax.broadcasted_iota(jnp.int32, total.shape, 1)
    weight = jnp.where(spot == 1, 1.0, jnp.where(spot == 2, 2.0, 0.0))
    traces_ref[0] = jnp.sum(jnp.where(spot == 0, total, 0.0))
    traces_ref[1] = jnp.sum(total * weight)


def shape(*dims):
    return jax.ShapeDtypeStruct(dims, F32)


def per_device(rows, values, radius, branch):
    both = ("row", "col")
    row, col = lax.axis_index("row"), lax.axis_index("col")
    pad = ((H, H),)
    radii = lax.dynamic_slice(jnp.pad(radius, pad, constant_values=-1), (H * row,), (3 * H,))
    flags = lax.dynamic_slice(jnp.pad(branch, ((0, 0),) + pad), (0, H * row), (2, 3 * H))
    scalars = jnp.concatenate(
        [jnp.stack([col // 2, col % 2, col, col // 4]).astype(jnp.int32), radii, flags[0], flags[1]]
    )

    def swap(x):
        return lax.ppermute(x, "col", [(c, c ^ 1) for c in range(8)])

    def to_rows(x, pairs):
        return lax.ppermute(x, both, pairs)

    def index(r, c):
        return r * 8 + c

    ends = [(r, c) for r in range(rows - 1) for c in range(4)]

    packed, diag = pl.pallas_call(
        pack_kernel, out_shape=[shape(N, 128), shape(256, 128)], in_specs=[VMEM],
        out_specs=[VMEM] * 2, compiler_params=params(8), name="pack",
    )(values)
    near = lax.ppermute(packed, "col", [(c, c ^ 2) for c in range(8)])
    d1 = lax.ppermute(diag, "col", [(4, 2)])
    d2 = lax.ppermute(diag, "col", [(4, 0)])
    later, d1 = lax.optimization_barrier((packed, d1))
    cross = lax.ppermute(later, "col", [(c, c ^ 4) for c in range(8)])
    near, packed2 = lax.optimization_barrier((near, swap(later)))
    triangle = pl.pallas_call(
        triangle_kernel,
        out_shape=shape(640, 128),
        in_specs=[SMEM] + [VMEM] * 4,
        out_specs=VMEM,
        scratch_shapes=[pltpu.VMEM((N, 128), F32)] * 2,
        compiler_params=params(8),
        name="triangle",
    )(scalars, packed, near, d1, d2)
    pairs = [(index(r, c + 4), index(r + 1, c)) for r, c in ends]
    ta = lax.ppermute(triangle, both, pairs + [(b, a) for a, b in pairs])
    near, triangle = lax.optimization_barrier((near, triangle))
    cross, near2 = lax.optimization_barrier((cross, swap(near)))
    forward = lax.ppermute(cross, "col", [(c, c ^ 2) for c in range(8)])
    mine = [packed, near, cross, forward]
    others = [packed2, near2, swap(cross), swap(forward)]

    *old, trace = pl.pallas_call(
        square_kernel,
        out_shape=[
            shape(N, N), shape(N, N), jax.ShapeDtypeStruct((N, N), BF16),
            jax.ShapeDtypeStruct((N, N), BF16), shape(N, N), shape(1, 128),
        ],
        in_specs=[SMEM] + [VMEM] * 8,
        out_specs=[VMEM] * 6,
        scratch_shapes=[
            pltpu.VMEM((N, 2 * N), F32),
            pltpu.VMEM((N, W), F32),
            pltpu.VMEM((N, W), BF16),
            pltpu.VMEM((N, W), BF16),
        ],
        compiler_params=params(24),
        name="square",
    )(scalars, *mine, *others)

    ta, trace = lax.optimization_barrier((ta, trace))
    tb = swap(ta)
    own, far, near, sums = pl.pallas_call(
        second_kernel,
        out_shape=[shape(2, N, 128), shape(N, 128), shape(N, 128), shape(rows, 128)],
        in_specs=[SMEM] + [VMEM] * 8,
        out_specs=[VMEM] * 4,
        scratch_shapes=[
            pltpu.VMEM((2, 640, 128), F32),
            pltpu.VMEM((N, N), F32),
            pltpu.VMEM((18 * B, 2 * N), BF16),
            pltpu.VMEM((18 * B, 2 * N), BF16),
        ],
        compiler_params=params(24),
        name="second",
    )(scalars, *old, trace, ta, tb)

    pairs = [(index(r, 7 - c), index(r + 1, c)) for r, c in ends]
    far = lax.ppermute(far, both, pairs + [(b, a) for a, b in pairs])
    near = lax.ppermute(near, "col", [(c, 7 - c) for c in range(8)])
    sums = lax.all_to_all(sums, "row", 0, 0, tiled=True)
    return pl.pallas_call(
        last_kernel,
        out_shape=[shape(H, 2, B, B), shape(2)],
        in_specs=[SMEM] + [VMEM] * 4,
        out_specs=[VMEM, SMEM],
        compiler_params=params(8),
        name="last",
    )(scalars, own, far, near, sums)


def solution(mesh):
    rows = mesh.shape["row"]

    def run(values, radius, branch):
        return per_device(rows, values, radius, branch)

    in_specs = (P("row", "col", None, None), P(), P())
    out_specs = (P("row", "col", None, None), P())
    return jax.shard_map(
        run, mesh=mesh, in_specs=in_specs, out_specs=out_specs, check_vma=False
    )
```

```python
import jax
import jax.numpy as jnp
from jax import lax
from jax.experimental import pallas as pl
from jax.experimental.pallas import tpu as pltpu
from jax.sharding import PartitionSpec as P

F32 = jnp.float32
BF16 = jnp.bfloat16
B = 64
H = 8
N = H * B
W = 3 * N
VMEM = pl.BlockSpec(memory_space=pltpu.VMEM)
SMEM = pl.BlockSpec(memory_space=pltpu.SMEM)
RAD, BR = 4, (28, 52)


def call(kernel, mib, name, **rest):
    return pl.pallas_call(
        kernel,
        name=name,
        compiler_params=pltpu.CompilerParams(vmem_limit_bytes=mib << 20),
        **rest,
    )


def halves(x):
    hi = x.astype(BF16)
    return hi, (x - hi.astype(F32)).astype(BF16)


def dot3(a, b, dims):
    (ah, al), (bh, bl) = a, b

    def one(x, y):
        return lax.dot_general(x, y, (dims, ((), ())), preferred_element_type=F32)

    return one(ah, bh) + (one(ah, bl) + one(al, bh))


NN = ((1,), (0,))
NT = ((1,), (1,))


def strip(i):
    return slice(i * B, (i + 1) * B)


class Rules:
    def __init__(self, s_ref, start, rows, cols):
        self.s_ref, self.start, self.rows, self.cols = s_ref, start, rows, cols
        block = lax.shift_right_logical(lax.broadcasted_iota(jnp.int32, (1, N), 1), 6)
        radii = flags = jnp.zeros((1, N), jnp.int32)
        for k in range(H):
            radii = jnp.where(block == k, s_ref[RAD + cols + k], radii)
            flags = jnp.where(block == k, s_ref[start + cols + k], flags)
        self.block, self.radii, self.flags = block + cols, radii, flags

    def strip(self, i):
        reach = jnp.minimum(self.radii, self.s_ref[RAD + self.rows + i])
        keep = jnp.abs(self.block - (self.rows + i)) <= reach
        return keep, self.flags * self.s_ref[self.start + self.rows + i] == 1


def pack_kernel(v_ref, out_ref, diag_ref):
    for i in range(H):
        out_ref[strip(i), :] = jnp.concatenate([v_ref[i, 0], v_ref[i, 1]], axis=1)
    for i in range(4):
        diag_ref[strip(i), :] = jnp.concatenate([v_ref[i, 0], v_ref[i + 4, 0]], axis=1)


def triangle_kernel(s_ref, own_ref, near_ref, d1_ref, d2_ref, out_ref, low, high):
    odd, core, upper = (s_ref[0] & 1) == 1, s_ref[1], s_ref[3]
    low[...] = jnp.where(odd, near_ref[...], own_ref[...])
    high[...] = jnp.where(odd, own_ref[...], near_ref[...])

    def rows(ref, first, last):
        return ref[first * B : (last + 1) * B, :]

    @pl.when((upper == 0) & (core == 0))
    def _():
        out_ref[0:256, :] = rows(high, 3, 6)
        out_ref[256:512, :] = d1_ref[...] + d2_ref[...]
        out_ref[512:640, :] = jnp.zeros((128, 128), F32)

    @pl.when((upper == 0) & (core == 1))
    def _():
        out_ref[0:384, :] = rows(high, 1, 6)
        out_ref[384:512, :] = rows(low, 5, 6)
        out_ref[512:640, :] = jnp.zeros((128, 128), F32)

    @pl.when((upper == 1) & (core == 0))
    def _():
        out_ref[0:448, :] = rows(low, 1, 7)
        out_ref[448:640, :] = rows(high, 1, 3)

    @pl.when((upper == 1) & (core == 1))
    def _():
        out_ref[0:320, :] = rows(low, 1, 5)
        out_ref[320:384, :] = rows(high, 1, 1)
        out_ref[384:640, :] = jnp.zeros((256, 128), F32)


def square_kernel(s_ref, *refs):
    packs, (p1_ref, v_ref, vh_ref, vl_ref, pv_ref, tr_ref) = refs[:8], refs[8:14]
    q_ref, r_ref, rh, rl = refs[14:]
    yl, core, upper = s_ref[0], s_ref[1], s_ref[3]
    for k in range(4):
        for other in range(2):
            place = 2 * (yl ^ k) + (core ^ other)
            q_ref[:, pl.ds(pl.multiple_of(place * 128, 128), 128)] = packs[4 * other + k][...]
    total = jnp.zeros((1, 2 * N), F32)
    for i in range(H):
        own = q_ref[strip(i), :]
        total += jnp.sum(own * own, axis=0, keepdims=True)
        at = i * B
        if i % 2:
            own = pltpu.roll(jnp.concatenate([own, jnp.zeros((B, 128), F32)], axis=1), B, 1)
            at -= B
        parts = [own]
        if at:
            parts.insert(0, jnp.zeros((B, at), F32))
        left = W - at - own.shape[1]
        if left:
            parts.append(jnp.zeros((B, left), F32))
        full = jnp.concatenate(parts, axis=1)
        r_ref[strip(i), :] = full
        rh[strip(i), :], rl[strip(i), :] = halves(full)
    tr_ref[...] = jnp.broadcast_to(jnp.sum(total, axis=1, keepdims=True), tr_ref.shape)

    def part(rows, cols):
        return rh[rows, cols], rl[rows, cols]

    lo, hi = slice(0, 256), slice(256, 512)
    mid = slice(N, 2 * N)
    side = pl.ds(pl.multiple_of(2 * N * upper, 128), N)
    v_ref[...] = r_ref[:, side]
    vh_ref[...], vl_ref[...] = rh[:, side], rl[:, side]
    pv_ref[...] = dot3(part(slice(None), mid), (vh_ref[...], vl_ref[...]), NN)

    p01 = dot3(part(lo, slice(256, 1280)), part(hi, slice(256, 1280)), NT)
    p1_ref[lo, lo] = dot3(part(lo, slice(0, 1280)), part(lo, slice(0, 1280)), NT)
    p1_ref[lo, hi] = p01
    p1_ref[hi, lo] = p01.T
    p1_ref[hi, hi] = dot3(part(hi, slice(256, W)), part(hi, slice(256, W)), NT)
    rules = Rules(s_ref, BR[0], H, H)
    for i in range(H):
        keep, pick = rules.strip(i)
        squared = jnp.where(keep, p1_ref[strip(i), :], 0.0)
        p1_ref[strip(i), :] = jnp.where(pick, 2.0 * r_ref[strip(i), mid] - squared, squared)


def second_kernel(s_ref, p1_ref, v_ref, vh_ref, vl_ref, pv_ref, tr_ref, ta, tb,
                  own_ref, far_ref, near_ref, sums_ref, t_ref, w_ref, mh, ml):
    core, col, upper = s_ref[1], s_ref[2], s_ref[3]
    lane = lax.broadcasted_iota(jnp.int32, (B, N), 1)
    zero = jnp.zeros((B, 128), F32)
    base, other = H * (1 - upper), H * upper
    t_ref[core, :, :] = ta[...]
    t_ref[1 - core, :, :] = tb[...]

    def line(which, start):
        return t_ref[which, start * B : (start + 1) * B, :]

    @pl.when(upper == 0)
    def _():
        w_ref[strip(0), :] = jnp.zeros((B, N), F32)
        for k in range(1, H):
            parts = [line(0, k - 1), zero, zero, zero]
            if k < 6:
                parts[1] = line(1, k - 1)
            if k < 4:
                parts[2] = line(0, 6 + k)
            if k < 2:
                parts[3] = line(1, 4 + k)
            turned = pltpu.roll(jnp.concatenate(parts, axis=1), k * B, 1)
            w_ref[strip(k), :] = jnp.where(lane >= k * B, turned, 0.0)

    @pl.when(upper == 1)
    def _():
        w_ref[strip(7), :] = jnp.zeros((B, N), F32)
        for k in range(7):
            diag = line(0, 4 + k % 4)
            if k >= 4:
                diag = pltpu.roll(diag, B, 1)
            parts = [zero, zero, zero, diag]
            if k >= 5:
                parts[0] = line(1, k + 1)
            if k >= 3:
                parts[1] = line(0, k - 3)
            if k >= 1:
                parts[2] = line(1, k - 1)
            turned = pltpu.roll(jnp.concatenate(parts, axis=1), ((k + 2) % 8) * B, 1)
            w_ref[strip(k), :] = jnp.where(lane < (k + 1) * B, turned, 0.0)

    full = w_ref[...]
    above = lax.shift_right_logical(lax.broadcasted_iota(jnp.int32, (N, N), 0), 6)
    along = lax.shift_right_logical(lax.broadcasted_iota(jnp.int32, (N, N), 1), 6)
    full = jnp.where(above == along, full, full + full.T)
    w_ref[...] = pv_ref[...] + dot3((vh_ref[...], vl_ref[...]), halves(full), NN)

    def at(block, size):
        return pl.ds(pl.multiple_of(block * B, B), size)

    def row(block, size=B):
        return at(block + 1, size)

    def lanes(block):
        return pl.ds(pl.multiple_of(block * B, 128), N)

    rules = Rules(s_ref, BR[0], H, 2 * H * upper)
    inner = jnp.zeros((1, N), F32)
    for i in range(H):
        keep, pick = rules.strip(i)
        squared = jnp.where(keep, w_ref[strip(i), :], 0.0)
        new = jnp.where(pick, 2.0 * v_ref[strip(i), :] - squared, squared)
        w_ref[strip(i), :] = new
        here = row(base + i)
        mh[here, lanes(other)], ml[here, lanes(other)] = halves(new)
        new = p1_ref[strip(i), :]
        inner += jnp.sum(new * new, axis=0, keepdims=True)
        mh[here, lanes(base)], ml[here, lanes(base)] = halves(new)
    turned = w_ref[...].T
    there = row(other, N)
    mh[there, lanes(base)], ml[there, lanes(base)] = halves(turned)
    blank = jnp.zeros((N, N), BF16)
    mh[there, lanes(other)] = blank
    ml[there, lanes(other)] = blank

    @pl.when(upper == 1)
    def _():
        w_ref[...] = turned

    outer = jnp.zeros((1, N), F32)
    for i in range(H):
        outer += jnp.sum(w_ref[strip(i), :] * w_ref[strip(i), :], axis=0, keepdims=True)

    spot = lax.broadcasted_iota(jnp.int32, (1, 128), 1)
    both = jnp.where(spot == 0, tr_ref[...], 0.0)
    both = jnp.where(spot == 1, jnp.sum(inner, axis=1, keepdims=True), both)
    both = jnp.where(spot == 2, jnp.sum(outer, axis=1, keepdims=True), both)
    sums_ref[...] = jnp.broadcast_to(both, sums_ref.shape)

    wide = (lax.broadcasted_iota(jnp.int32, (B, 128), 1) >= B).astype(jnp.int32)
    shift = 6 - 2 * col

    def share(i, rows, panel):
        block = rows + i + shift
        pair = row(jnp.clip(block, -1, 2 * H - 1), 128)
        span = lanes(panel)
        product = dot3(
            (mh[row(rows + i), span], ml[row(rows + i), span]),
            (mh[pair, span], ml[pair, span]), NT,
        )
        index = block + wide - base
        return jnp.where((index >= 0) & (index < H), product, 0.0)

    for i in range(H):
        far_ref[strip(i), :] = share(i, other, base)
        near_ref[strip(i), :] = share(i, base, other)
        here = row(base + i)
        block = base + i + 2 * col - H
        pair = row(block, 128)
        own_ref[0, strip(i), :] = dot3((mh[here, :], ml[here, :]), (mh[pair, :], ml[pair, :]), NT)
        if i % 2:
            span = pl.ds(pl.multiple_of((block - 1) * B, 128), 256)
            held = mh[here, span].astype(F32) + ml[here, span].astype(F32)
            held = held[:, B : B + 128]
        else:
            span = pl.ds(pl.multiple_of(block * B, 128), 128)
            held = mh[here, span].astype(F32) + ml[here, span].astype(F32)
        own_ref[1, strip(i), :] = held


def last_kernel(s_ref, own_ref, far_ref, near_ref, sums_ref, out_ref, traces_ref):
    col, upper = s_ref[2], s_ref[3]
    wide = lax.broadcasted_iota(jnp.int32, (B, 128), 1) >= B
    for i in range(H):
        squared = own_ref[0, strip(i), :] + (far_ref[strip(i), :] + near_ref[strip(i), :])
        keep, pick = [], []
        for h in range(2):
            far = jnp.abs(2 * col + h - H)
            reach = jnp.minimum(s_ref[RAD + H + i], s_ref[RAD + i + 2 * col + h])
            keep.append((far <= reach).astype(F32))
            pick.append((s_ref[BR[1] + H + i] * s_ref[BR[1] + i + 2 * col + h]).astype(F32))
        squared = squared * jnp.where(wide, keep[1], keep[0])
        chosen = jnp.where(wide, pick[1], pick[0]) == 1.0
        new = jnp.where(chosen, 2.0 * own_ref[1, strip(i), :] - squared, squared)
        out_ref[i, 0] = new[:, :B]
        out_ref[i, 1] = new[:, B:]
    sums = sums_ref[...]
    count = sums.shape[0]
    spot = lax.broadcasted_iota(jnp.int32, sums.shape, 1)
    line = lax.broadcasted_iota(jnp.int32, sums.shape, 0)
    turned = jnp.concatenate([sums[count - 1 :], sums[: count - 1]], axis=0)
    sums = jnp.where((spot == 2) & (upper + 0 * line == 1), turned, sums)
    total = jnp.sum(sums, axis=0, keepdims=True)
    spot = lax.broadcasted_iota(jnp.int32, total.shape, 1)
    weight = jnp.where(spot == 1, 1.0, jnp.where(spot == 2, 2.0, 0.0))
    traces_ref[0] = jnp.sum(jnp.where(spot == 0, total, 0.0))
    traces_ref[1] = jnp.sum(total * weight)


def shape(*dims):
    return jax.ShapeDtypeStruct(dims, F32)


def per_device(rows, values, radius, branch):
    both = ("row", "col")
    row, col = lax.axis_index("row"), lax.axis_index("col")
    pad = ((H, H),)
    radii = lax.dynamic_slice(jnp.pad(radius, pad, constant_values=-1), (H * row,), (3 * H,))
    flags = lax.dynamic_slice(jnp.pad(branch, ((0, 0),) + pad), (0, H * row), (2, 3 * H))
    scalars = jnp.concatenate(
        [jnp.stack([col // 2, col % 2, col, col // 4]).astype(jnp.int32), radii, flags[0], flags[1]]
    )

    def swap(x):
        return lax.ppermute(x, "col", [(c, c ^ 1) for c in range(8)])

    def to_rows(x, pairs):
        return lax.ppermute(x, both, pairs)

    def index(r, c):
        return r * 8 + c

    ends = [(r, c) for r in range(rows - 1) for c in range(4)]

    packed, diag = call(
        pack_kernel, out_shape=[shape(N, 128), shape(256, 128)], in_specs=[VMEM],
        out_specs=[VMEM] * 2, mib=8, name="pack",
    )(values)
    near = lax.ppermute(packed, "col", [(c, c ^ 2) for c in range(8)])
    d1 = lax.ppermute(diag, "col", [(4, 2)])
    d2 = lax.ppermute(diag, "col", [(4, 0)])
    later, d1 = lax.optimization_barrier((packed, d1))
    cross = lax.ppermute(later, "col", [(c, c ^ 4) for c in range(8)])
    triangle = call(
        triangle_kernel,
        out_shape=shape(640, 128),
        in_specs=[SMEM] + [VMEM] * 4,
        out_specs=VMEM,
        scratch_shapes=[pltpu.VMEM((N, 128), F32)] * 2,
        mib=8, name="triangle",
    )(scalars, packed, near, d1, d2)
    pairs = [(index(r, c + 4), index(r + 1, c)) for r, c in ends]
    ta = lax.ppermute(triangle, both, pairs + [(b, a) for a, b in pairs])
    packed, near, triangle = lax.optimization_barrier((packed, near, triangle))
    packed2, near2 = swap(packed), swap(near)
    cross, packed2, near2 = lax.optimization_barrier((cross, packed2, near2))
    forward = lax.ppermute(cross, "col", [(c, c ^ 2) for c in range(8)])
    forward, ta, cross2 = lax.optimization_barrier((forward, ta, swap(cross)))
    mine = [packed, near, cross, forward]
    others = [packed2, near2, cross2, swap(forward)]

    *old, trace = call(
        square_kernel,
        out_shape=[
            shape(N, N), shape(N, N), jax.ShapeDtypeStruct((N, N), BF16),
            jax.ShapeDtypeStruct((N, N), BF16), shape(N, N), shape(1, 128),
        ],
        in_specs=[SMEM] + [VMEM] * 8,
        out_specs=[VMEM] * 6,
        scratch_shapes=[
            pltpu.VMEM((N, 2 * N), F32),
            pltpu.VMEM((N, W), F32),
            pltpu.VMEM((N, W), BF16),
            pltpu.VMEM((N, W), BF16),
        ],
        mib=24, name="square",
    )(scalars, *mine, *others)

    tb = swap(ta)
    own, far, near, sums = call(
        second_kernel,
        out_shape=[shape(2, N, 128), shape(N, 128), shape(N, 128), shape(rows, 128)],
        in_specs=[SMEM] + [VMEM] * 8,
        out_specs=[VMEM] * 4,
        scratch_shapes=[
            pltpu.VMEM((2, 640, 128), F32),
            pltpu.VMEM((N, N), F32),
            pltpu.VMEM((18 * B, 2 * N), BF16),
            pltpu.VMEM((18 * B, 2 * N), BF16),
        ],
        mib=24, name="second",
    )(scalars, *old, trace, ta, tb)

    pairs = [(index(r, 7 - c), index(r + 1, c)) for r, c in ends]
    far = lax.ppermute(far, both, pairs + [(b, a) for a, b in pairs])
    near = lax.ppermute(near, "col", [(c, 7 - c) for c in range(8)])
    sums = lax.all_to_all(sums, "row", 0, 0, tiled=True)
    return call(
        last_kernel,
        out_shape=[shape(H, 2, B, B), shape(2)],
        in_specs=[SMEM] + [VMEM] * 4,
        out_specs=[VMEM, SMEM],
        mib=8, name="last",
    )(scalars, own, far, near, sums)


def solution(mesh):
    rows = mesh.shape["row"]

    def run(values, radius, branch):
        return per_device(rows, values, radius, branch)

    in_specs = (P("row", "col", None, None), P(), P())
    out_specs = (P("row", "col", None, None), P())
    return jax.shard_map(
        run, mesh=mesh, in_specs=in_specs, out_specs=out_specs, check_vma=False
    )
```

```python
import jax
import jax.numpy as jnp
from jax import lax
from jax.experimental import pallas as pl
from jax.experimental.pallas import tpu as pltpu
from jax.sharding import PartitionSpec as P

F32 = jnp.float32
BF16 = jnp.bfloat16
B = 64
H = 8
N = H * B
W = 3 * N
VMEM = pl.BlockSpec(memory_space=pltpu.VMEM)
SMEM = pl.BlockSpec(memory_space=pltpu.SMEM)
RAD, BR = 4, (28, 52)


def call(kernel, mib, name, **rest):
    return pl.pallas_call(
        kernel,
        name=name,
        compiler_params=pltpu.CompilerParams(vmem_limit_bytes=mib << 20),
        **rest,
    )


def halves(x):
    hi = x.astype(BF16)
    return hi, (x - hi.astype(F32)).astype(BF16)


def dot3(a, b, dims):
    (ah, al), (bh, bl) = a, b

    def one(x, y):
        return lax.dot_general(x, y, (dims, ((), ())), preferred_element_type=F32)

    return one(ah, bh) + (one(ah, bl) + one(al, bh))


NN = ((1,), (0,))
NT = ((1,), (1,))


def strip(i):
    return slice(i * B, (i + 1) * B)


class Rules:
    def __init__(self, s_ref, start, rows, cols):
        self.s_ref, self.start, self.rows, self.cols = s_ref, start, rows, cols
        block = lax.shift_right_logical(lax.broadcasted_iota(jnp.int32, (1, N), 1), 6)
        radii = flags = jnp.zeros((1, N), jnp.int32)
        for k in range(H):
            radii = jnp.where(block == k, s_ref[RAD + cols + k], radii)
            flags = jnp.where(block == k, s_ref[start + cols + k], flags)
        self.block, self.radii, self.flags = block + cols, radii, flags

    def strip(self, i):
        reach = jnp.minimum(self.radii, self.s_ref[RAD + self.rows + i])
        keep = jnp.abs(self.block - (self.rows + i)) <= reach
        return keep, self.flags * self.s_ref[self.start + self.rows + i] == 1


def pack_kernel(v_ref, out_ref, diag_ref):
    for i in range(H):
        out_ref[strip(i), :] = jnp.concatenate([v_ref[i, 0], v_ref[i, 1]], axis=1)
    for i in range(4):
        diag_ref[strip(i), :] = jnp.concatenate([v_ref[i, 0], v_ref[i + 4, 0]], axis=1)


def triangle_kernel(s_ref, own_ref, near_ref, d1_ref, d2_ref, out_ref, low, high):
    odd, core, upper = (s_ref[0] & 1) == 1, s_ref[1], s_ref[3]
    low[...] = jnp.where(odd, near_ref[...], own_ref[...])
    high[...] = jnp.where(odd, own_ref[...], near_ref[...])

    def rows(ref, first, last):
        return ref[first * B : (last + 1) * B, :]

    @pl.when((upper == 0) & (core == 0))
    def _():
        out_ref[0:256, :] = rows(high, 3, 6)
        out_ref[256:512, :] = d1_ref[...] + d2_ref[...]
        out_ref[512:576, :] = jnp.zeros((B, 128), F32)

    @pl.when((upper == 0) & (core == 1))
    def _():
        out_ref[0:384, :] = rows(high, 1, 6)
        out_ref[384:512, :] = rows(low, 5, 6)
        out_ref[512:576, :] = jnp.zeros((B, 128), F32)

    @pl.when((upper == 1) & (core == 0))
    def _():
        out_ref[0:384, :] = rows(low, 1, 6)
        out_ref[384:512, :] = rows(high, 1, 2)
        last = jnp.concatenate([rows(high, 3, 3)[:, :B], rows(low, 7, 7)[:, :B]], axis=1)
        out_ref[512:576, :] = last

    @pl.when((upper == 1) & (core == 1))
    def _():
        out_ref[0:320, :] = rows(low, 1, 5)
        out_ref[320:384, :] = rows(high, 1, 1)
        out_ref[384:576, :] = jnp.zeros((192, 128), F32)


def square_kernel(s_ref, *refs):
    packs, (p1_ref, v_ref, vh_ref, vl_ref, pv_ref, tr_ref) = refs[:8], refs[8:14]
    q_ref, r_ref, rh, rl = refs[14:]
    yl, core, upper = s_ref[0], s_ref[1], s_ref[3]
    for k in range(4):
        for other in range(2):
            place = 2 * (yl ^ k) + (core ^ other)
            q_ref[:, pl.ds(pl.multiple_of(place * 128, 128), 128)] = packs[4 * other + k][...]
    total = jnp.zeros((1, 2 * N), F32)
    for i in range(H):
        own = q_ref[strip(i), :]
        total += jnp.sum(own * own, axis=0, keepdims=True)
        at = i * B
        if i % 2:
            own = pltpu.roll(jnp.concatenate([own, jnp.zeros((B, 128), F32)], axis=1), B, 1)
            at -= B
        parts = [own]
        if at:
            parts.insert(0, jnp.zeros((B, at), F32))
        left = W - at - own.shape[1]
        if left:
            parts.append(jnp.zeros((B, left), F32))
        full = jnp.concatenate(parts, axis=1)
        r_ref[strip(i), :] = full
        rh[strip(i), :], rl[strip(i), :] = halves(full)
    tr_ref[...] = jnp.broadcast_to(jnp.sum(total, axis=1, keepdims=True), tr_ref.shape)

    def part(rows, cols):
        return rh[rows, cols], rl[rows, cols]

    lo, hi = slice(0, 256), slice(256, 512)
    mid = slice(N, 2 * N)
    side = pl.ds(pl.multiple_of(2 * N * upper, 128), N)
    v_ref[...] = r_ref[:, side]
    vh_ref[...], vl_ref[...] = rh[:, side], rl[:, side]
    pv_ref[...] = dot3(part(slice(None), mid), (vh_ref[...], vl_ref[...]), NN)

    p01 = dot3(part(lo, slice(256, 1280)), part(hi, slice(256, 1280)), NT)
    p1_ref[lo, lo] = dot3(part(lo, slice(0, 1280)), part(lo, slice(0, 1280)), NT)
    p1_ref[lo, hi] = p01
    p1_ref[hi, lo] = p01.T
    p1_ref[hi, hi] = dot3(part(hi, slice(256, W)), part(hi, slice(256, W)), NT)
    rules = Rules(s_ref, BR[0], H, H)
    for i in range(H):
        keep, pick = rules.strip(i)
        squared = jnp.where(keep, p1_ref[strip(i), :], 0.0)
        p1_ref[strip(i), :] = jnp.where(pick, 2.0 * r_ref[strip(i), mid] - squared, squared)


def second_kernel(s_ref, p1_ref, v_ref, vh_ref, vl_ref, pv_ref, tr_ref, ta, tb,
                  own_ref, far_ref, near_ref, sums_ref, t_ref, w_ref, mh, ml):
    core, col, upper = s_ref[1], s_ref[2], s_ref[3]
    lane = lax.broadcasted_iota(jnp.int32, (B, N), 1)
    zero = jnp.zeros((B, 128), F32)
    base, other = H * (1 - upper), H * upper
    t_ref[core, :, :] = ta[...]
    t_ref[1 - core, :, :] = tb[...]

    def line(which, start):
        return t_ref[which, start * B : (start + 1) * B, :]

    @pl.when(upper == 0)
    def _():
        w_ref[strip(0), :] = jnp.zeros((B, N), F32)
        for k in range(1, H):
            parts = [line(0, k - 1), zero, zero, zero]
            if k == 7:
                parts[0] = pltpu.roll(line(0, 8), B, 1)
            if k < 6:
                parts[1] = line(1, k - 1)
            if k < 4:
                parts[2] = line(0, 5 + k)
            if k < 2:
                parts[3] = line(1, 4 + k)
            turned = pltpu.roll(jnp.concatenate(parts, axis=1), k * B, 1)
            w_ref[strip(k), :] = jnp.where(lane >= k * B, turned, 0.0)

    @pl.when(upper == 1)
    def _():
        w_ref[strip(7), :] = jnp.zeros((B, N), F32)
        for k in range(7):
            diag = line(0, 4 + k % 4)
            if k >= 4:
                diag = pltpu.roll(diag, B, 1)
            parts = [zero, zero, zero, diag]
            if k >= 5:
                parts[0] = line(1, k + 1)
            if k >= 3:
                parts[1] = line(0, k - 3)
            if k >= 1:
                parts[2] = line(1, k - 1)
            turned = pltpu.roll(jnp.concatenate(parts, axis=1), ((k + 2) % 8) * B, 1)
            w_ref[strip(k), :] = jnp.where(lane < (k + 1) * B, turned, 0.0)

    full = w_ref[...]
    above = lax.shift_right_logical(lax.broadcasted_iota(jnp.int32, (N, N), 0), 6)
    along = lax.shift_right_logical(lax.broadcasted_iota(jnp.int32, (N, N), 1), 6)
    full = jnp.where(above == along, full, full + full.T)
    w_ref[...] = pv_ref[...] + dot3((vh_ref[...], vl_ref[...]), halves(full), NN)

    def at(block, size):
        return pl.ds(pl.multiple_of(block * B, B), size)

    def row(block, size=B):
        return at(block + 1, size)

    def lanes(block):
        return pl.ds(pl.multiple_of(block * B, 128), N)

    rules = Rules(s_ref, BR[0], H, 2 * H * upper)
    inner = jnp.zeros((1, N), F32)
    for i in range(H):
        keep, pick = rules.strip(i)
        squared = jnp.where(keep, w_ref[strip(i), :], 0.0)
        new = jnp.where(pick, 2.0 * v_ref[strip(i), :] - squared, squared)
        w_ref[strip(i), :] = new
        here = row(base + i)
        mh[here, lanes(other)], ml[here, lanes(other)] = halves(new)
        new = p1_ref[strip(i), :]
        inner += jnp.sum(new * new, axis=0, keepdims=True)
        mh[here, lanes(base)], ml[here, lanes(base)] = halves(new)
    turned = w_ref[...].T
    there = row(other, N)
    mh[there, lanes(base)], ml[there, lanes(base)] = halves(turned)
    blank = jnp.zeros((N, N), BF16)
    mh[there, lanes(other)] = blank
    ml[there, lanes(other)] = blank

    @pl.when(upper == 1)
    def _():
        w_ref[...] = turned

    outer = jnp.zeros((1, N), F32)
    for i in range(H):
        outer += jnp.sum(w_ref[strip(i), :] * w_ref[strip(i), :], axis=0, keepdims=True)

    spot = lax.broadcasted_iota(jnp.int32, (1, 128), 1)
    both = jnp.where(spot == 0, tr_ref[...], 0.0)
    both = jnp.where(spot == 1, jnp.sum(inner, axis=1, keepdims=True), both)
    both = jnp.where(spot == 2, jnp.sum(outer, axis=1, keepdims=True), both)
    sums_ref[...] = jnp.broadcast_to(both, sums_ref.shape)

    wide = (lax.broadcasted_iota(jnp.int32, (B, 128), 1) >= B).astype(jnp.int32)
    shift = 6 - 2 * col

    def share(i, rows, panel):
        block = rows + i + shift
        pair = row(jnp.clip(block, -1, 2 * H - 1), 128)
        span = lanes(panel)
        product = dot3(
            (mh[row(rows + i), span], ml[row(rows + i), span]),
            (mh[pair, span], ml[pair, span]), NT,
        )
        index = block + wide - base
        return jnp.where((index >= 0) & (index < H), product, 0.0)

    for i in range(H):
        far_ref[strip(i), :] = share(i, other, base)
        near_ref[strip(i), :] = share(i, base, other)
        here = row(base + i)
        block = base + i + 2 * col - H
        pair = row(block, 128)
        own_ref[0, strip(i), :] = dot3((mh[here, :], ml[here, :]), (mh[pair, :], ml[pair, :]), NT)
        if i % 2:
            span = pl.ds(pl.multiple_of((block - 1) * B, 128), 256)
            held = mh[here, span].astype(F32) + ml[here, span].astype(F32)
            held = held[:, B : B + 128]
        else:
            span = pl.ds(pl.multiple_of(block * B, 128), 128)
            held = mh[here, span].astype(F32) + ml[here, span].astype(F32)
        own_ref[1, strip(i), :] = held


def last_kernel(s_ref, own_ref, far_ref, near_ref, sums_ref, out_ref, traces_ref):
    col, upper = s_ref[2], s_ref[3]
    wide = lax.broadcasted_iota(jnp.int32, (B, 128), 1) >= B
    for i in range(H):
        squared = own_ref[0, strip(i), :] + (far_ref[strip(i), :] + near_ref[strip(i), :])
        keep, pick = [], []
        for h in range(2):
            far = jnp.abs(2 * col + h - H)
            reach = jnp.minimum(s_ref[RAD + H + i], s_ref[RAD + i + 2 * col + h])
            keep.append((far <= reach).astype(F32))
            pick.append((s_ref[BR[1] + H + i] * s_ref[BR[1] + i + 2 * col + h]).astype(F32))
        squared = squared * jnp.where(wide, keep[1], keep[0])
        chosen = jnp.where(wide, pick[1], pick[0]) == 1.0
        new = jnp.where(chosen, 2.0 * own_ref[1, strip(i), :] - squared, squared)
        out_ref[i, 0] = new[:, :B]
        out_ref[i, 1] = new[:, B:]
    sums = sums_ref[...]
    count = sums.shape[0]
    spot = lax.broadcasted_iota(jnp.int32, sums.shape, 1)
    line = lax.broadcasted_iota(jnp.int32, sums.shape, 0)
    turned = jnp.concatenate([sums[count - 1 :], sums[: count - 1]], axis=0)
    sums = jnp.where((spot == 2) & (upper + 0 * line == 1), turned, sums)
    total = jnp.sum(sums, axis=0, keepdims=True)
    spot = lax.broadcasted_iota(jnp.int32, total.shape, 1)
    weight = jnp.where(spot == 1, 1.0, jnp.where(spot == 2, 2.0, 0.0))
    traces_ref[0] = jnp.sum(jnp.where(spot == 0, total, 0.0))
    traces_ref[1] = jnp.sum(total * weight)


def shape(*dims):
    return jax.ShapeDtypeStruct(dims, F32)


def per_device(rows, values, radius, branch):
    both = ("row", "col")
    row, col = lax.axis_index("row"), lax.axis_index("col")
    pad = ((H, H),)
    radii = lax.dynamic_slice(jnp.pad(radius, pad, constant_values=-1), (H * row,), (3 * H,))
    flags = lax.dynamic_slice(jnp.pad(branch, ((0, 0),) + pad), (0, H * row), (2, 3 * H))
    scalars = jnp.concatenate(
        [jnp.stack([col // 2, col % 2, col, col // 4]).astype(jnp.int32), radii, flags[0], flags[1]]
    )

    def swap(x):
        return lax.ppermute(x, "col", [(c, c ^ 1) for c in range(8)])

    def to_rows(x, pairs):
        return lax.ppermute(x, both, pairs)

    def index(r, c):
        return r * 8 + c

    ends = [(r, c) for r in range(rows - 1) for c in range(4)]

    packed, diag = call(
        pack_kernel, out_shape=[shape(N, 128), shape(256, 128)], in_specs=[VMEM],
        out_specs=[VMEM] * 2, mib=8, name="pack",
    )(values)
    near = lax.ppermute(packed, "col", [(c, c ^ 2) for c in range(8)])
    d1 = lax.ppermute(diag, "col", [(4, 2)])
    d2 = lax.ppermute(diag, "col", [(4, 0)])
    later, d1 = lax.optimization_barrier((packed, d1))
    cross = lax.ppermute(later, "col", [(c, c ^ 4) for c in range(8)])
    triangle = call(
        triangle_kernel,
        out_shape=shape(576, 128),
        in_specs=[SMEM] + [VMEM] * 4,
        out_specs=VMEM,
        scratch_shapes=[pltpu.VMEM((N, 128), F32)] * 2,
        mib=8, name="triangle",
    )(scalars, packed, near, d1, d2)
    pairs = [(index(r, c + 4), index(r + 1, c)) for r, c in ends]
    ta = lax.ppermute(triangle, both, pairs + [(b, a) for a, b in pairs])
    packed, near, cross, triangle = lax.optimization_barrier((packed, near, cross, triangle))
    forward = lax.ppermute(cross, "col", [(c, c ^ 2) for c in range(8)])
    swapped = [swap(packed), swap(near), swap(cross)]
    forward, ta, *swapped = lax.optimization_barrier((forward, ta, *swapped))
    mine = [packed, near, cross, forward]
    others = swapped + [swap(forward)]

    *old, trace = call(
        square_kernel,
        out_shape=[
            shape(N, N), shape(N, N), jax.ShapeDtypeStruct((N, N), BF16),
            jax.ShapeDtypeStruct((N, N), BF16), shape(N, N), shape(1, 128),
        ],
        in_specs=[SMEM] + [VMEM] * 8,
        out_specs=[VMEM] * 6,
        scratch_shapes=[
            pltpu.VMEM((N, 2 * N), F32),
            pltpu.VMEM((N, W), F32),
            pltpu.VMEM((N, W), BF16),
            pltpu.VMEM((N, W), BF16),
        ],
        mib=24, name="square",
    )(scalars, *mine, *others)

    tb = swap(ta)
    own, far, near, sums = call(
        second_kernel,
        out_shape=[shape(2, N, 128), shape(N, 128), shape(N, 128), shape(rows, 128)],
        in_specs=[SMEM] + [VMEM] * 8,
        out_specs=[VMEM] * 4,
        scratch_shapes=[
            pltpu.VMEM((2, 576, 128), F32),
            pltpu.VMEM((N, N), F32),
            pltpu.VMEM((18 * B, 2 * N), BF16),
            pltpu.VMEM((18 * B, 2 * N), BF16),
        ],
        mib=24, name="second",
    )(scalars, *old, trace, ta, tb)

    pairs = [(index(r, 7 - c), index(r + 1, c)) for r, c in ends]
    far = lax.ppermute(far, both, pairs + [(b, a) for a, b in pairs])
    near = lax.ppermute(near, "col", [(c, 7 - c) for c in range(8)])
    sums = lax.all_to_all(sums, "row", 0, 0, tiled=True)
    return call(
        last_kernel,
        out_shape=[shape(H, 2, B, B), shape(2)],
        in_specs=[SMEM] + [VMEM] * 4,
        out_specs=[VMEM, SMEM],
        mib=8, name="last",
    )(scalars, own, far, near, sums)


def solution(mesh):
    rows = mesh.shape["row"]

    def run(values, radius, branch):
        return per_device(rows, values, radius, branch)

    in_specs = (P("row", "col", None, None), P(), P())
    out_specs = (P("row", "col", None, None), P())
    return jax.shard_map(
        run, mesh=mesh, in_specs=in_specs, out_specs=out_specs, check_vma=False
    )
```

```python
import jax
import jax.numpy as jnp
from jax import lax
from jax.experimental import pallas as pl
from jax.experimental.pallas import tpu as pltpu
from jax.sharding import PartitionSpec as P

F32 = jnp.float32
BF16 = jnp.bfloat16
B = 64
H = 8
N = H * B
W = 3 * N
VMEM = pl.BlockSpec(memory_space=pltpu.VMEM)
SMEM = pl.BlockSpec(memory_space=pltpu.SMEM)
RAD, BR = 4, (28, 52)


def call(kernel, mib, name, **rest):
    return pl.pallas_call(
        kernel,
        name=name,
        compiler_params=pltpu.CompilerParams(vmem_limit_bytes=mib << 20),
        **rest,
    )


def halves(x):
    hi = x.astype(BF16)
    return hi, (x - hi.astype(F32)).astype(BF16)


def dot3(a, b, dims):
    (ah, al), (bh, bl) = a, b

    def one(x, y):
        return lax.dot_general(x, y, (dims, ((), ())), preferred_element_type=F32)

    return one(ah, bh) + (one(ah, bl) + one(al, bh))


NN = ((1,), (0,))
NT = ((1,), (1,))


def strip(i):
    return slice(i * B, (i + 1) * B)


class Rules:
    def __init__(self, s_ref, start, rows, cols):
        self.s_ref, self.start, self.rows, self.cols = s_ref, start, rows, cols
        block = lax.shift_right_logical(lax.broadcasted_iota(jnp.int32, (1, N), 1), 6)
        radii = flags = jnp.zeros((1, N), jnp.int32)
        for k in range(H):
            radii = jnp.where(block == k, s_ref[RAD + cols + k], radii)
            flags = jnp.where(block == k, s_ref[start + cols + k], flags)
        self.block, self.radii, self.flags = block + cols, radii, flags

    def strip(self, i):
        reach = jnp.minimum(self.radii, self.s_ref[RAD + self.rows + i])
        keep = jnp.abs(self.block - (self.rows + i)) <= reach
        return keep, self.flags * self.s_ref[self.start + self.rows + i] == 1


def pack_kernel(v_ref, out_ref, diag_ref):
    for i in range(H):
        out_ref[strip(i), :] = jnp.concatenate([v_ref[i, 0], v_ref[i, 1]], axis=1)
    for i in range(4):
        diag_ref[strip(i), :] = jnp.concatenate([v_ref[i, 0], v_ref[i + 4, 0]], axis=1)


def triangle_kernel(s_ref, own_ref, near_ref, d1_ref, d2_ref, out_ref, both_ref, low, high):
    odd, core, upper = (s_ref[0] & 1) == 1, s_ref[1], s_ref[3]
    both_ref[0:N, :] = own_ref[...]
    both_ref[N : 2 * N, :] = near_ref[...]
    low[...] = jnp.where(odd, near_ref[...], own_ref[...])
    high[...] = jnp.where(odd, own_ref[...], near_ref[...])

    def rows(ref, first, last):
        return ref[first * B : (last + 1) * B, :]

    @pl.when((upper == 0) & (core == 0))
    def _():
        out_ref[0:256, :] = rows(high, 3, 6)
        out_ref[256:512, :] = d1_ref[...] + d2_ref[...]
        out_ref[512:576, :] = jnp.zeros((B, 128), F32)

    @pl.when((upper == 0) & (core == 1))
    def _():
        out_ref[0:384, :] = rows(high, 1, 6)
        out_ref[384:512, :] = rows(low, 5, 6)
        out_ref[512:576, :] = jnp.zeros((B, 128), F32)

    @pl.when((upper == 1) & (core == 0))
    def _():
        out_ref[0:384, :] = rows(low, 1, 6)
        out_ref[384:512, :] = rows(high, 1, 2)
        last = jnp.concatenate([rows(high, 3, 3)[:, :B], rows(low, 7, 7)[:, :B]], axis=1)
        out_ref[512:576, :] = last

    @pl.when((upper == 1) & (core == 1))
    def _():
        out_ref[0:320, :] = rows(low, 1, 5)
        out_ref[320:384, :] = rows(high, 1, 1)
        out_ref[384:576, :] = jnp.zeros((192, 128), F32)


def square_kernel(s_ref, *refs):
    packs, (p1_ref, v_ref, vh_ref, vl_ref, pv_ref, tr_ref) = refs[:6], refs[6:12]
    q_ref, r_ref, rh, rl = refs[12:]
    yl, core, upper = s_ref[0], s_ref[1], s_ref[3]
    for k in range(4):
        for other in range(2):
            place = 2 * (yl ^ k) + (core ^ other)
            part = packs[2 * k - 2 + other][...] if k > 1 else packs[other][k * N : (k + 1) * N, :]
            q_ref[:, pl.ds(pl.multiple_of(place * 128, 128), 128)] = part
    total = jnp.zeros((1, 2 * N), F32)
    for i in range(H):
        own = q_ref[strip(i), :]
        total += jnp.sum(own * own, axis=0, keepdims=True)
        at = i * B
        if i % 2:
            own = pltpu.roll(jnp.concatenate([own, jnp.zeros((B, 128), F32)], axis=1), B, 1)
            at -= B
        parts = [own]
        if at:
            parts.insert(0, jnp.zeros((B, at), F32))
        left = W - at - own.shape[1]
        if left:
            parts.append(jnp.zeros((B, left), F32))
        full = jnp.concatenate(parts, axis=1)
        r_ref[strip(i), :] = full
        rh[strip(i), :], rl[strip(i), :] = halves(full)
    tr_ref[...] = jnp.broadcast_to(jnp.sum(total, axis=1, keepdims=True), tr_ref.shape)

    def part(rows, cols):
        return rh[rows, cols], rl[rows, cols]

    lo, hi = slice(0, 256), slice(256, 512)
    mid = slice(N, 2 * N)
    side = pl.ds(pl.multiple_of(2 * N * upper, 128), N)
    v_ref[...] = r_ref[:, side]
    vh_ref[...], vl_ref[...] = rh[:, side], rl[:, side]
    pv_ref[...] = dot3(part(slice(None), mid), (vh_ref[...], vl_ref[...]), NN)

    p01 = dot3(part(lo, slice(256, 1280)), part(hi, slice(256, 1280)), NT)
    p1_ref[lo, lo] = dot3(part(lo, slice(0, 1280)), part(lo, slice(0, 1280)), NT)
    p1_ref[lo, hi] = p01
    p1_ref[hi, lo] = p01.T
    p1_ref[hi, hi] = dot3(part(hi, slice(256, W)), part(hi, slice(256, W)), NT)
    rules = Rules(s_ref, BR[0], H, H)
    for i in range(H):
        keep, pick = rules.strip(i)
        squared = jnp.where(keep, p1_ref[strip(i), :], 0.0)
        p1_ref[strip(i), :] = jnp.where(pick, 2.0 * r_ref[strip(i), mid] - squared, squared)


def second_kernel(s_ref, p1_ref, v_ref, vh_ref, vl_ref, pv_ref, tr_ref, ta, tb,
                  own_ref, far_ref, near_ref, sums_ref, t_ref, w_ref, mh, ml):
    core, col, upper = s_ref[1], s_ref[2], s_ref[3]
    lane = lax.broadcasted_iota(jnp.int32, (B, N), 1)
    zero = jnp.zeros((B, 128), F32)
    base, other = H * (1 - upper), H * upper
    t_ref[core, :, :] = ta[...]
    t_ref[1 - core, :, :] = tb[...]

    def line(which, start):
        return t_ref[which, start * B : (start + 1) * B, :]

    @pl.when(upper == 0)
    def _():
        w_ref[strip(0), :] = jnp.zeros((B, N), F32)
        for k in range(1, H):
            parts = [line(0, k - 1), zero, zero, zero]
            if k == 7:
                parts[0] = pltpu.roll(line(0, 8), B, 1)
            if k < 6:
                parts[1] = line(1, k - 1)
            if k < 4:
                parts[2] = line(0, 5 + k)
            if k < 2:
                parts[3] = line(1, 4 + k)
            turned = pltpu.roll(jnp.concatenate(parts, axis=1), k * B, 1)
            w_ref[strip(k), :] = jnp.where(lane >= k * B, turned, 0.0)

    @pl.when(upper == 1)
    def _():
        w_ref[strip(7), :] = jnp.zeros((B, N), F32)
        for k in range(7):
            diag = line(0, 4 + k % 4)
            if k >= 4:
                diag = pltpu.roll(diag, B, 1)
            parts = [zero, zero, zero, diag]
            if k >= 5:
                parts[0] = line(1, k + 1)
            if k >= 3:
                parts[1] = line(0, k - 3)
            if k >= 1:
                parts[2] = line(1, k - 1)
            turned = pltpu.roll(jnp.concatenate(parts, axis=1), ((k + 2) % 8) * B, 1)
            w_ref[strip(k), :] = jnp.where(lane < (k + 1) * B, turned, 0.0)

    full = w_ref[...]
    above = lax.shift_right_logical(lax.broadcasted_iota(jnp.int32, (N, N), 0), 6)
    along = lax.shift_right_logical(lax.broadcasted_iota(jnp.int32, (N, N), 1), 6)
    full = jnp.where(above == along, full, full + full.T)
    w_ref[...] = pv_ref[...] + dot3((vh_ref[...], vl_ref[...]), halves(full), NN)

    def at(block, size):
        return pl.ds(pl.multiple_of(block * B, B), size)

    def row(block, size=B):
        return at(block + 1, size)

    def lanes(block):
        return pl.ds(pl.multiple_of(block * B, 128), N)

    rules = Rules(s_ref, BR[0], H, 2 * H * upper)
    inner = jnp.zeros((1, N), F32)
    for i in range(H):
        keep, pick = rules.strip(i)
        squared = jnp.where(keep, w_ref[strip(i), :], 0.0)
        new = jnp.where(pick, 2.0 * v_ref[strip(i), :] - squared, squared)
        w_ref[strip(i), :] = new
        here = row(base + i)
        mh[here, lanes(other)], ml[here, lanes(other)] = halves(new)
        new = p1_ref[strip(i), :]
        inner += jnp.sum(new * new, axis=0, keepdims=True)
        mh[here, lanes(base)], ml[here, lanes(base)] = halves(new)
    turned = w_ref[...].T
    there = row(other, N)
    mh[there, lanes(base)], ml[there, lanes(base)] = halves(turned)
    blank = jnp.zeros((N, N), BF16)
    mh[there, lanes(other)] = blank
    ml[there, lanes(other)] = blank

    @pl.when(upper == 1)
    def _():
        w_ref[...] = turned

    outer = jnp.zeros((1, N), F32)
    for i in range(H):
        outer += jnp.sum(w_ref[strip(i), :] * w_ref[strip(i), :], axis=0, keepdims=True)

    spot = lax.broadcasted_iota(jnp.int32, (1, 128), 1)
    both = jnp.where(spot == 0, tr_ref[...], 0.0)
    both = jnp.where(spot == 1, jnp.sum(inner, axis=1, keepdims=True), both)
    both = jnp.where(spot == 2, jnp.sum(outer, axis=1, keepdims=True), both)
    sums_ref[...] = jnp.broadcast_to(both, sums_ref.shape)

    wide = (lax.broadcasted_iota(jnp.int32, (B, 128), 1) >= B).astype(jnp.int32)
    shift = 6 - 2 * col

    def share(i, rows, panel):
        block = rows + i + shift
        pair = row(jnp.clip(block, -1, 2 * H - 1), 128)
        span = lanes(panel)
        product = dot3(
            (mh[row(rows + i), span], ml[row(rows + i), span]),
            (mh[pair, span], ml[pair, span]), NT,
        )
        index = block + wide - base
        return jnp.where((index >= 0) & (index < H), product, 0.0)

    for i in range(H):
        far_ref[strip(i), :] = share(i, other, base)
        near_ref[strip(i), :] = share(i, base, other)
        here = row(base + i)
        block = base + i + 2 * col - H
        pair = row(block, 128)
        own_ref[0, strip(i), :] = dot3((mh[here, :], ml[here, :]), (mh[pair, :], ml[pair, :]), NT)
        if i % 2:
            span = pl.ds(pl.multiple_of((block - 1) * B, 128), 256)
            held = mh[here, span].astype(F32) + ml[here, span].astype(F32)
            held = held[:, B : B + 128]
        else:
            span = pl.ds(pl.multiple_of(block * B, 128), 128)
            held = mh[here, span].astype(F32) + ml[here, span].astype(F32)
        own_ref[1, strip(i), :] = held


def last_kernel(s_ref, own_ref, far_ref, near_ref, sums_ref, out_ref, traces_ref):
    col, upper = s_ref[2], s_ref[3]
    wide = lax.broadcasted_iota(jnp.int32, (B, 128), 1) >= B
    for i in range(H):
        squared = own_ref[0, strip(i), :] + (far_ref[strip(i), :] + near_ref[strip(i), :])
        keep, pick = [], []
        for h in range(2):
            far = jnp.abs(2 * col + h - H)
            reach = jnp.minimum(s_ref[RAD + H + i], s_ref[RAD + i + 2 * col + h])
            keep.append((far <= reach).astype(F32))
            pick.append((s_ref[BR[1] + H + i] * s_ref[BR[1] + i + 2 * col + h]).astype(F32))
        squared = squared * jnp.where(wide, keep[1], keep[0])
        chosen = jnp.where(wide, pick[1], pick[0]) == 1.0
        new = jnp.where(chosen, 2.0 * own_ref[1, strip(i), :] - squared, squared)
        out_ref[i, 0] = new[:, :B]
        out_ref[i, 1] = new[:, B:]
    sums = sums_ref[...]
    count = sums.shape[0]
    spot = lax.broadcasted_iota(jnp.int32, sums.shape, 1)
    line = lax.broadcasted_iota(jnp.int32, sums.shape, 0)
    turned = jnp.concatenate([sums[count - 1 :], sums[: count - 1]], axis=0)
    sums = jnp.where((spot == 2) & (upper + 0 * line == 1), turned, sums)
    total = jnp.sum(sums, axis=0, keepdims=True)
    spot = lax.broadcasted_iota(jnp.int32, total.shape, 1)
    weight = jnp.where(spot == 1, 1.0, jnp.where(spot == 2, 2.0, 0.0))
    traces_ref[0] = jnp.sum(jnp.where(spot == 0, total, 0.0))
    traces_ref[1] = jnp.sum(total * weight)


def shape(*dims):
    return jax.ShapeDtypeStruct(dims, F32)


def per_device(rows, values, radius, branch):
    both = ("row", "col")
    row, col = lax.axis_index("row"), lax.axis_index("col")
    pad = ((H, H),)
    radii = lax.dynamic_slice(jnp.pad(radius, pad, constant_values=-1), (H * row,), (3 * H,))
    flags = lax.dynamic_slice(jnp.pad(branch, ((0, 0),) + pad), (0, H * row), (2, 3 * H))
    scalars = jnp.concatenate(
        [jnp.stack([col // 2, col % 2, col, col // 4]).astype(jnp.int32), radii, flags[0], flags[1]]
    )

    def swap(x):
        return lax.ppermute(x, "col", [(c, c ^ 1) for c in range(8)])

    def to_rows(x, pairs):
        return lax.ppermute(x, both, pairs)

    def index(r, c):
        return r * 8 + c

    ends = [(r, c) for r in range(rows - 1) for c in range(4)]

    packed, diag = call(
        pack_kernel, out_shape=[shape(N, 128), shape(256, 128)], in_specs=[VMEM],
        out_specs=[VMEM] * 2, mib=8, name="pack",
    )(values)
    near = lax.ppermute(packed, "col", [(c, c ^ 2) for c in range(8)])
    d1 = lax.ppermute(diag, "col", [(4, 2)])
    d2 = lax.ppermute(diag, "col", [(4, 0)])
    later, d1 = lax.optimization_barrier((packed, d1))
    cross = lax.ppermute(later, "col", [(c, c ^ 4) for c in range(8)])
    triangle, joined = call(
        triangle_kernel,
        out_shape=[shape(576, 128), shape(2 * N, 128)],
        in_specs=[SMEM] + [VMEM] * 4,
        out_specs=[VMEM] * 2,
        scratch_shapes=[pltpu.VMEM((N, 128), F32)] * 2,
        mib=8, name="triangle",
    )(scalars, packed, near, d1, d2)
    pairs = [(index(r, c + 4), index(r + 1, c)) for r, c in ends]
    ta = lax.ppermute(triangle, both, pairs + [(b, a) for a, b in pairs])
    cross, joined, triangle = lax.optimization_barrier((cross, joined, triangle))
    forward = lax.ppermute(cross, "col", [(c, c ^ 2) for c in range(8)])
    joined2, cross2 = swap(joined), swap(cross)
    forward, cross2 = lax.optimization_barrier((forward, cross2))
    forward2 = swap(forward)
    ta, forward = lax.optimization_barrier((ta, forward))
    tb = swap(ta)

    *old, trace = call(
        square_kernel,
        out_shape=[
            shape(N, N), shape(N, N), jax.ShapeDtypeStruct((N, N), BF16),
            jax.ShapeDtypeStruct((N, N), BF16), shape(N, N), shape(1, 128),
        ],
        in_specs=[SMEM] + [VMEM] * 6,
        out_specs=[VMEM] * 6,
        scratch_shapes=[
            pltpu.VMEM((N, 2 * N), F32),
            pltpu.VMEM((N, W), F32),
            pltpu.VMEM((N, W), BF16),
            pltpu.VMEM((N, W), BF16),
        ],
        mib=24, name="square",
    )(scalars, joined, joined2, cross, cross2, forward, forward2)

    own, far, near, sums = call(
        second_kernel,
        out_shape=[shape(2, N, 128), shape(N, 128), shape(N, 128), shape(rows, 128)],
        in_specs=[SMEM] + [VMEM] * 8,
        out_specs=[VMEM] * 4,
        scratch_shapes=[
            pltpu.VMEM((2, 576, 128), F32),
            pltpu.VMEM((N, N), F32),
            pltpu.VMEM((18 * B, 2 * N), BF16),
            pltpu.VMEM((18 * B, 2 * N), BF16),
        ],
        mib=24, name="second",
    )(scalars, *old, trace, ta, tb)

    pairs = [(index(r, 7 - c), index(r + 1, c)) for r, c in ends]
    far = lax.ppermute(far, both, pairs + [(b, a) for a, b in pairs])
    near = lax.ppermute(near, "col", [(c, 7 - c) for c in range(8)])
    sums = lax.all_to_all(sums, "row", 0, 0, tiled=True)
    return call(
        last_kernel,
        out_shape=[shape(H, 2, B, B), shape(2)],
        in_specs=[SMEM] + [VMEM] * 4,
        out_specs=[VMEM, SMEM],
        mib=8, name="last",
    )(scalars, own, far, near, sums)


def solution(mesh):
    rows = mesh.shape["row"]

    def run(values, radius, branch):
        return per_device(rows, values, radius, branch)

    in_specs = (P("row", "col", None, None), P(), P())
    out_specs = (P("row", "col", None, None), P())
    return jax.shard_map(
        run, mesh=mesh, in_specs=in_specs, out_specs=out_specs, check_vma=False
    )
```

```python
import jax
import jax.numpy as jnp
from jax import lax
from jax.experimental import pallas as pl
from jax.experimental.pallas import tpu as pltpu
from jax.sharding import PartitionSpec as P

F32 = jnp.float32
BF16 = jnp.bfloat16
B = 64
H = 8
N = H * B
W = 3 * N
VMEM = pl.BlockSpec(memory_space=pltpu.VMEM)
SMEM = pl.BlockSpec(memory_space=pltpu.SMEM)
RAD, BR = 4, (28, 52)


def call(kernel, mib, name, **rest):
    return pl.pallas_call(
        kernel,
        name=name,
        compiler_params=pltpu.CompilerParams(vmem_limit_bytes=mib << 20),
        **rest,
    )


def halves(x):
    hi = x.astype(BF16)
    return hi, (x - hi.astype(F32)).astype(BF16)


def dot3(a, b, dims):
    (ah, al), (bh, bl) = a, b

    def one(x, y):
        return lax.dot_general(x, y, (dims, ((), ())), preferred_element_type=F32)

    return one(ah, bh) + (one(ah, bl) + one(al, bh))


NN = ((1,), (0,))
NT = ((1,), (1,))


def strip(i):
    return slice(i * B, (i + 1) * B)


class Rules:
    def __init__(self, s_ref, start, rows, cols):
        self.s_ref, self.start, self.rows, self.cols = s_ref, start, rows, cols
        block = lax.shift_right_logical(lax.broadcasted_iota(jnp.int32, (1, N), 1), 6)
        radii = flags = jnp.zeros((1, N), jnp.int32)
        for k in range(H):
            radii = jnp.where(block == k, s_ref[RAD + cols + k], radii)
            flags = jnp.where(block == k, s_ref[start + cols + k], flags)
        self.block, self.radii, self.flags = block + cols, radii, flags

    def strip(self, i):
        reach = jnp.minimum(self.radii, self.s_ref[RAD + self.rows + i])
        keep = jnp.abs(self.block - (self.rows + i)) <= reach
        return keep, self.flags * self.s_ref[self.start + self.rows + i] == 1


def pack_kernel(v_ref, out_ref, diag_ref):
    for i in range(H):
        out_ref[strip(i), :] = jnp.concatenate([v_ref[i, 0], v_ref[i, 1]], axis=1)
    for i in range(4):
        diag_ref[strip(i), :] = jnp.concatenate([v_ref[i, 0], v_ref[i + 4, 0]], axis=1)


def join_kernel(first_ref, second_ref, out_ref):
    out_ref[0:N, :] = first_ref[...]
    out_ref[N : 2 * N, :] = second_ref[...]


def triangle_kernel(s_ref, own_ref, near_ref, d1_ref, d2_ref, out_ref, both_ref, low, high):
    odd, core, upper = (s_ref[0] & 1) == 1, s_ref[1], s_ref[3]
    both_ref[0:N, :] = own_ref[...]
    both_ref[N : 2 * N, :] = near_ref[...]
    low[...] = jnp.where(odd, near_ref[...], own_ref[...])
    high[...] = jnp.where(odd, own_ref[...], near_ref[...])

    def rows(ref, first, last):
        return ref[first * B : (last + 1) * B, :]

    @pl.when((upper == 0) & (core == 0))
    def _():
        out_ref[0:256, :] = rows(high, 3, 6)
        out_ref[256:512, :] = d1_ref[...] + d2_ref[...]
        out_ref[512:576, :] = jnp.zeros((B, 128), F32)

    @pl.when((upper == 0) & (core == 1))
    def _():
        out_ref[0:384, :] = rows(high, 1, 6)
        out_ref[384:512, :] = rows(low, 5, 6)
        out_ref[512:576, :] = jnp.zeros((B, 128), F32)

    @pl.when((upper == 1) & (core == 0))
    def _():
        out_ref[0:384, :] = rows(low, 1, 6)
        out_ref[384:512, :] = rows(high, 1, 2)
        last = jnp.concatenate([rows(high, 3, 3)[:, :B], rows(low, 7, 7)[:, :B]], axis=1)
        out_ref[512:576, :] = last

    @pl.when((upper == 1) & (core == 1))
    def _():
        out_ref[0:320, :] = rows(low, 1, 5)
        out_ref[320:384, :] = rows(high, 1, 1)
        out_ref[384:576, :] = jnp.zeros((192, 128), F32)


def square_kernel(s_ref, *refs):
    packs, (p1_ref, v_ref, vh_ref, vl_ref, pv_ref, tr_ref) = refs[:4], refs[4:10]
    q_ref, r_ref, rh, rl = refs[10:]
    yl, core, upper = s_ref[0], s_ref[1], s_ref[3]
    for k in range(4):
        for other in range(2):
            place = 2 * (yl ^ k) + (core ^ other)
            part = packs[k // 2 * 2 + other][k % 2 * N : (k % 2 + 1) * N, :]
            q_ref[:, pl.ds(pl.multiple_of(place * 128, 128), 128)] = part
    total = jnp.zeros((1, 2 * N), F32)
    for i in range(H):
        own = q_ref[strip(i), :]
        total += jnp.sum(own * own, axis=0, keepdims=True)
        at = i * B
        if i % 2:
            own = pltpu.roll(jnp.concatenate([own, jnp.zeros((B, 128), F32)], axis=1), B, 1)
            at -= B
        parts = [own]
        if at:
            parts.insert(0, jnp.zeros((B, at), F32))
        left = W - at - own.shape[1]
        if left:
            parts.append(jnp.zeros((B, left), F32))
        full = jnp.concatenate(parts, axis=1)
        r_ref[strip(i), :] = full
        rh[strip(i), :], rl[strip(i), :] = halves(full)
    tr_ref[...] = jnp.broadcast_to(jnp.sum(total, axis=1, keepdims=True), tr_ref.shape)

    def part(rows, cols):
        return rh[rows, cols], rl[rows, cols]

    lo, hi = slice(0, 256), slice(256, 512)
    mid = slice(N, 2 * N)
    side = pl.ds(pl.multiple_of(2 * N * upper, 128), N)
    v_ref[...] = r_ref[:, side]
    vh_ref[...], vl_ref[...] = rh[:, side], rl[:, side]
    pv_ref[...] = dot3(part(slice(None), mid), (vh_ref[...], vl_ref[...]), NN)

    p01 = dot3(part(lo, slice(256, 1280)), part(hi, slice(256, 1280)), NT)
    p1_ref[lo, lo] = dot3(part(lo, slice(0, 1280)), part(lo, slice(0, 1280)), NT)
    p1_ref[lo, hi] = p01
    p1_ref[hi, lo] = p01.T
    p1_ref[hi, hi] = dot3(part(hi, slice(256, W)), part(hi, slice(256, W)), NT)
    rules = Rules(s_ref, BR[0], H, H)
    for i in range(H):
        keep, pick = rules.strip(i)
        squared = jnp.where(keep, p1_ref[strip(i), :], 0.0)
        p1_ref[strip(i), :] = jnp.where(pick, 2.0 * r_ref[strip(i), mid] - squared, squared)


def second_kernel(s_ref, p1_ref, v_ref, vh_ref, vl_ref, pv_ref, tr_ref, ta, tb,
                  own_ref, far_ref, near_ref, sums_ref, t_ref, w_ref, mh, ml):
    core, col, upper = s_ref[1], s_ref[2], s_ref[3]
    lane = lax.broadcasted_iota(jnp.int32, (B, N), 1)
    zero = jnp.zeros((B, 128), F32)
    base, other = H * (1 - upper), H * upper
    t_ref[core, :, :] = ta[...]
    t_ref[1 - core, :, :] = tb[...]

    def line(which, start):
        return t_ref[which, start * B : (start + 1) * B, :]

    @pl.when(upper == 0)
    def _():
        w_ref[strip(0), :] = jnp.zeros((B, N), F32)
        for k in range(1, H):
            parts = [line(0, k - 1), zero, zero, zero]
            if k == 7:
                parts[0] = pltpu.roll(line(0, 8), B, 1)
            if k < 6:
                parts[1] = line(1, k - 1)
            if k < 4:
                parts[2] = line(0, 5 + k)
            if k < 2:
                parts[3] = line(1, 4 + k)
            turned = pltpu.roll(jnp.concatenate(parts, axis=1), k * B, 1)
            w_ref[strip(k), :] = jnp.where(lane >= k * B, turned, 0.0)

    @pl.when(upper == 1)
    def _():
        w_ref[strip(7), :] = jnp.zeros((B, N), F32)
        for k in range(7):
            diag = line(0, 4 + k % 4)
            if k >= 4:
                diag = pltpu.roll(diag, B, 1)
            parts = [zero, zero, zero, diag]
            if k >= 5:
                parts[0] = line(1, k + 1)
            if k >= 3:
                parts[1] = line(0, k - 3)
            if k >= 1:
                parts[2] = line(1, k - 1)
            turned = pltpu.roll(jnp.concatenate(parts, axis=1), ((k + 2) % 8) * B, 1)
            w_ref[strip(k), :] = jnp.where(lane < (k + 1) * B, turned, 0.0)

    full = w_ref[...]
    above = lax.shift_right_logical(lax.broadcasted_iota(jnp.int32, (N, N), 0), 6)
    along = lax.shift_right_logical(lax.broadcasted_iota(jnp.int32, (N, N), 1), 6)
    full = jnp.where(above == along, full, full + full.T)
    w_ref[...] = pv_ref[...] + dot3((vh_ref[...], vl_ref[...]), halves(full), NN)

    def at(block, size):
        return pl.ds(pl.multiple_of(block * B, B), size)

    def row(block, size=B):
        return at(block + 1, size)

    def lanes(block):
        return pl.ds(pl.multiple_of(block * B, 128), N)

    rules = Rules(s_ref, BR[0], H, 2 * H * upper)
    inner = jnp.zeros((1, N), F32)
    for i in range(H):
        keep, pick = rules.strip(i)
        squared = jnp.where(keep, w_ref[strip(i), :], 0.0)
        new = jnp.where(pick, 2.0 * v_ref[strip(i), :] - squared, squared)
        w_ref[strip(i), :] = new
        here = row(base + i)
        mh[here, lanes(other)], ml[here, lanes(other)] = halves(new)
        new = p1_ref[strip(i), :]
        inner += jnp.sum(new * new, axis=0, keepdims=True)
        mh[here, lanes(base)], ml[here, lanes(base)] = halves(new)
    turned = w_ref[...].T
    there = row(other, N)
    mh[there, lanes(base)], ml[there, lanes(base)] = halves(turned)
    blank = jnp.zeros((N, N), BF16)
    mh[there, lanes(other)] = blank
    ml[there, lanes(other)] = blank

    @pl.when(upper == 1)
    def _():
        w_ref[...] = turned

    outer = jnp.zeros((1, N), F32)
    for i in range(H):
        outer += jnp.sum(w_ref[strip(i), :] * w_ref[strip(i), :], axis=0, keepdims=True)

    spot = lax.broadcasted_iota(jnp.int32, (1, 128), 1)
    both = jnp.where(spot == 0, tr_ref[...], 0.0)
    both = jnp.where(spot == 1, jnp.sum(inner, axis=1, keepdims=True), both)
    both = jnp.where(spot == 2, jnp.sum(outer, axis=1, keepdims=True), both)
    sums_ref[...] = jnp.broadcast_to(both, sums_ref.shape)

    wide = (lax.broadcasted_iota(jnp.int32, (B, 128), 1) >= B).astype(jnp.int32)
    shift = 6 - 2 * col

    def share(i, rows, panel):
        block = rows + i + shift
        pair = row(jnp.clip(block, -1, 2 * H - 1), 128)
        span = lanes(panel)
        product = dot3(
            (mh[row(rows + i), span], ml[row(rows + i), span]),
            (mh[pair, span], ml[pair, span]), NT,
        )
        index = block + wide - base
        return jnp.where((index >= 0) & (index < H), product, 0.0)

    for i in range(H):
        far_ref[strip(i), :] = share(i, other, base)
        near_ref[strip(i), :] = share(i, base, other)
        here = row(base + i)
        block = base + i + 2 * col - H
        pair = row(block, 128)
        own_ref[0, strip(i), :] = dot3((mh[here, :], ml[here, :]), (mh[pair, :], ml[pair, :]), NT)
        if i % 2:
            span = pl.ds(pl.multiple_of((block - 1) * B, 128), 256)
            held = mh[here, span].astype(F32) + ml[here, span].astype(F32)
            held = held[:, B : B + 128]
        else:
            span = pl.ds(pl.multiple_of(block * B, 128), 128)
            held = mh[here, span].astype(F32) + ml[here, span].astype(F32)
        own_ref[1, strip(i), :] = held


def last_kernel(s_ref, own_ref, far_ref, near_ref, sums_ref, out_ref, traces_ref):
    col, upper = s_ref[2], s_ref[3]
    wide = lax.broadcasted_iota(jnp.int32, (B, 128), 1) >= B
    for i in range(H):
        squared = own_ref[0, strip(i), :] + (far_ref[strip(i), :] + near_ref[strip(i), :])
        keep, pick = [], []
        for h in range(2):
            far = jnp.abs(2 * col + h - H)
            reach = jnp.minimum(s_ref[RAD + H + i], s_ref[RAD + i + 2 * col + h])
            keep.append((far <= reach).astype(F32))
            pick.append((s_ref[BR[1] + H + i] * s_ref[BR[1] + i + 2 * col + h]).astype(F32))
        squared = squared * jnp.where(wide, keep[1], keep[0])
        chosen = jnp.where(wide, pick[1], pick[0]) == 1.0
        new = jnp.where(chosen, 2.0 * own_ref[1, strip(i), :] - squared, squared)
        out_ref[i, 0] = new[:, :B]
        out_ref[i, 1] = new[:, B:]
    sums = sums_ref[...]
    count = sums.shape[0]
    spot = lax.broadcasted_iota(jnp.int32, sums.shape, 1)
    line = lax.broadcasted_iota(jnp.int32, sums.shape, 0)
    turned = jnp.concatenate([sums[count - 1 :], sums[: count - 1]], axis=0)
    sums = jnp.where((spot == 2) & (upper + 0 * line == 1), turned, sums)
    total = jnp.sum(sums, axis=0, keepdims=True)
    spot = lax.broadcasted_iota(jnp.int32, total.shape, 1)
    weight = jnp.where(spot == 1, 1.0, jnp.where(spot == 2, 2.0, 0.0))
    traces_ref[0] = jnp.sum(jnp.where(spot == 0, total, 0.0))
    traces_ref[1] = jnp.sum(total * weight)


def shape(*dims):
    return jax.ShapeDtypeStruct(dims, F32)


def per_device(rows, values, radius, branch):
    both = ("row", "col")
    row, col = lax.axis_index("row"), lax.axis_index("col")
    pad = ((H, H),)
    radii = lax.dynamic_slice(jnp.pad(radius, pad, constant_values=-1), (H * row,), (3 * H,))
    flags = lax.dynamic_slice(jnp.pad(branch, ((0, 0),) + pad), (0, H * row), (2, 3 * H))
    scalars = jnp.concatenate(
        [jnp.stack([col // 2, col % 2, col, col // 4]).astype(jnp.int32), radii, flags[0], flags[1]]
    )

    def swap(x):
        return lax.ppermute(x, "col", [(c, c ^ 1) for c in range(8)])

    def to_rows(x, pairs):
        return lax.ppermute(x, both, pairs)

    def index(r, c):
        return r * 8 + c

    ends = [(r, c) for r in range(rows - 1) for c in range(4)]

    packed, diag = call(
        pack_kernel, out_shape=[shape(N, 128), shape(256, 128)], in_specs=[VMEM],
        out_specs=[VMEM] * 2, mib=8, name="pack",
    )(values)
    near = lax.ppermute(packed, "col", [(c, c ^ 2) for c in range(8)])
    d1 = lax.ppermute(diag, "col", [(4, 2)])
    d2 = lax.ppermute(diag, "col", [(4, 0)])
    later, d1 = lax.optimization_barrier((packed, d1))
    cross = lax.ppermute(later, "col", [(c, c ^ 4) for c in range(8)])
    far = lax.ppermute(later, "col", [(c, c ^ 6) for c in range(8)])
    triangle, joined = call(
        triangle_kernel,
        out_shape=[shape(576, 128), shape(2 * N, 128)],
        in_specs=[SMEM] + [VMEM] * 4,
        out_specs=[VMEM] * 2,
        scratch_shapes=[pltpu.VMEM((N, 128), F32)] * 2,
        mib=8, name="triangle",
    )(scalars, packed, near, d1, d2)
    pairs = [(index(r, c + 4), index(r + 1, c)) for r, c in ends]
    ta = lax.ppermute(triangle, both, pairs + [(b, a) for a, b in pairs])
    joined2 = swap(joined)
    distant = call(
        join_kernel, out_shape=shape(2 * N, 128), in_specs=[VMEM] * 2, out_specs=VMEM,
        mib=8, name="join",
    )(cross, far)
    distant2 = swap(distant)
    tb = swap(ta)

    *old, trace = call(
        square_kernel,
        out_shape=[
            shape(N, N), shape(N, N), jax.ShapeDtypeStruct((N, N), BF16),
            jax.ShapeDtypeStruct((N, N), BF16), shape(N, N), shape(1, 128),
        ],
        in_specs=[SMEM] + [VMEM] * 4,
        out_specs=[VMEM] * 6,
        scratch_shapes=[
            pltpu.VMEM((N, 2 * N), F32),
            pltpu.VMEM((N, W), F32),
            pltpu.VMEM((N, W), BF16),
            pltpu.VMEM((N, W), BF16),
        ],
        mib=24, name="square",
    )(scalars, joined, joined2, distant, distant2)

    own, far, near, sums = call(
        second_kernel,
        out_shape=[shape(2, N, 128), shape(N, 128), shape(N, 128), shape(rows, 128)],
        in_specs=[SMEM] + [VMEM] * 8,
        out_specs=[VMEM] * 4,
        scratch_shapes=[
            pltpu.VMEM((2, 576, 128), F32),
            pltpu.VMEM((N, N), F32),
            pltpu.VMEM((18 * B, 2 * N), BF16),
            pltpu.VMEM((18 * B, 2 * N), BF16),
        ],
        mib=24, name="second",
    )(scalars, *old, trace, ta, tb)

    pairs = [(index(r, 7 - c), index(r + 1, c)) for r, c in ends]
    far = lax.ppermute(far, both, pairs + [(b, a) for a, b in pairs])
    near = lax.ppermute(near, "col", [(c, 7 - c) for c in range(8)])
    sums = lax.all_to_all(sums, "row", 0, 0, tiled=True)
    return call(
        last_kernel,
        out_shape=[shape(H, 2, B, B), shape(2)],
        in_specs=[SMEM] + [VMEM] * 4,
        out_specs=[VMEM, SMEM],
        mib=8, name="last",
    )(scalars, own, far, near, sums)


def solution(mesh):
    rows = mesh.shape["row"]

    def run(values, radius, branch):
        return per_device(rows, values, radius, branch)

    in_specs = (P("row", "col", None, None), P(), P())
    out_specs = (P("row", "col", None, None), P())
    return jax.shard_map(
        run, mesh=mesh, in_specs=in_specs, out_specs=out_specs, check_vma=False
    )
```

```python
import jax
import jax.numpy as jnp
from jax import lax
from jax.experimental import pallas as pl
from jax.experimental.pallas import tpu as pltpu
from jax.sharding import PartitionSpec as P

F32 = jnp.float32
BF16 = jnp.bfloat16
B = 64
H = 8
N = H * B
W = 3 * N
VMEM = pl.BlockSpec(memory_space=pltpu.VMEM)
SMEM = pl.BlockSpec(memory_space=pltpu.SMEM)
RAD, BR = 4, (28, 52)


def call(kernel, mib, name, **rest):
    return pl.pallas_call(
        kernel,
        name=name,
        compiler_params=pltpu.CompilerParams(vmem_limit_bytes=mib << 20),
        **rest,
    )


def halves(x):
    hi = x.astype(BF16)
    return hi, (x - hi.astype(F32)).astype(BF16)


def dot3(a, b, dims):
    (ah, al), (bh, bl) = a, b

    def one(x, y):
        return lax.dot_general(x, y, (dims, ((), ())), preferred_element_type=F32)

    return one(ah, bh) + (one(ah, bl) + one(al, bh))


def dot3_stacked(a, b):
    (ah, al), (bh, bl) = a, b
    size = ah.shape[0]

    def one(x, y):
        return lax.dot_general(x, y, (NT, ((), ())), preferred_element_type=F32)

    both = one(jnp.concatenate([ah, al], axis=0), bh)
    return both[:size] + (one(ah, bl) + both[size:])


NN = ((1,), (0,))
NT = ((1,), (1,))


def strip(i):
    return slice(i * B, (i + 1) * B)


class Rules:
    def __init__(self, s_ref, start, rows, cols):
        self.s_ref, self.start, self.rows, self.cols = s_ref, start, rows, cols
        block = lax.shift_right_logical(lax.broadcasted_iota(jnp.int32, (1, N), 1), 6)
        radii = flags = jnp.zeros((1, N), jnp.int32)
        for k in range(H):
            radii = jnp.where(block == k, s_ref[RAD + cols + k], radii)
            flags = jnp.where(block == k, s_ref[start + cols + k], flags)
        self.block, self.radii, self.flags = block + cols, radii, flags

    def strip(self, i):
        reach = jnp.minimum(self.radii, self.s_ref[RAD + self.rows + i])
        keep = jnp.abs(self.block - (self.rows + i)) <= reach
        return keep, self.flags * self.s_ref[self.start + self.rows + i] == 1


def pack_kernel(v_ref, out_ref, diag_ref):
    for i in range(H):
        out_ref[strip(i), :] = jnp.concatenate([v_ref[i, 0], v_ref[i, 1]], axis=1)
    for i in range(4):
        diag_ref[strip(i), :] = jnp.concatenate([v_ref[i, 0], v_ref[i + 4, 0]], axis=1)


def join_kernel(first_ref, second_ref, out_ref):
    out_ref[0:N, :] = first_ref[...]
    out_ref[N : 2 * N, :] = second_ref[...]


def triangle_kernel(s_ref, own_ref, near_ref, d1_ref, d2_ref, out_ref, both_ref, low, high):
    odd, core, upper = (s_ref[0] & 1) == 1, s_ref[1], s_ref[3]
    both_ref[0:N, :] = own_ref[...]
    both_ref[N : 2 * N, :] = near_ref[...]
    low[...] = jnp.where(odd, near_ref[...], own_ref[...])
    high[...] = jnp.where(odd, own_ref[...], near_ref[...])

    def rows(ref, first, last):
        return ref[first * B : (last + 1) * B, :]

    @pl.when((upper == 0) & (core == 0))
    def _():
        out_ref[0:256, :] = rows(high, 3, 6)
        out_ref[256:512, :] = d1_ref[...] + d2_ref[...]
        out_ref[512:576, :] = jnp.zeros((B, 128), F32)

    @pl.when((upper == 0) & (core == 1))
    def _():
        out_ref[0:384, :] = rows(high, 1, 6)
        out_ref[384:512, :] = rows(low, 5, 6)
        out_ref[512:576, :] = jnp.zeros((B, 128), F32)

    @pl.when((upper == 1) & (core == 0))
    def _():
        out_ref[0:384, :] = rows(low, 1, 6)
        out_ref[384:512, :] = rows(high, 1, 2)
        last = jnp.concatenate([rows(high, 3, 3)[:, :B], rows(low, 7, 7)[:, :B]], axis=1)
        out_ref[512:576, :] = last

    @pl.when((upper == 1) & (core == 1))
    def _():
        out_ref[0:320, :] = rows(low, 1, 5)
        out_ref[320:384, :] = rows(high, 1, 1)
        out_ref[384:576, :] = jnp.zeros((192, 128), F32)


def square_kernel(s_ref, *refs):
    packs, (p1_ref, v_ref, vh_ref, vl_ref, pv_ref, tr_ref) = refs[:4], refs[4:10]
    q_ref, r_ref, rh, rl = refs[10:]
    yl, core, upper = s_ref[0], s_ref[1], s_ref[3]
    for k in range(4):
        for other in range(2):
            place = 2 * (yl ^ k) + (core ^ other)
            part = packs[k // 2 * 2 + other][k % 2 * N : (k % 2 + 1) * N, :]
            q_ref[:, pl.ds(pl.multiple_of(place * 128, 128), 128)] = part
    total = jnp.zeros((1, 2 * N), F32)
    for i in range(H):
        own = q_ref[strip(i), :]
        total += jnp.sum(own * own, axis=0, keepdims=True)
        at = i * B
        if i % 2:
            own = pltpu.roll(jnp.concatenate([own, jnp.zeros((B, 128), F32)], axis=1), B, 1)
            at -= B
        parts = [own]
        if at:
            parts.insert(0, jnp.zeros((B, at), F32))
        left = W - at - own.shape[1]
        if left:
            parts.append(jnp.zeros((B, left), F32))
        full = jnp.concatenate(parts, axis=1)
        r_ref[strip(i), :] = full
        rh[strip(i), :], rl[strip(i), :] = halves(full)
    tr_ref[...] = jnp.broadcast_to(jnp.sum(total, axis=1, keepdims=True), tr_ref.shape)

    def part(rows, cols):
        return rh[rows, cols], rl[rows, cols]

    lo, hi = slice(0, 256), slice(256, 512)
    mid = slice(N, 2 * N)
    side = pl.ds(pl.multiple_of(2 * N * upper, 128), N)
    v_ref[...] = r_ref[:, side]
    vh_ref[...], vl_ref[...] = rh[:, side], rl[:, side]
    pv_ref[...] = dot3(part(slice(None), mid), (vh_ref[...], vl_ref[...]), NN)

    p01 = dot3(part(lo, slice(256, 1280)), part(hi, slice(256, 1280)), NT)
    p1_ref[lo, lo] = dot3(part(lo, slice(0, 1280)), part(lo, slice(0, 1280)), NT)
    p1_ref[lo, hi] = p01
    p1_ref[hi, lo] = p01.T
    p1_ref[hi, hi] = dot3(part(hi, slice(256, W)), part(hi, slice(256, W)), NT)
    rules = Rules(s_ref, BR[0], H, H)
    for i in range(H):
        keep, pick = rules.strip(i)
        squared = jnp.where(keep, p1_ref[strip(i), :], 0.0)
        p1_ref[strip(i), :] = jnp.where(pick, 2.0 * r_ref[strip(i), mid] - squared, squared)


def second_kernel(s_ref, p1_ref, v_ref, vh_ref, vl_ref, pv_ref, tr_ref, ta, tb,
                  own_ref, share_ref, sums_ref, t_ref, w_ref, mh, ml):
    core, col, upper = s_ref[1], s_ref[2], s_ref[3]
    lane = lax.broadcasted_iota(jnp.int32, (B, N), 1)
    zero = jnp.zeros((B, 128), F32)
    base, other = H * (1 - upper), H * upper
    t_ref[core, :, :] = ta[...]
    t_ref[1 - core, :, :] = tb[...]

    def line(which, start):
        return t_ref[which, start * B : (start + 1) * B, :]

    @pl.when(upper == 0)
    def _():
        w_ref[strip(0), :] = jnp.zeros((B, N), F32)
        for k in range(1, H):
            parts = [line(0, k - 1), zero, zero, zero]
            if k == 7:
                parts[0] = pltpu.roll(line(0, 8), B, 1)
            if k < 6:
                parts[1] = line(1, k - 1)
            if k < 4:
                parts[2] = line(0, 5 + k)
            if k < 2:
                parts[3] = line(1, 4 + k)
            turned = pltpu.roll(jnp.concatenate(parts, axis=1), k * B, 1)
            w_ref[strip(k), :] = jnp.where(lane >= k * B, turned, 0.0)

    @pl.when(upper == 1)
    def _():
        w_ref[strip(7), :] = jnp.zeros((B, N), F32)
        for k in range(7):
            diag = line(0, 4 + k % 4)
            if k >= 4:
                diag = pltpu.roll(diag, B, 1)
            parts = [zero, zero, zero, diag]
            if k >= 5:
                parts[0] = line(1, k + 1)
            if k >= 3:
                parts[1] = line(0, k - 3)
            if k >= 1:
                parts[2] = line(1, k - 1)
            turned = pltpu.roll(jnp.concatenate(parts, axis=1), ((k + 2) % 8) * B, 1)
            w_ref[strip(k), :] = jnp.where(lane < (k + 1) * B, turned, 0.0)

    full = w_ref[...]
    above = lax.shift_right_logical(lax.broadcasted_iota(jnp.int32, (N, N), 0), 6)
    along = lax.shift_right_logical(lax.broadcasted_iota(jnp.int32, (N, N), 1), 6)
    full = jnp.where(above == along, full, full + full.T)
    w_ref[...] = pv_ref[...] + dot3((vh_ref[...], vl_ref[...]), halves(full), NN)

    def at(block, size):
        return pl.ds(pl.multiple_of(block * B, B), size)

    def row(block, size=B):
        return at(block + 1, size)

    def lanes(block):
        return pl.ds(pl.multiple_of(block * B, 128), N)

    rules = Rules(s_ref, BR[0], H, 2 * H * upper)
    inner = jnp.zeros((1, N), F32)
    for i in range(H):
        keep, pick = rules.strip(i)
        squared = jnp.where(keep, w_ref[strip(i), :], 0.0)
        new = jnp.where(pick, 2.0 * v_ref[strip(i), :] - squared, squared)
        w_ref[strip(i), :] = new
        here = row(base + i)
        mh[here, lanes(other)], ml[here, lanes(other)] = halves(new)
        new = p1_ref[strip(i), :]
        inner += jnp.sum(new * new, axis=0, keepdims=True)
        mh[here, lanes(base)], ml[here, lanes(base)] = halves(new)
    turned = w_ref[...].T
    there = row(other, N)
    mh[there, lanes(base)], ml[there, lanes(base)] = halves(turned)
    blank = jnp.zeros((N, N), BF16)
    mh[there, lanes(other)] = blank
    ml[there, lanes(other)] = blank

    @pl.when(upper == 1)
    def _():
        w_ref[...] = turned

    outer = jnp.zeros((1, N), F32)
    for i in range(H):
        outer += jnp.sum(w_ref[strip(i), :] * w_ref[strip(i), :], axis=0, keepdims=True)

    spot = lax.broadcasted_iota(jnp.int32, (1, 128), 1)
    both = jnp.where(spot == 0, tr_ref[...], 0.0)
    both = jnp.where(spot == 1, jnp.sum(inner, axis=1, keepdims=True), both)
    both = jnp.where(spot == 2, jnp.sum(outer, axis=1, keepdims=True), both)
    sums_ref[...] = jnp.broadcast_to(both, sums_ref.shape)

    shift = 6 - 2 * col

    def share(i, rows, block, panel):
        pair, span = row(block, 128), lanes(panel)
        return dot3_stacked(
            (mh[row(rows + i), span], ml[row(rows + i), span]), (mh[pair, span], ml[pair, span])
        )

    for i in range(H):
        far = (upper == 0) & (shift + i >= H) | (upper == 1) & (shift + i < 0)
        rows = jnp.where(far, other, base)
        share_ref[strip(i), :] = share(i, rows, rows + i + shift, jnp.where(far, base, other))
        here = row(base + i)
        block = base + i + 2 * col - H
        pair = row(block, 128)
        own_ref[0, strip(i), :] = dot3_stacked(
            (mh[here, :], ml[here, :]), (mh[pair, :], ml[pair, :])
        )
        if i % 2:
            span = pl.ds(pl.multiple_of((block - 1) * B, 128), 256)
            held = mh[here, span].astype(F32) + ml[here, span].astype(F32)
            held = held[:, B : B + 128]
        else:
            span = pl.ds(pl.multiple_of(block * B, 128), 128)
            held = mh[here, span].astype(F32) + ml[here, span].astype(F32)
        own_ref[1, strip(i), :] = held
    i = 2 * (col & 3) + 1
    here = at(i, B)
    wide = lax.broadcasted_iota(jnp.int32, (B, 128), 1) >= B
    share_ref[here, :] = jnp.where(wide, share(i, 0, 7 - 8 * upper, H), share_ref[here, :])


def last_kernel(s_ref, own_ref, far_ref, near_ref, sums_ref, out_ref, traces_ref):
    col, upper = s_ref[2], s_ref[3]
    wide = lax.broadcasted_iota(jnp.int32, (B, 128), 1) >= B
    for i in range(H):
        index = i + 2 * col - H + wide.astype(jnp.int32)
        inside = (index >= 0) & (index < H)
        share = jnp.where(inside, near_ref[strip(i), :], far_ref[strip(i), :])
        squared = own_ref[0, strip(i), :] + share
        keep, pick = [], []
        for h in range(2):
            far = jnp.abs(2 * col + h - H)
            reach = jnp.minimum(s_ref[RAD + H + i], s_ref[RAD + i + 2 * col + h])
            keep.append((far <= reach).astype(F32))
            pick.append((s_ref[BR[1] + H + i] * s_ref[BR[1] + i + 2 * col + h]).astype(F32))
        squared = squared * jnp.where(wide, keep[1], keep[0])
        chosen = jnp.where(wide, pick[1], pick[0]) == 1.0
        new = jnp.where(chosen, 2.0 * own_ref[1, strip(i), :] - squared, squared)
        out_ref[i, 0] = new[:, :B]
        out_ref[i, 1] = new[:, B:]
    sums = sums_ref[...]
    count = sums.shape[0]
    spot = lax.broadcasted_iota(jnp.int32, sums.shape, 1)
    line = lax.broadcasted_iota(jnp.int32, sums.shape, 0)
    turned = jnp.concatenate([sums[count - 1 :], sums[: count - 1]], axis=0)
    sums = jnp.where((spot == 2) & (upper + 0 * line == 1), turned, sums)
    total = jnp.sum(sums, axis=0, keepdims=True)
    spot = lax.broadcasted_iota(jnp.int32, total.shape, 1)
    weight = jnp.where(spot == 1, 1.0, jnp.where(spot == 2, 2.0, 0.0))
    traces_ref[0] = jnp.sum(jnp.where(spot == 0, total, 0.0))
    traces_ref[1] = jnp.sum(total * weight)


def shape(*dims):
    return jax.ShapeDtypeStruct(dims, F32)


def per_device(rows, values, radius, branch):
    both = ("row", "col")
    row, col = lax.axis_index("row"), lax.axis_index("col")
    pad = ((H, H),)
    radii = lax.dynamic_slice(jnp.pad(radius, pad, constant_values=-1), (H * row,), (3 * H,))
    flags = lax.dynamic_slice(jnp.pad(branch, ((0, 0),) + pad), (0, H * row), (2, 3 * H))
    scalars = jnp.concatenate(
        [jnp.stack([col // 2, col % 2, col, col // 4]).astype(jnp.int32), radii, flags[0], flags[1]]
    )

    def swap(x):
        return lax.ppermute(x, "col", [(c, c ^ 1) for c in range(8)])

    def to_rows(x, pairs):
        return lax.ppermute(x, both, pairs)

    def index(r, c):
        return r * 8 + c

    ends = [(r, c) for r in range(rows - 1) for c in range(4)]

    packed, diag = call(
        pack_kernel, out_shape=[shape(N, 128), shape(256, 128)], in_specs=[VMEM],
        out_specs=[VMEM] * 2, mib=8, name="pack",
    )(values)
    near = lax.ppermute(packed, "col", [(c, c ^ 2) for c in range(8)])
    d1 = lax.ppermute(diag, "col", [(4, 2)])
    d2 = lax.ppermute(diag, "col", [(4, 0)])
    later, d1 = lax.optimization_barrier((packed, d1))
    cross = lax.ppermute(later, "col", [(c, c ^ 4) for c in range(8)])
    far = lax.ppermute(later, "col", [(c, c ^ 6) for c in range(8)])
    triangle, joined = call(
        triangle_kernel,
        out_shape=[shape(576, 128), shape(2 * N, 128)],
        in_specs=[SMEM] + [VMEM] * 4,
        out_specs=[VMEM] * 2,
        scratch_shapes=[pltpu.VMEM((N, 128), F32)] * 2,
        mib=8, name="triangle",
    )(scalars, packed, near, d1, d2)
    pairs = [(index(r, c + 4), index(r + 1, c)) for r, c in ends]
    ta = lax.ppermute(triangle, both, pairs + [(b, a) for a, b in pairs])
    joined2 = swap(joined)
    distant = call(
        join_kernel, out_shape=shape(2 * N, 128), in_specs=[VMEM] * 2, out_specs=VMEM,
        mib=8, name="join",
    )(cross, far)
    distant2 = swap(distant)
    tb = swap(ta)

    *old, trace = call(
        square_kernel,
        out_shape=[
            shape(N, N), shape(N, N), jax.ShapeDtypeStruct((N, N), BF16),
            jax.ShapeDtypeStruct((N, N), BF16), shape(N, N), shape(1, 128),
        ],
        in_specs=[SMEM] + [VMEM] * 4,
        out_specs=[VMEM] * 6,
        scratch_shapes=[
            pltpu.VMEM((N, 2 * N), F32),
            pltpu.VMEM((N, W), F32),
            pltpu.VMEM((N, W), BF16),
            pltpu.VMEM((N, W), BF16),
        ],
        mib=24, name="square",
    )(scalars, joined, joined2, distant, distant2)

    own, share, sums = call(
        second_kernel,
        out_shape=[shape(2, N, 128), shape(N, 128), shape(rows, 128)],
        in_specs=[SMEM] + [VMEM] * 8,
        out_specs=[VMEM] * 3,
        scratch_shapes=[
            pltpu.VMEM((2, 576, 128), F32),
            pltpu.VMEM((N, N), F32),
            pltpu.VMEM((18 * B, 2 * N), BF16),
            pltpu.VMEM((18 * B, 2 * N), BF16),
        ],
        mib=24, name="second",
    )(scalars, *old, trace, ta, tb)

    pairs = [(index(r, 7 - c), index(r + 1, c)) for r, c in ends]
    far = lax.ppermute(share, both, pairs + [(b, a) for a, b in pairs])
    near = lax.ppermute(share, "col", [(c, 7 - c) for c in range(8)])
    sums = lax.all_to_all(sums, "row", 0, 0, tiled=True)
    return call(
        last_kernel,
        out_shape=[shape(H, 2, B, B), shape(2)],
        in_specs=[SMEM] + [VMEM] * 4,
        out_specs=[VMEM, SMEM],
        mib=8, name="last",
    )(scalars, own, far, near, sums)


def solution(mesh):
    rows = mesh.shape["row"]

    def run(values, radius, branch):
        return per_device(rows, values, radius, branch)

    in_specs = (P("row", "col", None, None), P(), P())
    out_specs = (P("row", "col", None, None), P())
    return jax.shard_map(
        run, mesh=mesh, in_specs=in_specs, out_specs=out_specs, check_vma=False
    )
```

```python
import jax
import jax.numpy as jnp
from jax import lax
from jax.experimental import pallas as pl
from jax.experimental.pallas import tpu as pltpu
from jax.sharding import PartitionSpec as P

F32 = jnp.float32
BF16 = jnp.bfloat16
B = 64
H = 8
N = H * B
W = 3 * N
VMEM = pl.BlockSpec(memory_space=pltpu.VMEM)
SMEM = pl.BlockSpec(memory_space=pltpu.SMEM)
RAD, BR = 4, (28, 52)


def call(kernel, mib, name, **rest):
    return pl.pallas_call(
        kernel,
        name=name,
        compiler_params=pltpu.CompilerParams(vmem_limit_bytes=mib << 20),
        **rest,
    )


def halves(x):
    hi = x.astype(BF16)
    return hi, (x - hi.astype(F32)).astype(BF16)


def dot3(a, b, dims):
    (ah, al), (bh, bl) = a, b

    def one(x, y):
        return lax.dot_general(x, y, (dims, ((), ())), preferred_element_type=F32)

    return one(ah, bh) + (one(ah, bl) + one(al, bh))


def dot3_stacked(a, b):
    (ah, al), (bh, bl) = a, b
    size = ah.shape[0]

    def one(x, y):
        return lax.dot_general(x, y, (NT, ((), ())), preferred_element_type=F32)

    both = one(jnp.concatenate([ah, al], axis=0), bh)
    return both[:size] + (one(ah, bl) + both[size:])


NN = ((1,), (0,))
NT = ((1,), (1,))


def strip(i):
    return slice(i * B, (i + 1) * B)


class Rules:
    def __init__(self, s_ref, start, rows, cols):
        self.s_ref, self.start, self.rows, self.cols = s_ref, start, rows, cols
        block = lax.shift_right_logical(lax.broadcasted_iota(jnp.int32, (1, N), 1), 6)
        radii = flags = jnp.zeros((1, N), jnp.int32)
        for k in range(H):
            radii = jnp.where(block == k, s_ref[RAD + cols + k], radii)
            flags = jnp.where(block == k, s_ref[start + cols + k], flags)
        self.block, self.radii, self.flags = block + cols, radii, flags

    def strip(self, i):
        reach = jnp.minimum(self.radii, self.s_ref[RAD + self.rows + i])
        keep = jnp.abs(self.block - (self.rows + i)) <= reach
        return keep, self.flags * self.s_ref[self.start + self.rows + i] == 1


def pack_kernel(v_ref, out_ref, diag_ref, cut_ref):
    for i in range(H):
        out_ref[strip(i), :] = jnp.concatenate([v_ref[i, 0], v_ref[i, 1]], axis=1)
    for i in range(4):
        diag_ref[strip(i), :] = jnp.concatenate([v_ref[i, 0], v_ref[i + 4, 0]], axis=1)
    col = lax.axis_index("col")

    @pl.when(col < 4)
    def _():
        cut_ref[...] = out_ref[0 : N - B, :]

    @pl.when(col >= 4)
    def _():
        cut_ref[...] = out_ref[B:N, :]

    @pl.when(col == 4)
    def _():
        cut_ref[0:B, :] = jnp.concatenate([v_ref[1, 0], v_ref[0, 0]], axis=1)


def join_kernel(first_ref, second_ref, out_ref):
    out_ref[0 : N - B, :] = first_ref[...]
    out_ref[N - B : 2 * (N - B), :] = second_ref[...]


def triangle_kernel(s_ref, own_ref, near_ref, d1_ref, d2_ref, out_ref, both_ref, low, high):
    odd, core, upper = (s_ref[0] & 1) == 1, s_ref[1], s_ref[3]
    both_ref[0:N, :] = own_ref[...]
    both_ref[N : 2 * N, :] = near_ref[...]
    low[...] = jnp.where(odd, near_ref[...], own_ref[...])
    high[...] = jnp.where(odd, own_ref[...], near_ref[...])

    def rows(ref, first, last):
        return ref[first * B : (last + 1) * B, :]

    @pl.when((upper == 0) & (core == 0))
    def _():
        out_ref[0:256, :] = rows(high, 3, 6)
        out_ref[256:512, :] = d1_ref[...] + d2_ref[...]
        out_ref[512:576, :] = jnp.zeros((B, 128), F32)

    @pl.when((upper == 0) & (core == 1))
    def _():
        out_ref[0:384, :] = rows(high, 1, 6)
        out_ref[384:512, :] = rows(low, 5, 6)
        out_ref[512:576, :] = jnp.zeros((B, 128), F32)

    @pl.when((upper == 1) & (core == 0))
    def _():
        out_ref[0:384, :] = rows(low, 1, 6)
        out_ref[384:512, :] = rows(high, 1, 2)
        last = jnp.concatenate([rows(high, 3, 3)[:, :B], rows(low, 7, 7)[:, :B]], axis=1)
        out_ref[512:576, :] = last

    @pl.when((upper == 1) & (core == 1))
    def _():
        out_ref[0:320, :] = rows(low, 1, 5)
        out_ref[320:384, :] = rows(high, 1, 1)
        out_ref[384:576, :] = jnp.zeros((192, 128), F32)


def square_kernel(s_ref, *refs):
    packs, (p1_ref, v_ref, vh_ref, vl_ref, pv_ref, tr_ref) = refs[:4], refs[4:10]
    q_ref, r_ref, rh, rl = refs[10:]
    yl, core, upper = s_ref[0], s_ref[1], s_ref[3]
    def place(k, other):
        return pl.ds(pl.multiple_of(128 * (2 * (yl ^ k) + (core ^ other)), 128), 128)

    for other in range(2):
        for k in range(2):
            q_ref[:, place(k, other)] = packs[other][k * N : (k + 1) * N, :]

    def cut(k, other):
        return packs[2 + other][(k - 2) * (N - B) : (k - 1) * (N - B), :]

    @pl.when(upper == 0)
    def _():
        for other in range(2):
            for k in range(2, 4):
                q_ref[B:N, place(k, other)] = cut(k, other)
        first = pltpu.roll(q_ref[B : 2 * B, N : N + 128], B, 1)
        lane = lax.broadcasted_iota(jnp.int32, (B, 128), 1)
        q_ref[0:B, N : N + 128] = jnp.where(lane < B, first, 0.0)
        q_ref[0:B, N + 128 : 2 * N] = jnp.zeros((B, N - 128), F32)

    @pl.when(upper == 1)
    def _():
        for other in range(2):
            for k in range(2, 4):
                q_ref[0 : N - B, place(k, other)] = cut(k, other)
        q_ref[N - B : N, 0:N] = jnp.zeros((B, N), F32)

    for i in range(H):
        own = q_ref[strip(i), :]
        at = i * B
        if i % 2:
            own = pltpu.roll(jnp.concatenate([own, jnp.zeros((B, 128), F32)], axis=1), B, 1)
            at -= B
        parts = [own]
        if at:
            parts.insert(0, jnp.zeros((B, at), F32))
        left = W - at - own.shape[1]
        if left:
            parts.append(jnp.zeros((B, left), F32))
        r_ref[strip(i), :] = jnp.concatenate(parts, axis=1)
    inner = r_ref[:, N : 2 * N]
    above = lax.shift_right_logical(lax.broadcasted_iota(jnp.int32, (N, N), 0), 6)
    along = lax.shift_right_logical(lax.broadcasted_iota(jnp.int32, (N, N), 1), 6)
    half = jnp.where((above - along) * (1 - 2 * upper) > 0, inner, 0.0)
    r_ref[:, N : 2 * N] = jnp.where(above == along, inner, half + half.T)
    total = jnp.zeros((1, W), F32)
    for i in range(H):
        full = r_ref[strip(i), :]
        total += jnp.sum(full * full, axis=0, keepdims=True)
        rh[strip(i), :], rl[strip(i), :] = halves(full)
    tr_ref[...] = jnp.broadcast_to(jnp.sum(total, axis=1, keepdims=True), tr_ref.shape)

    def part(rows, cols):
        return rh[rows, cols], rl[rows, cols]

    lo, hi = slice(0, 256), slice(256, 512)
    mid = slice(N, 2 * N)
    side = pl.ds(pl.multiple_of(2 * N * upper, 128), N)
    v_ref[...] = r_ref[:, side]
    vh_ref[...], vl_ref[...] = rh[:, side], rl[:, side]
    pv_ref[...] = dot3(part(slice(None), mid), (vh_ref[...], vl_ref[...]), NN)

    p01 = dot3(part(lo, slice(256, 1280)), part(hi, slice(256, 1280)), NT)
    p1_ref[lo, lo] = dot3(part(lo, slice(0, 1280)), part(lo, slice(0, 1280)), NT)
    p1_ref[lo, hi] = p01
    p1_ref[hi, lo] = p01.T
    p1_ref[hi, hi] = dot3(part(hi, slice(256, W)), part(hi, slice(256, W)), NT)
    rules = Rules(s_ref, BR[0], H, H)
    for i in range(H):
        keep, pick = rules.strip(i)
        squared = jnp.where(keep, p1_ref[strip(i), :], 0.0)
        p1_ref[strip(i), :] = jnp.where(pick, 2.0 * r_ref[strip(i), mid] - squared, squared)


def second_kernel(s_ref, p1_ref, v_ref, vh_ref, vl_ref, pv_ref, tr_ref, ta, tb,
                  own_ref, share_ref, sums_ref, t_ref, w_ref, mh, ml):
    core, col, upper = s_ref[1], s_ref[2], s_ref[3]
    lane = lax.broadcasted_iota(jnp.int32, (B, N), 1)
    zero = jnp.zeros((B, 128), F32)
    base, other = H * (1 - upper), H * upper
    t_ref[core, :, :] = ta[...]
    t_ref[1 - core, :, :] = tb[...]

    def line(which, start):
        return t_ref[which, start * B : (start + 1) * B, :]

    @pl.when(upper == 0)
    def _():
        w_ref[strip(0), :] = jnp.zeros((B, N), F32)
        for k in range(1, H):
            parts = [line(0, k - 1), zero, zero, zero]
            if k == 7:
                parts[0] = pltpu.roll(line(0, 8), B, 1)
            if k < 6:
                parts[1] = line(1, k - 1)
            if k < 4:
                parts[2] = line(0, 5 + k)
            if k < 2:
                parts[3] = line(1, 4 + k)
            turned = pltpu.roll(jnp.concatenate(parts, axis=1), k * B, 1)
            w_ref[strip(k), :] = jnp.where(lane >= k * B, turned, 0.0)

    @pl.when(upper == 1)
    def _():
        w_ref[strip(7), :] = jnp.zeros((B, N), F32)
        for k in range(7):
            diag = line(0, 4 + k % 4)
            if k >= 4:
                diag = pltpu.roll(diag, B, 1)
            parts = [zero, zero, zero, diag]
            if k >= 5:
                parts[0] = line(1, k + 1)
            if k >= 3:
                parts[1] = line(0, k - 3)
            if k >= 1:
                parts[2] = line(1, k - 1)
            turned = pltpu.roll(jnp.concatenate(parts, axis=1), ((k + 2) % 8) * B, 1)
            w_ref[strip(k), :] = jnp.where(lane < (k + 1) * B, turned, 0.0)

    full = w_ref[...]
    above = lax.shift_right_logical(lax.broadcasted_iota(jnp.int32, (N, N), 0), 6)
    along = lax.shift_right_logical(lax.broadcasted_iota(jnp.int32, (N, N), 1), 6)
    full = jnp.where(above == along, full, full + full.T)
    w_ref[...] = pv_ref[...] + dot3((vh_ref[...], vl_ref[...]), halves(full), NN)

    def at(block, size):
        return pl.ds(pl.multiple_of(block * B, B), size)

    def row(block, size=B):
        return at(block + 1, size)

    def lanes(block):
        return pl.ds(pl.multiple_of(block * B, 128), N)

    rules = Rules(s_ref, BR[0], H, 2 * H * upper)
    inner = jnp.zeros((1, N), F32)
    for i in range(H):
        keep, pick = rules.strip(i)
        squared = jnp.where(keep, w_ref[strip(i), :], 0.0)
        new = jnp.where(pick, 2.0 * v_ref[strip(i), :] - squared, squared)
        w_ref[strip(i), :] = new
        here = row(base + i)
        mh[here, lanes(other)], ml[here, lanes(other)] = halves(new)
        new = p1_ref[strip(i), :]
        inner += jnp.sum(new * new, axis=0, keepdims=True)
        mh[here, lanes(base)], ml[here, lanes(base)] = halves(new)
    turned = w_ref[...].T
    there = row(other, N)
    mh[there, lanes(base)], ml[there, lanes(base)] = halves(turned)
    blank = jnp.zeros((N, N), BF16)
    mh[there, lanes(other)] = blank
    ml[there, lanes(other)] = blank

    @pl.when(upper == 1)
    def _():
        w_ref[...] = turned

    outer = jnp.zeros((1, N), F32)
    for i in range(H):
        outer += jnp.sum(w_ref[strip(i), :] * w_ref[strip(i), :], axis=0, keepdims=True)

    spot = lax.broadcasted_iota(jnp.int32, (1, 128), 1)
    both = jnp.where(spot == 0, tr_ref[...], 0.0)
    both = jnp.where(spot == 1, jnp.sum(inner, axis=1, keepdims=True), both)
    both = jnp.where(spot == 2, jnp.sum(outer, axis=1, keepdims=True), both)
    sums_ref[...] = jnp.broadcast_to(both, sums_ref.shape)

    shift = 6 - 2 * col

    def share(i, rows, block, panel):
        pair, span = row(block, 128), lanes(panel)
        return dot3_stacked(
            (mh[row(rows + i), span], ml[row(rows + i), span]), (mh[pair, span], ml[pair, span])
        )

    for i in range(H):
        far = (upper == 0) & (shift + i >= H) | (upper == 1) & (shift + i < 0)
        rows = jnp.where(far, other, base)
        share_ref[strip(i), :] = share(i, rows, rows + i + shift, jnp.where(far, base, other))
        here = row(base + i)
        block = base + i + 2 * col - H
        pair = row(block, 128)
        own_ref[0, strip(i), :] = dot3_stacked(
            (mh[here, :], ml[here, :]), (mh[pair, :], ml[pair, :])
        )
        if i % 2:
            span = pl.ds(pl.multiple_of((block - 1) * B, 128), 256)
            held = mh[here, span].astype(F32) + ml[here, span].astype(F32)
            held = held[:, B : B + 128]
        else:
            span = pl.ds(pl.multiple_of(block * B, 128), 128)
            held = mh[here, span].astype(F32) + ml[here, span].astype(F32)
        own_ref[1, strip(i), :] = held
    i = 2 * (col & 3) + 1
    here = at(i, B)
    wide = lax.broadcasted_iota(jnp.int32, (B, 128), 1) >= B
    share_ref[here, :] = jnp.where(wide, share(i, 0, 7 - 8 * upper, H), share_ref[here, :])


def last_kernel(s_ref, own_ref, far_ref, near_ref, sums_ref, out_ref, traces_ref):
    col, upper = s_ref[2], s_ref[3]
    wide = lax.broadcasted_iota(jnp.int32, (B, 128), 1) >= B
    for i in range(H):
        index = i + 2 * col - H + wide.astype(jnp.int32)
        inside = (index >= 0) & (index < H)
        share = jnp.where(inside, near_ref[strip(i), :], far_ref[strip(i), :])
        squared = own_ref[0, strip(i), :] + share
        keep, pick = [], []
        for h in range(2):
            far = jnp.abs(2 * col + h - H)
            reach = jnp.minimum(s_ref[RAD + H + i], s_ref[RAD + i + 2 * col + h])
            keep.append((far <= reach).astype(F32))
            pick.append((s_ref[BR[1] + H + i] * s_ref[BR[1] + i + 2 * col + h]).astype(F32))
        squared = squared * jnp.where(wide, keep[1], keep[0])
        chosen = jnp.where(wide, pick[1], pick[0]) == 1.0
        new = jnp.where(chosen, 2.0 * own_ref[1, strip(i), :] - squared, squared)
        out_ref[i, 0] = new[:, :B]
        out_ref[i, 1] = new[:, B:]
    sums = sums_ref[...]
    count = sums.shape[0]
    spot = lax.broadcasted_iota(jnp.int32, sums.shape, 1)
    line = lax.broadcasted_iota(jnp.int32, sums.shape, 0)
    turned = jnp.concatenate([sums[count - 1 :], sums[: count - 1]], axis=0)
    sums = jnp.where((spot == 2) & (upper + 0 * line == 1), turned, sums)
    total = jnp.sum(sums, axis=0, keepdims=True)
    spot = lax.broadcasted_iota(jnp.int32, total.shape, 1)
    weight = jnp.where(spot == 1, 1.0, jnp.where(spot == 2, 2.0, 0.0))
    traces_ref[0] = jnp.sum(jnp.where(spot == 0, total, 0.0))
    traces_ref[1] = jnp.sum(total * weight)


def shape(*dims):
    return jax.ShapeDtypeStruct(dims, F32)


def per_device(rows, values, radius, branch):
    both = ("row", "col")
    row, col = lax.axis_index("row"), lax.axis_index("col")
    pad = ((H, H),)
    radii = lax.dynamic_slice(jnp.pad(radius, pad, constant_values=-1), (H * row,), (3 * H,))
    flags = lax.dynamic_slice(jnp.pad(branch, ((0, 0),) + pad), (0, H * row), (2, 3 * H))
    scalars = jnp.concatenate(
        [jnp.stack([col // 2, col % 2, col, col // 4]).astype(jnp.int32), radii, flags[0], flags[1]]
    )

    def swap(x):
        return lax.ppermute(x, "col", [(c, c ^ 1) for c in range(8)])

    def to_rows(x, pairs):
        return lax.ppermute(x, both, pairs)

    def index(r, c):
        return r * 8 + c

    ends = [(r, c) for r in range(rows - 1) for c in range(4)]

    packed, diag, cut = call(
        pack_kernel, out_shape=[shape(N, 128), shape(256, 128), shape(N - B, 128)],
        in_specs=[VMEM], out_specs=[VMEM] * 3, mib=8, name="pack",
    )(values)
    near = lax.ppermute(packed, "col", [(c, c ^ 2) for c in range(8)])
    d1 = lax.ppermute(diag, "col", [(4, 2)])
    d2 = lax.ppermute(diag, "col", [(4, 0)])
    cut, d1 = lax.optimization_barrier((cut, d1))
    cross = lax.ppermute(cut, "col", [(c, c ^ 4) for c in range(8)])
    far = lax.ppermute(cut, "col", [(c, c ^ 6) for c in range(8)])
    triangle, joined = call(
        triangle_kernel,
        out_shape=[shape(576, 128), shape(2 * N, 128)],
        in_specs=[SMEM] + [VMEM] * 4,
        out_specs=[VMEM] * 2,
        scratch_shapes=[pltpu.VMEM((N, 128), F32)] * 2,
        mib=8, name="triangle",
    )(scalars, packed, near, d1, d2)
    pairs = [(index(r, c + 4), index(r + 1, c)) for r, c in ends]
    ta = lax.ppermute(triangle, both, pairs + [(b, a) for a, b in pairs])
    joined2 = swap(joined)
    distant = call(
        join_kernel, out_shape=shape(2 * (N - B), 128), in_specs=[VMEM] * 2, out_specs=VMEM,
        mib=8, name="join",
    )(cross, far)
    distant2 = swap(distant)
    tb = swap(ta)

    *old, trace = call(
        square_kernel,
        out_shape=[
            shape(N, N), shape(N, N), jax.ShapeDtypeStruct((N, N), BF16),
            jax.ShapeDtypeStruct((N, N), BF16), shape(N, N), shape(1, 128),
        ],
        in_specs=[SMEM] + [VMEM] * 4,
        out_specs=[VMEM] * 6,
        scratch_shapes=[
            pltpu.VMEM((N, 2 * N), F32),
            pltpu.VMEM((N, W), F32),
            pltpu.VMEM((N, W), BF16),
            pltpu.VMEM((N, W), BF16),
        ],
        mib=24, name="square",
    )(scalars, joined, joined2, distant, distant2)

    own, share, sums = call(
        second_kernel,
        out_shape=[shape(2, N, 128), shape(N, 128), shape(rows, 128)],
        in_specs=[SMEM] + [VMEM] * 8,
        out_specs=[VMEM] * 3,
        scratch_shapes=[
            pltpu.VMEM((2, 576, 128), F32),
            pltpu.VMEM((N, N), F32),
            pltpu.VMEM((18 * B, 2 * N), BF16),
            pltpu.VMEM((18 * B, 2 * N), BF16),
        ],
        mib=24, name="second",
    )(scalars, *old, trace, ta, tb)

    pairs = [(index(r, 7 - c), index(r + 1, c)) for r, c in ends]
    far = lax.ppermute(share, both, pairs + [(b, a) for a, b in pairs])
    near = lax.ppermute(share, "col", [(c, 7 - c) for c in range(8)])
    sums = lax.all_to_all(sums, "row", 0, 0, tiled=True)
    return call(
        last_kernel,
        out_shape=[shape(H, 2, B, B), shape(2)],
        in_specs=[SMEM] + [VMEM] * 4,
        out_specs=[VMEM, SMEM],
        mib=8, name="last",
    )(scalars, own, far, near, sums)


def solution(mesh):
    rows = mesh.shape["row"]

    def run(values, radius, branch):
        return per_device(rows, values, radius, branch)

    in_specs = (P("row", "col", None, None), P(), P())
    out_specs = (P("row", "col", None, None), P())
    return jax.shard_map(
        run, mesh=mesh, in_specs=in_specs, out_specs=out_specs, check_vma=False
    )
```

```python
import jax
import jax.numpy as jnp
from jax import lax
from jax.experimental import pallas as pl
from jax.experimental.pallas import tpu as pltpu
from jax.sharding import PartitionSpec as P

F32 = jnp.float32
BF16 = jnp.bfloat16
B = 64
H = 8
N = H * B
W = 3 * N
VMEM = pl.BlockSpec(memory_space=pltpu.VMEM)
SMEM = pl.BlockSpec(memory_space=pltpu.SMEM)
RAD, BR = 4, (28, 52)


def call(kernel, mib, name, **rest):
    return pl.pallas_call(
        kernel,
        name=name,
        compiler_params=pltpu.CompilerParams(vmem_limit_bytes=mib << 20),
        **rest,
    )


def halves(x):
    hi = x.astype(BF16)
    return hi, (x - hi.astype(F32)).astype(BF16)


def dot3(a, b, dims):
    (ah, al), (bh, bl) = a, b

    def one(x, y):
        return lax.dot_general(x, y, (dims, ((), ())), preferred_element_type=F32)

    return one(ah, bh) + (one(ah, bl) + one(al, bh))


def dot3_stacked(a, b):
    (ah, al), (bh, bl) = a, b
    size = ah.shape[0]

    def one(x, y):
        return lax.dot_general(x, y, (NT, ((), ())), preferred_element_type=F32)

    both = one(jnp.concatenate([ah, al], axis=0), bh)
    return both[:size] + (one(ah, bl) + both[size:])


NN = ((1,), (0,))
NT = ((1,), (1,))


def strip(i):
    return slice(i * B, (i + 1) * B)


class Rules:
    def __init__(self, s_ref, start, rows, cols):
        self.s_ref, self.start, self.rows, self.cols = s_ref, start, rows, cols
        block = lax.shift_right_logical(lax.broadcasted_iota(jnp.int32, (1, N), 1), 6)
        radii = flags = jnp.zeros((1, N), jnp.int32)
        for k in range(H):
            radii = jnp.where(block == k, s_ref[RAD + cols + k], radii)
            flags = jnp.where(block == k, s_ref[start + cols + k], flags)
        self.block, self.radii, self.flags = block + cols, radii, flags

    def strip(self, i):
        reach = jnp.minimum(self.radii, self.s_ref[RAD + self.rows + i])
        keep = jnp.abs(self.block - (self.rows + i)) <= reach
        return keep, self.flags * self.s_ref[self.start + self.rows + i] == 1


def pack_kernel(v_ref, out_ref, diag_ref, cut_ref):
    for i in range(H):
        out_ref[strip(i), :] = jnp.concatenate([v_ref[i, 0], v_ref[i, 1]], axis=1)
    for i in range(4):
        diag_ref[strip(i), :] = jnp.concatenate([v_ref[i, 0], v_ref[i + 4, 0]], axis=1)
    col = lax.axis_index("col")

    @pl.when(col < 4)
    def _():
        cut_ref[...] = out_ref[0 : N - B, :]

    @pl.when(col >= 4)
    def _():
        cut_ref[...] = out_ref[B:N, :]

    @pl.when(col == 4)
    def _():
        cut_ref[0:B, :] = jnp.concatenate([v_ref[1, 0], v_ref[0, 0]], axis=1)


def join_kernel(first_ref, second_ref, out_ref):
    out_ref[0 : N - B, :] = first_ref[...]
    out_ref[N - B : 2 * (N - B), :] = second_ref[...]


def triangle_kernel(own_ref, near_ref, d1_ref, d2_ref, out_ref, both_ref, low, high):
    col = lax.axis_index("col")
    odd, core, upper = (col & 2) == 2, col & 1, lax.shift_right_logical(col, 2)
    both_ref[0:N, :] = own_ref[...]
    both_ref[N : 2 * N, :] = near_ref[...]
    low[...] = jnp.where(odd, near_ref[...], own_ref[...])
    high[...] = jnp.where(odd, own_ref[...], near_ref[...])

    def rows(ref, first, last):
        return ref[first * B : (last + 1) * B, :]

    @pl.when((upper == 0) & (core == 0))
    def _():
        out_ref[0:256, :] = rows(high, 3, 6)
        out_ref[256:512, :] = d1_ref[...] + d2_ref[...]
        out_ref[512:576, :] = jnp.zeros((B, 128), F32)

    @pl.when((upper == 0) & (core == 1))
    def _():
        out_ref[0:384, :] = rows(high, 1, 6)
        out_ref[384:512, :] = rows(low, 5, 6)
        out_ref[512:576, :] = jnp.zeros((B, 128), F32)

    @pl.when((upper == 1) & (core == 0))
    def _():
        out_ref[0:384, :] = rows(low, 1, 6)
        out_ref[384:512, :] = rows(high, 1, 2)
        last = jnp.concatenate([rows(high, 3, 3)[:, :B], rows(low, 7, 7)[:, :B]], axis=1)
        out_ref[512:576, :] = last

    @pl.when((upper == 1) & (core == 1))
    def _():
        out_ref[0:320, :] = rows(low, 1, 5)
        out_ref[320:384, :] = rows(high, 1, 1)
        out_ref[384:576, :] = jnp.zeros((192, 128), F32)


def square_kernel(s_ref, *refs):
    packs, (p1_ref, v_ref, vh_ref, vl_ref, pv_ref, tr_ref) = refs[:4], refs[4:10]
    q_ref, r_ref, rh, rl = refs[10:]
    yl, core, upper = s_ref[0], s_ref[1], s_ref[3]
    def place(k, other):
        return pl.ds(pl.multiple_of(128 * (2 * (yl ^ k) + (core ^ other)), 128), 128)

    for other in range(2):
        for k in range(2):
            q_ref[:, place(k, other)] = packs[other][k * N : (k + 1) * N, :]

    def cut(k, other):
        return packs[2 + other][(k - 2) * (N - B) : (k - 1) * (N - B), :]

    @pl.when(upper == 0)
    def _():
        for other in range(2):
            for k in range(2, 4):
                q_ref[B:N, place(k, other)] = cut(k, other)
        first = pltpu.roll(q_ref[B : 2 * B, N : N + 128], B, 1)
        lane = lax.broadcasted_iota(jnp.int32, (B, 128), 1)
        q_ref[0:B, N : N + 128] = jnp.where(lane < B, first, 0.0)
        q_ref[0:B, N + 128 : 2 * N] = jnp.zeros((B, N - 128), F32)

    @pl.when(upper == 1)
    def _():
        for other in range(2):
            for k in range(2, 4):
                q_ref[0 : N - B, place(k, other)] = cut(k, other)
        q_ref[N - B : N, 0:N] = jnp.zeros((B, N), F32)

    for i in range(H):
        own = q_ref[strip(i), :]
        at = i * B
        if i % 2:
            own = pltpu.roll(jnp.concatenate([own, jnp.zeros((B, 128), F32)], axis=1), B, 1)
            at -= B
        parts = [own]
        if at:
            parts.insert(0, jnp.zeros((B, at), F32))
        left = W - at - own.shape[1]
        if left:
            parts.append(jnp.zeros((B, left), F32))
        r_ref[strip(i), :] = jnp.concatenate(parts, axis=1)
    inner = r_ref[:, N : 2 * N]
    above = lax.shift_right_logical(lax.broadcasted_iota(jnp.int32, (N, N), 0), 6)
    along = lax.shift_right_logical(lax.broadcasted_iota(jnp.int32, (N, N), 1), 6)
    half = jnp.where((above - along) * (1 - 2 * upper) > 0, inner, 0.0)
    r_ref[:, N : 2 * N] = jnp.where(above == along, inner, half + half.T)
    total = jnp.zeros((1, W), F32)
    for i in range(H):
        full = r_ref[strip(i), :]
        total += jnp.sum(full * full, axis=0, keepdims=True)
        rh[strip(i), :], rl[strip(i), :] = halves(full)
    tr_ref[...] = jnp.broadcast_to(jnp.sum(total, axis=1, keepdims=True), tr_ref.shape)

    def part(rows, cols):
        return rh[rows, cols], rl[rows, cols]

    def gram(rows, cols):
        high, low = part(rows, cols)
        mixed = lax.dot_general(high, low, (NT, ((), ())), preferred_element_type=F32)
        square = lax.dot_general(high, high, (NT, ((), ())), preferred_element_type=F32)
        return square + (mixed + mixed.T)

    lo, hi = slice(0, 256), slice(256, 512)
    mid = slice(N, 2 * N)
    side = pl.ds(pl.multiple_of(2 * N * upper, 128), N)
    v_ref[...] = r_ref[:, side]
    vh_ref[...], vl_ref[...] = rh[:, side], rl[:, side]
    full = pl.ds(pl.multiple_of(256 * (1 - upper), 128), 256)
    pv_ref[:, full] = dot3(part(slice(None), mid), (vh_ref[:, full], vl_ref[:, full]), NN)
    tile = pl.ds(pl.multiple_of(256 * upper, 128), 256)
    near = pl.ds(pl.multiple_of(N + 256 * upper, 128), 256)
    pv_ref[:, tile] = dot3(part(slice(None), near), (vh_ref[tile, tile], vl_ref[tile, tile]), NN)

    p01 = dot3(part(lo, slice(256, 1280)), part(hi, slice(256, 1280)), NT)
    p1_ref[lo, lo] = gram(lo, slice(0, 1280))
    p1_ref[lo, hi] = p01
    p1_ref[hi, lo] = p01.T
    p1_ref[hi, hi] = gram(hi, slice(256, W))
    rules = Rules(s_ref, BR[0], H, H)
    for i in range(H):
        keep, pick = rules.strip(i)
        squared = jnp.where(keep, p1_ref[strip(i), :], 0.0)
        p1_ref[strip(i), :] = jnp.where(pick, 2.0 * r_ref[strip(i), mid] - squared, squared)


def second_kernel(s_ref, p1_ref, v_ref, vh_ref, vl_ref, pv_ref, tr_ref, ta, tb,
                  own_ref, share_ref, sums_ref, t_ref, w_ref, mh, ml):
    core, col, upper = s_ref[1], s_ref[2], s_ref[3]
    lane = lax.broadcasted_iota(jnp.int32, (B, N), 1)
    zero = jnp.zeros((B, 128), F32)
    base, other = H * (1 - upper), H * upper
    t_ref[core, :, :] = ta[...]
    t_ref[1 - core, :, :] = tb[...]

    def line(which, start):
        return t_ref[which, start * B : (start + 1) * B, :]

    @pl.when(upper == 0)
    def _():
        w_ref[strip(0), :] = jnp.zeros((B, N), F32)
        for k in range(1, H):
            parts = [line(0, k - 1), zero, zero, zero]
            if k == 7:
                parts[0] = pltpu.roll(line(0, 8), B, 1)
            if k < 6:
                parts[1] = line(1, k - 1)
            if k < 4:
                parts[2] = line(0, 5 + k)
            if k < 2:
                parts[3] = line(1, 4 + k)
            turned = pltpu.roll(jnp.concatenate(parts, axis=1), k * B, 1)
            w_ref[strip(k), :] = jnp.where(lane >= k * B, turned, 0.0)

    @pl.when(upper == 1)
    def _():
        w_ref[strip(7), :] = jnp.zeros((B, N), F32)
        for k in range(7):
            diag = line(0, 4 + k % 4)
            if k >= 4:
                diag = pltpu.roll(diag, B, 1)
            parts = [zero, zero, zero, diag]
            if k >= 5:
                parts[0] = line(1, k + 1)
            if k >= 3:
                parts[1] = line(0, k - 3)
            if k >= 1:
                parts[2] = line(1, k - 1)
            turned = pltpu.roll(jnp.concatenate(parts, axis=1), ((k + 2) % 8) * B, 1)
            w_ref[strip(k), :] = jnp.where(lane < (k + 1) * B, turned, 0.0)

    full = w_ref[...]
    above = lax.shift_right_logical(lax.broadcasted_iota(jnp.int32, (N, N), 0), 6)
    along = lax.shift_right_logical(lax.broadcasted_iota(jnp.int32, (N, N), 1), 6)
    full = jnp.where(above == along, full, full + full.T)
    w_ref[...] = pv_ref[...] + dot3((vh_ref[...], vl_ref[...]), halves(full), NN)

    def at(block, size):
        return pl.ds(pl.multiple_of(block * B, B), size)

    def row(block, size=B):
        return at(block + 1, size)

    def lanes(block):
        return pl.ds(pl.multiple_of(block * B, 128), N)

    rules = Rules(s_ref, BR[0], H, 2 * H * upper)
    inner = jnp.zeros((1, N), F32)
    for i in range(H):
        keep, pick = rules.strip(i)
        squared = jnp.where(keep, w_ref[strip(i), :], 0.0)
        new = jnp.where(pick, 2.0 * v_ref[strip(i), :] - squared, squared)
        w_ref[strip(i), :] = new
        here = row(base + i)
        mh[here, lanes(other)], ml[here, lanes(other)] = halves(new)
        new = p1_ref[strip(i), :]
        inner += jnp.sum(new * new, axis=0, keepdims=True)
        mh[here, lanes(base)], ml[here, lanes(base)] = halves(new)
    turned = w_ref[...].T
    there = row(other, N)
    mh[there, lanes(base)], ml[there, lanes(base)] = halves(turned)
    blank = jnp.zeros((N, N), BF16)
    mh[there, lanes(other)] = blank
    ml[there, lanes(other)] = blank

    @pl.when(upper == 1)
    def _():
        w_ref[...] = turned

    outer = jnp.zeros((1, N), F32)
    for i in range(H):
        outer += jnp.sum(w_ref[strip(i), :] * w_ref[strip(i), :], axis=0, keepdims=True)

    spot = lax.broadcasted_iota(jnp.int32, (1, 128), 1)
    both = jnp.where(spot == 0, tr_ref[...], 0.0)
    both = jnp.where(spot == 1, jnp.sum(inner, axis=1, keepdims=True), both)
    both = jnp.where(spot == 2, jnp.sum(outer, axis=1, keepdims=True), both)
    sums_ref[...] = jnp.broadcast_to(both, sums_ref.shape)

    shift = 6 - 2 * col

    def share(i, rows, block, panel):
        pair, span = row(block, 128), lanes(panel)
        return dot3_stacked(
            (mh[row(rows + i), span], ml[row(rows + i), span]), (mh[pair, span], ml[pair, span])
        )

    for i in range(H):
        far = (upper == 0) & (shift + i >= H) | (upper == 1) & (shift + i < 0)
        rows = jnp.where(far, other, base)
        share_ref[strip(i), :] = share(i, rows, rows + i + shift, jnp.where(far, base, other))
        here = row(base + i)
        block = base + i + 2 * col - H
        pair = row(block, 128)
        own_ref[0, strip(i), :] = dot3_stacked(
            (mh[here, :], ml[here, :]), (mh[pair, :], ml[pair, :])
        )
        if i % 2:
            span = pl.ds(pl.multiple_of((block - 1) * B, 128), 256)
            held = mh[here, span].astype(F32) + ml[here, span].astype(F32)
            held = held[:, B : B + 128]
        else:
            span = pl.ds(pl.multiple_of(block * B, 128), 128)
            held = mh[here, span].astype(F32) + ml[here, span].astype(F32)
        own_ref[1, strip(i), :] = held
    i = 2 * (col & 3) + 1
    here = at(i, B)
    wide = lax.broadcasted_iota(jnp.int32, (B, 128), 1) >= B
    share_ref[here, :] = jnp.where(wide, share(i, 0, 7 - 8 * upper, H), share_ref[here, :])


def last_kernel(s_ref, own_ref, far_ref, near_ref, sums_ref, out_ref, traces_ref):
    col, upper = s_ref[2], s_ref[3]
    wide = lax.broadcasted_iota(jnp.int32, (B, 128), 1) >= B
    for i in range(H):
        index = i + 2 * col - H + wide.astype(jnp.int32)
        inside = (index >= 0) & (index < H)
        share = jnp.where(inside, near_ref[strip(i), :], far_ref[strip(i), :])
        squared = own_ref[0, strip(i), :] + share
        keep, pick = [], []
        for h in range(2):
            far = jnp.abs(2 * col + h - H)
            reach = jnp.minimum(s_ref[RAD + H + i], s_ref[RAD + i + 2 * col + h])
            keep.append((far <= reach).astype(F32))
            pick.append((s_ref[BR[1] + H + i] * s_ref[BR[1] + i + 2 * col + h]).astype(F32))
        squared = squared * jnp.where(wide, keep[1], keep[0])
        chosen = jnp.where(wide, pick[1], pick[0]) == 1.0
        new = jnp.where(chosen, 2.0 * own_ref[1, strip(i), :] - squared, squared)
        out_ref[i, 0] = new[:, :B]
        out_ref[i, 1] = new[:, B:]
    sums = sums_ref[...]
    count = sums.shape[0]
    spot = lax.broadcasted_iota(jnp.int32, sums.shape, 1)
    line = lax.broadcasted_iota(jnp.int32, sums.shape, 0)
    turned = jnp.concatenate([sums[count - 1 :], sums[: count - 1]], axis=0)
    sums = jnp.where((spot == 2) & (upper + 0 * line == 1), turned, sums)
    total = jnp.sum(sums, axis=0, keepdims=True)
    spot = lax.broadcasted_iota(jnp.int32, total.shape, 1)
    weight = jnp.where(spot == 1, 1.0, jnp.where(spot == 2, 2.0, 0.0))
    traces_ref[0] = jnp.sum(jnp.where(spot == 0, total, 0.0))
    traces_ref[1] = jnp.sum(total * weight)


def shape(*dims):
    return jax.ShapeDtypeStruct(dims, F32)


def per_device(rows, values, radius, branch):
    both = ("row", "col")
    row, col = lax.axis_index("row"), lax.axis_index("col")

    def swap(x):
        return lax.ppermute(x, "col", [(c, c ^ 1) for c in range(8)])

    def index(r, c):
        return r * 8 + c

    ends = [(r, c) for r in range(rows - 1) for c in range(4)]

    packed, diag, cut = call(
        pack_kernel, out_shape=[shape(N, 128), shape(256, 128), shape(N - B, 128)],
        in_specs=[VMEM], out_specs=[VMEM] * 3, mib=8, name="pack",
    )(values)
    near = lax.ppermute(packed, "col", [(c, c ^ 2) for c in range(8)])
    d1 = lax.ppermute(diag, "col", [(4, 2)])
    d2 = lax.ppermute(diag, "col", [(4, 0)])
    cross = lax.ppermute(cut, "col", [(c, c ^ 4) for c in range(8)])
    far = lax.ppermute(cut, "col", [(c, c ^ 6) for c in range(8)])
    triangle, joined = call(
        triangle_kernel,
        out_shape=[shape(576, 128), shape(2 * N, 128)],
        in_specs=[VMEM] * 4,
        out_specs=[VMEM] * 2,
        scratch_shapes=[pltpu.VMEM((N, 128), F32)] * 2,
        mib=8, name="triangle",
    )(packed, near, d1, d2)
    pairs = [(index(r, c + 4), index(r + 1, c)) for r, c in ends]
    ta = lax.ppermute(triangle, both, pairs + [(b, a) for a, b in pairs])
    radius, branch, joined = lax.optimization_barrier((radius, branch, joined))
    pad = ((H, H),)
    radii = lax.dynamic_slice(jnp.pad(radius, pad, constant_values=-1), (H * row,), (3 * H,))
    flags = lax.dynamic_slice(jnp.pad(branch, ((0, 0),) + pad), (0, H * row), (2, 3 * H))
    scalars = jnp.concatenate(
        [jnp.stack([col // 2, col % 2, col, col // 4]).astype(jnp.int32), radii, flags[0], flags[1]]
    )
    cross, scalars = lax.optimization_barrier((cross, scalars))
    joined2 = swap(joined)
    distant = call(
        join_kernel, out_shape=shape(2 * (N - B), 128), in_specs=[VMEM] * 2, out_specs=VMEM,
        mib=8, name="join",
    )(cross, far)
    distant2 = swap(distant)
    tb = swap(ta)

    *old, trace = call(
        square_kernel,
        out_shape=[
            shape(N, N), shape(N, N), jax.ShapeDtypeStruct((N, N), BF16),
            jax.ShapeDtypeStruct((N, N), BF16), shape(N, N), shape(1, 128),
        ],
        in_specs=[SMEM] + [VMEM] * 4,
        out_specs=[VMEM] * 6,
        scratch_shapes=[
            pltpu.VMEM((N, 2 * N), F32),
            pltpu.VMEM((N, W), F32),
            pltpu.VMEM((N, W), BF16),
            pltpu.VMEM((N, W), BF16),
        ],
        mib=24, name="square",
    )(scalars, joined, joined2, distant, distant2)

    own, share, sums = call(
        second_kernel,
        out_shape=[shape(2, N, 128), shape(N, 128), shape(rows, 128)],
        in_specs=[SMEM] + [VMEM] * 8,
        out_specs=[VMEM] * 3,
        scratch_shapes=[
            pltpu.VMEM((2, 576, 128), F32),
            pltpu.VMEM((N, N), F32),
            pltpu.VMEM((18 * B, 2 * N), BF16),
            pltpu.VMEM((18 * B, 2 * N), BF16),
        ],
        mib=24, name="second",
    )(scalars, *old, trace, ta, tb)

    pairs = [(index(r, 7 - c), index(r + 1, c)) for r, c in ends]
    far = lax.ppermute(share, both, pairs + [(b, a) for a, b in pairs])
    near = lax.ppermute(share, "col", [(c, 7 - c) for c in range(8)])
    sums = lax.all_to_all(sums, "row", 0, 0, tiled=True)
    return call(
        last_kernel,
        out_shape=[shape(H, 2, B, B), shape(2)],
        in_specs=[SMEM] + [VMEM] * 4,
        out_specs=[VMEM, SMEM],
        mib=8, name="last",
    )(scalars, own, far, near, sums)


def solution(mesh):
    rows = mesh.shape["row"]

    def run(values, radius, branch):
        return per_device(rows, values, radius, branch)

    in_specs = (P("row", "col", None, None), P(), P())
    out_specs = (P("row", "col", None, None), P())
    return jax.shard_map(
        run, mesh=mesh, in_specs=in_specs, out_specs=out_specs, check_vma=False
    )
```

```python
import jax
import jax.numpy as jnp
from jax import lax
from jax.experimental import pallas as pl
from jax.experimental.pallas import tpu as pltpu
from jax.sharding import PartitionSpec as P

F32 = jnp.float32
BF16 = jnp.bfloat16
B = 64
H = 8
N = H * B
W = 3 * N
VMEM = pl.BlockSpec(memory_space=pltpu.VMEM)
SMEM = pl.BlockSpec(memory_space=pltpu.SMEM)
RAD, BR = 4, (28, 52)


def call(kernel, mib, name, **rest):
    return pl.pallas_call(
        kernel,
        name=name,
        compiler_params=pltpu.CompilerParams(vmem_limit_bytes=mib << 20),
        **rest,
    )


def halves(x):
    hi = x.astype(BF16)
    return hi, (x - hi.astype(F32)).astype(BF16)


def dot3(a, b, dims):
    (ah, al), (bh, bl) = a, b

    def one(x, y):
        return lax.dot_general(x, y, (dims, ((), ())), preferred_element_type=F32)

    return one(ah, bh) + (one(ah, bl) + one(al, bh))


def dot3_stacked(a, b):
    (ah, al), (bh, bl) = a, b
    size = ah.shape[0]

    def one(x, y):
        return lax.dot_general(x, y, (NT, ((), ())), preferred_element_type=F32)

    both = one(jnp.concatenate([ah, al], axis=0), bh)
    return both[:size] + (one(ah, bl) + both[size:])


NN = ((1,), (0,))
NT = ((1,), (1,))


def strip(i):
    return slice(i * B, (i + 1) * B)


class Rules:
    def __init__(self, s_ref, start, rows, cols):
        self.s_ref, self.start, self.rows, self.cols = s_ref, start, rows, cols
        block = lax.shift_right_logical(lax.broadcasted_iota(jnp.int32, (1, N), 1), 6)
        radii = flags = jnp.zeros((1, N), jnp.int32)
        for k in range(H):
            radii = jnp.where(block == k, s_ref[RAD + cols + k], radii)
            flags = jnp.where(block == k, s_ref[start + cols + k], flags)
        self.block, self.radii, self.flags = block + cols, radii, flags

    def strip(self, i):
        reach = jnp.minimum(self.radii, self.s_ref[RAD + self.rows + i])
        keep = jnp.abs(self.block - (self.rows + i)) <= reach
        return keep, self.flags * self.s_ref[self.start + self.rows + i] == 1


def pack_kernel(v_ref, out_ref, diag_ref, cut_ref):
    for i in range(H):
        out_ref[strip(i), :] = jnp.concatenate([v_ref[i, 0], v_ref[i, 1]], axis=1)
    for i in range(4):
        diag_ref[strip(i), :] = jnp.concatenate([v_ref[i, 0], v_ref[i + 4, 0]], axis=1)
    col = lax.axis_index("col")

    @pl.when(col < 4)
    def _():
        cut_ref[...] = out_ref[0 : N - B, :]

    @pl.when(col >= 4)
    def _():
        cut_ref[...] = out_ref[B:N, :]

    @pl.when(col == 4)
    def _():
        cut_ref[0:B, :] = jnp.concatenate([v_ref[1, 0], v_ref[0, 0]], axis=1)


def join_kernel(first_ref, second_ref, out_ref):
    out_ref[0 : N - B, :] = first_ref[...]
    out_ref[N - B : 2 * (N - B), :] = second_ref[...]


def triangle_kernel(s_ref, own_ref, near_ref, d1_ref, d2_ref, out_ref, both_ref, low, high):
    odd, core, upper = (s_ref[0] & 1) == 1, s_ref[1], s_ref[3]
    both_ref[0:N, :] = own_ref[...]
    both_ref[N : 2 * N, :] = near_ref[...]
    low[...] = jnp.where(odd, near_ref[...], own_ref[...])
    high[...] = jnp.where(odd, own_ref[...], near_ref[...])

    def rows(ref, first, last):
        return ref[first * B : (last + 1) * B, :]

    @pl.when((upper == 0) & (core == 0))
    def _():
        out_ref[0:256, :] = rows(high, 3, 6)
        out_ref[256:512, :] = d1_ref[...] + d2_ref[...]
        out_ref[512:576, :] = jnp.zeros((B, 128), F32)

    @pl.when((upper == 0) & (core == 1))
    def _():
        out_ref[0:384, :] = rows(high, 1, 6)
        out_ref[384:512, :] = rows(low, 5, 6)
        out_ref[512:576, :] = jnp.zeros((B, 128), F32)

    @pl.when((upper == 1) & (core == 0))
    def _():
        out_ref[0:384, :] = rows(low, 1, 6)
        out_ref[384:512, :] = rows(high, 1, 2)
        last = jnp.concatenate([rows(high, 3, 3)[:, :B], rows(low, 7, 7)[:, :B]], axis=1)
        out_ref[512:576, :] = last

    @pl.when((upper == 1) & (core == 1))
    def _():
        out_ref[0:320, :] = rows(low, 1, 5)
        out_ref[320:384, :] = rows(high, 1, 1)
        out_ref[384:576, :] = jnp.zeros((192, 128), F32)


def square_kernel(s_ref, *refs):
    packs, (p1_ref, v_ref, vh_ref, vl_ref, pv_ref, tr_ref) = refs[:4], refs[4:10]
    q_ref, r_ref, rh, rl = refs[10:]
    yl, core, upper = s_ref[0], s_ref[1], s_ref[3]
    def place(k, other):
        return pl.ds(pl.multiple_of(128 * (2 * (yl ^ k) + (core ^ other)), 128), 128)

    for other in range(2):
        for k in range(2):
            q_ref[:, place(k, other)] = packs[other][k * N : (k + 1) * N, :]

    def cut(k, other):
        return packs[2 + other][(k - 2) * (N - B) : (k - 1) * (N - B), :]

    @pl.when(upper == 0)
    def _():
        for other in range(2):
            for k in range(2, 4):
                q_ref[B:N, place(k, other)] = cut(k, other)
        first = pltpu.roll(q_ref[B : 2 * B, N : N + 128], B, 1)
        lane = lax.broadcasted_iota(jnp.int32, (B, 128), 1)
        q_ref[0:B, N : N + 128] = jnp.where(lane < B, first, 0.0)
        q_ref[0:B, N + 128 : 2 * N] = jnp.zeros((B, N - 128), F32)

    @pl.when(upper == 1)
    def _():
        for other in range(2):
            for k in range(2, 4):
                q_ref[0 : N - B, place(k, other)] = cut(k, other)
        q_ref[N - B : N, 0:N] = jnp.zeros((B, N), F32)

    for i in range(H):
        own = q_ref[strip(i), :]
        at = i * B
        if i % 2:
            own = pltpu.roll(jnp.concatenate([own, jnp.zeros((B, 128), F32)], axis=1), B, 1)
            at -= B
        parts = [own]
        if at:
            parts.insert(0, jnp.zeros((B, at), F32))
        left = W - at - own.shape[1]
        if left:
            parts.append(jnp.zeros((B, left), F32))
        r_ref[strip(i), :] = jnp.concatenate(parts, axis=1)
    inner = r_ref[:, N : 2 * N]
    above = lax.shift_right_logical(lax.broadcasted_iota(jnp.int32, (N, N), 0), 6)
    along = lax.shift_right_logical(lax.broadcasted_iota(jnp.int32, (N, N), 1), 6)
    half = jnp.where((above - along) * (1 - 2 * upper) > 0, inner, 0.0)
    r_ref[:, N : 2 * N] = jnp.where(above == along, inner, half + half.T)
    total = jnp.zeros((1, W), F32)
    for i in range(H):
        full = r_ref[strip(i), :]
        total += jnp.sum(full * full, axis=0, keepdims=True)
        rh[strip(i), :], rl[strip(i), :] = halves(full)
    tr_ref[...] = jnp.broadcast_to(jnp.sum(total, axis=1, keepdims=True), tr_ref.shape)

    def part(rows, cols):
        return rh[rows, cols], rl[rows, cols]

    def gram(rows, cols):
        high, low = part(rows, cols)
        mixed = lax.dot_general(high, low, (NT, ((), ())), preferred_element_type=F32)
        square = lax.dot_general(high, high, (NT, ((), ())), preferred_element_type=F32)
        return square + (mixed + mixed.T)

    lo, hi = slice(0, 256), slice(256, 512)
    mid = slice(N, 2 * N)
    side = pl.ds(pl.multiple_of(2 * N * upper, 128), N)
    v_ref[...] = r_ref[:, side]
    vh_ref[...], vl_ref[...] = rh[:, side], rl[:, side]
    full = pl.ds(pl.multiple_of(256 * (1 - upper), 128), 256)
    pv_ref[:, full] = dot3(part(slice(None), mid), (vh_ref[:, full], vl_ref[:, full]), NN)
    tile = pl.ds(pl.multiple_of(256 * upper, 128), 256)
    near = pl.ds(pl.multiple_of(N + 256 * upper, 128), 256)
    pv_ref[:, tile] = dot3(part(slice(None), near), (vh_ref[tile, tile], vl_ref[tile, tile]), NN)

    p01 = dot3(part(lo, slice(256, 1280)), part(hi, slice(256, 1280)), NT)
    p1_ref[lo, lo] = gram(lo, slice(0, 1280))
    p1_ref[lo, hi] = p01
    p1_ref[hi, lo] = p01.T
    p1_ref[hi, hi] = gram(hi, slice(256, W))
    rules = Rules(s_ref, BR[0], H, H)
    for i in range(H):
        keep, pick = rules.strip(i)
        squared = jnp.where(keep, p1_ref[strip(i), :], 0.0)
        p1_ref[strip(i), :] = jnp.where(pick, 2.0 * r_ref[strip(i), mid] - squared, squared)


def second_kernel(s_ref, p1_ref, v_ref, vh_ref, vl_ref, pv_ref, tr_ref, ta, tb,
                  own_ref, share_ref, sums_ref, t_ref, w_ref, mh, ml):
    core, col, upper = s_ref[1], s_ref[2], s_ref[3]
    lane = lax.broadcasted_iota(jnp.int32, (B, N), 1)
    zero = jnp.zeros((B, 128), F32)
    base, other = H * (1 - upper), H * upper
    t_ref[core, :, :] = ta[...]
    t_ref[1 - core, :, :] = tb[...]

    def line(which, start):
        return t_ref[which, start * B : (start + 1) * B, :]

    @pl.when(upper == 0)
    def _():
        w_ref[strip(0), :] = jnp.zeros((B, N), F32)
        for k in range(1, H):
            parts = [line(0, k - 1), zero, zero, zero]
            if k == 7:
                parts[0] = pltpu.roll(line(0, 8), B, 1)
            if k < 6:
                parts[1] = line(1, k - 1)
            if k < 4:
                parts[2] = line(0, 5 + k)
            if k < 2:
                parts[3] = line(1, 4 + k)
            turned = pltpu.roll(jnp.concatenate(parts, axis=1), k * B, 1)
            w_ref[strip(k), :] = jnp.where(lane >= k * B, turned, 0.0)

    @pl.when(upper == 1)
    def _():
        w_ref[strip(7), :] = jnp.zeros((B, N), F32)
        for k in range(7):
            diag = line(0, 4 + k % 4)
            if k >= 4:
                diag = pltpu.roll(diag, B, 1)
            parts = [zero, zero, zero, diag]
            if k >= 5:
                parts[0] = line(1, k + 1)
            if k >= 3:
                parts[1] = line(0, k - 3)
            if k >= 1:
                parts[2] = line(1, k - 1)
            turned = pltpu.roll(jnp.concatenate(parts, axis=1), ((k + 2) % 8) * B, 1)
            w_ref[strip(k), :] = jnp.where(lane < (k + 1) * B, turned, 0.0)

    full = w_ref[...]
    above = lax.shift_right_logical(lax.broadcasted_iota(jnp.int32, (N, N), 0), 6)
    along = lax.shift_right_logical(lax.broadcasted_iota(jnp.int32, (N, N), 1), 6)
    full = jnp.where(above == along, full, full + full.T)
    w_ref[...] = pv_ref[...] + dot3((vh_ref[...], vl_ref[...]), halves(full), NN)

    def at(block, size):
        return pl.ds(pl.multiple_of(block * B, B), size)

    def row(block, size=B):
        return at(block + 1, size)

    def lanes(block):
        return pl.ds(pl.multiple_of(block * B, 128), N)

    rules = Rules(s_ref, BR[0], H, 2 * H * upper)
    inner = jnp.zeros((1, N), F32)
    for i in range(H):
        keep, pick = rules.strip(i)
        squared = jnp.where(keep, w_ref[strip(i), :], 0.0)
        new = jnp.where(pick, 2.0 * v_ref[strip(i), :] - squared, squared)
        w_ref[strip(i), :] = new
        here = row(base + i)
        mh[here, lanes(other)], ml[here, lanes(other)] = halves(new)
        new = p1_ref[strip(i), :]
        inner += jnp.sum(new * new, axis=0, keepdims=True)
        mh[here, lanes(base)], ml[here, lanes(base)] = halves(new)
    turned = w_ref[...].T
    there = row(other, N)
    mh[there, lanes(base)], ml[there, lanes(base)] = halves(turned)
    blank = jnp.zeros((N, N), BF16)
    mh[there, lanes(other)] = blank
    ml[there, lanes(other)] = blank

    @pl.when(upper == 1)
    def _():
        w_ref[...] = turned

    outer = jnp.zeros((1, N), F32)
    for i in range(H):
        outer += jnp.sum(w_ref[strip(i), :] * w_ref[strip(i), :], axis=0, keepdims=True)

    spot = lax.broadcasted_iota(jnp.int32, (1, 128), 1)
    both = jnp.where(spot == 0, tr_ref[...], 0.0)
    both = jnp.where(spot == 1, jnp.sum(inner, axis=1, keepdims=True), both)
    both = jnp.where(spot == 2, jnp.sum(outer, axis=1, keepdims=True), both)
    sums_ref[...] = jnp.broadcast_to(both, sums_ref.shape)

    shift = 6 - 2 * col

    def share(i, rows, block, panel):
        pair, span = row(block, 128), lanes(panel)
        return dot3_stacked(
            (mh[row(rows + i), span], ml[row(rows + i), span]), (mh[pair, span], ml[pair, span])
        )

    for i in range(H):
        far = (upper == 0) & (shift + i >= H) | (upper == 1) & (shift + i < 0)
        rows = jnp.where(far, other, base)
        share_ref[strip(i), :] = share(i, rows, rows + i + shift, jnp.where(far, base, other))
        here = row(base + i)
        block = base + i + 2 * col - H
        pair = row(block, 128)
        own_ref[0, strip(i), :] = dot3_stacked(
            (mh[here, :], ml[here, :]), (mh[pair, :], ml[pair, :])
        )
        if i % 2:
            span = pl.ds(pl.multiple_of((block - 1) * B, 128), 256)
            held = mh[here, span].astype(F32) + ml[here, span].astype(F32)
            held = held[:, B : B + 128]
        else:
            span = pl.ds(pl.multiple_of(block * B, 128), 128)
            held = mh[here, span].astype(F32) + ml[here, span].astype(F32)
        own_ref[1, strip(i), :] = held
    i = 2 * (col & 3) + 1
    here = at(i, B)
    wide = lax.broadcasted_iota(jnp.int32, (B, 128), 1) >= B
    share_ref[here, :] = jnp.where(wide, share(i, 0, 7 - 8 * upper, H), share_ref[here, :])


def last_kernel(s_ref, own_ref, far_ref, near_ref, sums_ref, out_ref, traces_ref):
    col, upper = s_ref[2], s_ref[3]
    wide = lax.broadcasted_iota(jnp.int32, (B, 128), 1) >= B
    for i in range(H):
        index = i + 2 * col - H + wide.astype(jnp.int32)
        inside = (index >= 0) & (index < H)
        share = jnp.where(inside, near_ref[strip(i), :], far_ref[strip(i), :])
        squared = own_ref[0, strip(i), :] + share
        keep, pick = [], []
        for h in range(2):
            far = jnp.abs(2 * col + h - H)
            reach = jnp.minimum(s_ref[RAD + H + i], s_ref[RAD + i + 2 * col + h])
            keep.append((far <= reach).astype(F32))
            pick.append((s_ref[BR[1] + H + i] * s_ref[BR[1] + i + 2 * col + h]).astype(F32))
        squared = squared * jnp.where(wide, keep[1], keep[0])
        chosen = jnp.where(wide, pick[1], pick[0]) == 1.0
        new = jnp.where(chosen, 2.0 * own_ref[1, strip(i), :] - squared, squared)
        out_ref[i, 0] = new[:, :B]
        out_ref[i, 1] = new[:, B:]
    sums = sums_ref[...]
    count = sums.shape[0]
    spot = lax.broadcasted_iota(jnp.int32, sums.shape, 1)
    line = lax.broadcasted_iota(jnp.int32, sums.shape, 0)
    turned = jnp.concatenate([sums[count - 1 :], sums[: count - 1]], axis=0)
    sums = jnp.where((spot == 2) & (upper + 0 * line == 1), turned, sums)
    total = jnp.sum(sums, axis=0, keepdims=True)
    spot = lax.broadcasted_iota(jnp.int32, total.shape, 1)
    weight = jnp.where(spot == 1, 1.0, jnp.where(spot == 2, 2.0, 0.0))
    traces_ref[0] = jnp.sum(jnp.where(spot == 0, total, 0.0))
    traces_ref[1] = jnp.sum(total * weight)


def shape(*dims):
    return jax.ShapeDtypeStruct(dims, F32)


def per_device(rows, values, radius, branch):
    both = ("row", "col")
    row, col = lax.axis_index("row"), lax.axis_index("col")
    pad = ((H, H),)
    radii = lax.dynamic_slice(jnp.pad(radius, pad, constant_values=-1), (H * row,), (3 * H,))
    flags = lax.dynamic_slice(jnp.pad(branch, ((0, 0),) + pad), (0, H * row), (2, 3 * H))
    scalars = jnp.concatenate(
        [jnp.stack([col // 2, col % 2, col, col // 4]).astype(jnp.int32), radii, flags[0], flags[1]]
    )

    def swap(x):
        return lax.ppermute(x, "col", [(c, c ^ 1) for c in range(8)])

    def to_rows(x, pairs):
        return lax.ppermute(x, both, pairs)

    def index(r, c):
        return r * 8 + c

    ends = [(r, c) for r in range(rows - 1) for c in range(4)]

    packed, diag, cut = call(
        pack_kernel, out_shape=[shape(N, 128), shape(256, 128), shape(N - B, 128)],
        in_specs=[VMEM], out_specs=[VMEM] * 3, mib=8, name="pack",
    )(values)
    near = lax.ppermute(packed, "col", [(c, c ^ 2) for c in range(8)])
    d1 = lax.ppermute(diag, "col", [(4, 2)])
    d2 = lax.ppermute(diag, "col", [(4, 0)])
    cut, d1 = lax.optimization_barrier((cut, d1))
    cross = lax.ppermute(cut, "col", [(c, c ^ 4) for c in range(8)])
    far = lax.ppermute(cut, "col", [(c, c ^ 6) for c in range(8)])
    triangle, joined = call(
        triangle_kernel,
        out_shape=[shape(576, 128), shape(2 * N, 128)],
        in_specs=[SMEM] + [VMEM] * 4,
        out_specs=[VMEM] * 2,
        scratch_shapes=[pltpu.VMEM((N, 128), F32)] * 2,
        mib=8, name="triangle",
    )(scalars, packed, near, d1, d2)
    pairs = [(index(r, c + 4), index(r + 1, c)) for r, c in ends]
    ta = lax.ppermute(triangle, both, pairs + [(b, a) for a, b in pairs])
    joined2 = swap(joined)
    distant = call(
        join_kernel, out_shape=shape(2 * (N - B), 128), in_specs=[VMEM] * 2, out_specs=VMEM,
        mib=8, name="join",
    )(cross, far)
    distant2 = swap(distant)
    tb = swap(ta)

    *old, trace = call(
        square_kernel,
        out_shape=[
            shape(N, N), shape(N, N), jax.ShapeDtypeStruct((N, N), BF16),
            jax.ShapeDtypeStruct((N, N), BF16), shape(N, N), shape(1, 128),
        ],
        in_specs=[SMEM] + [VMEM] * 4,
        out_specs=[VMEM] * 6,
        scratch_shapes=[
            pltpu.VMEM((N, 2 * N), F32),
            pltpu.VMEM((N, W), F32),
            pltpu.VMEM((N, W), BF16),
            pltpu.VMEM((N, W), BF16),
        ],
        mib=24, name="square",
    )(scalars, joined, joined2, distant, distant2)

    own, share, sums = call(
        second_kernel,
        out_shape=[shape(2, N, 128), shape(N, 128), shape(rows, 128)],
        in_specs=[SMEM] + [VMEM] * 8,
        out_specs=[VMEM] * 3,
        scratch_shapes=[
            pltpu.VMEM((2, 576, 128), F32),
            pltpu.VMEM((N, N), F32),
            pltpu.VMEM((18 * B, 2 * N), BF16),
            pltpu.VMEM((18 * B, 2 * N), BF16),
        ],
        mib=24, name="second",
    )(scalars, *old, trace, ta, tb)

    pairs = [(index(r, 7 - c), index(r + 1, c)) for r, c in ends]
    far = lax.ppermute(share, both, pairs + [(b, a) for a, b in pairs])
    near = lax.ppermute(share, "col", [(c, 7 - c) for c in range(8)])
    sums = lax.all_to_all(sums, "row", 0, 0, tiled=True)
    return call(
        last_kernel,
        out_shape=[shape(H, 2, B, B), shape(2)],
        in_specs=[SMEM] + [VMEM] * 4,
        out_specs=[VMEM, SMEM],
        mib=8, name="last",
    )(scalars, own, far, near, sums)


def solution(mesh):
    rows = mesh.shape["row"]

    def run(values, radius, branch):
        return per_device(rows, values, radius, branch)

    in_specs = (P("row", "col", None, None), P(), P())
    out_specs = (P("row", "col", None, None), P())
    return jax.shard_map(
        run, mesh=mesh, in_specs=in_specs, out_specs=out_specs, check_vma=False
    )
```
